32 devices in a mesh: dp: 16 (over z, x, core), tensor: 2 (over y).
Axes of the slice: x: 2, y: 2, z: 4, core: 2. Of those that a mesh axis runs over, the one named last changes fastest.
Arguments:
- tokens: bfloat16 [4096, 768], P(('dp', 'tensor')), may hold values from -6 to 6
- cotangent: bfloat16 [4096, 768], P(('dp', 'tensor')), may hold values from -6 to 6
- query_weight: bfloat16 [768, 768], P('dp', 'tensor'), may hold values from -0.21875 to 0.21875
- key_weight: bfloat16 [768, 768], P('dp', 'tensor'), may hold values from -0.21875 to 0.21875
- value_weight: bfloat16 [768, 768], P('dp', 'tensor'), may hold values from -0.21875 to 0.21875
- output_weight: bfloat16 [768, 768], P('dp', 'tensor'), may hold values from -0.875 to 0.875
- attention_scale: bfloat16 [768], P('dp'), may hold values from 0.5 to 1.5
- expert_scale: bfloat16 [768], P('dp'), may hold values from 0.5 to 1.5
- router: bfloat16 [768, 4], P('dp'), may hold values from -0.15625 to 0.15625
- bucket_bias: float32 [32, 12], P(None, 'tensor'), may hold values from -4 to 4
- expert_up_weight: bfloat16 [768, 12288], P(None, ('dp', 'tensor')), may hold values from -0.21875 to 0.21875
- expert_down_weight: bfloat16 [768, 12288], P(None, ('dp', 'tensor')), may hold values from -0.625 to 0.625
- routes: int32 [4096, 1], P('dp'), may hold values from 0 to 3; in each aligned block of 256 rows (0 to 255, 256 to 511, ...) at most 80 rows name the same one
- lengths: int32 [16, 2], P('dp'), may hold values from 0 to 256, as said below
- buckets: int32 [511], replicated, may hold values from 0 to 31
Outputs:
- layer_out: bfloat16 [4096, 768], P(('dp', 'tensor'))
- grad_tokens: bfloat16 [4096, 768], P(('dp', 'tensor'))
- grad_query: float32 [768, 768], P('dp', 'tensor')
- grad_key: float32 [768, 768], P('dp', 'tensor')
- grad_value: float32 [768, 768], P('dp', 'tensor')
- grad_output: float32 [768, 768], P('dp', 'tensor')
- grad_gain_attn: float32 [768], P('dp')
- grad_gain_moe: float32 [768], P('dp')
- grad_router: float32 [768, 4], P('dp')
- grad_table: float32 [32, 12], P(None, 'tensor')
- grad_w_in: float32 [768, 12288], P(None, ('dp', 'tensor'))
- grad_w_out: float32 [768, 12288], P(None, ('dp', 'tensor'))
The draws below stay inside these ranges and needn't reach their ends.
Inputs may be any that keep to these rules, and one draw needn't show every extreme that they name: `routes`: in the 256 rows of one block no expert is named more than 80 times; some expert is named exactly 80 times in some block. The two lengths of a block sum to at most 256; some block holds one sequence of all 256 slots.
All inputs are finite; a program needn't handle non-finite values.
Results may differ from the reference program's by a relative error of at most 0.02.
Values may be sent and summed in bfloat16 or wider, within the bound.
No kernel may reach another device: no remote copies, remote signals or barrier semaphores. Data moves between devices by JAX's collectives and lax.ppermute only.
A program may use at most 128 MiB of HBM per device.

```python
import math
from functools import partial
import jax
import jax.numpy as jnp
import numpy as np
from jax import lax

MODEL_DIM = 768
HEADS = 12
HEAD_DIM = 64
FF = 3072
BUCKETS = 32
TOKEN_SLOTS_PART = 256
EXPERTS = 4
CAP = 80
TOKEN_SLOTS = 4096
N_DP = 16


def draw_lengths(key, part):
    key = jax.random.fold_in(key, 11)
    key_live, key_first, key_full = jax.random.split(key, 3)
    active_count = jax.random.randint(key_live, (N_DP,), TOKEN_SLOTS_PART // 2, TOKEN_SLOTS_PART + 1)
    first_len = jax.random.randint(key_first, (N_DP,), 1, active_count + 1)
    second_len = active_count - first_len
    full_row = jax.random.randint(key_full, (), 0, N_DP)
    row_ids = jnp.arange(N_DP)
    first_len = jnp.where(row_ids == full_row, TOKEN_SLOTS_PART, first_len)
    second_len = jnp.where(row_ids == full_row, 0, second_len)
    return jnp.stack([first_len, second_len], axis=1).astype(jnp.int32)


def place_ends(result, own_key, least, largest):
    index_at = [jax.random.randint(jax.random.fold_in(own_key, axis), (), 0, length) for axis, length in enumerate(result.shape)]
    main_axis = result.shape.index(max(result.shape))
    neighbour = index_at[:main_axis] + [(index_at[main_axis] + 1) % result.shape[main_axis]] + index_at[main_axis + 1:]
    return result.at[tuple(index_at)].set(least).at[tuple(neighbour)].set(largest)


def spiked(result, stream_key, source, target, parts, factor):
    owner, partner = [(jnp.arange(result.shape[position]) // (result.shape[position] // parts)).reshape([-1 if axis == position else 1 for axis in range(result.ndim)]) for position in (source, target)]
    chosen = jax.random.permutation(stream_key, parts)[partner]
    strong = (owner == chosen) | (owner == (partner + parts // 2) % parts)
    return jnp.where(strong, factor * result, result)


def block_scale(rng, extent, cuts, least, high):
    factor_of, own = 1.0, jax.random.fold_in(rng, 6)
    for dim, shards_of in cuts:
        heights = jnp.exp(jax.random.uniform(jax.random.fold_in(own, dim), (shards_of,), jnp.float32, least / len(cuts), high / len(cuts)))
        factor_of = factor_of * jnp.repeat(heights, extent[dim] // shards_of).reshape([-1 if axis == dim else 1 for axis in range(len(extent))])
    return factor_of


def routed_block(stream_key, own, number, rows, number_of, top, reach, slope):
    sequence = jax.random.permutation(stream_key, number_of)
    crowded, ordinary = shares(number_of, rows * top, reach, slope, True), shares(number_of, rows * top, reach, slope, False)
    places = jnp.arange(number_of)

    def named(tallies, turn):
        used = int((tallies > 0).sum())
        fixed = max(1, used // 4)
        shifted = fixed + (places - fixed + turn * (used - fixed)) % max(1, number_of - fixed)
        return jnp.zeros((number_of,), jnp.int32).at[sequence[jnp.where(places < fixed, places, shifted)]].set(jnp.asarray(tallies, jnp.int32))

    tallies = jnp.where(number % 4 == 0, named(crowded, number // 4), named(ordinary, number - number // 4 - 1))
    mixed = jax.random.permutation(jax.random.fold_in(own, 3), number_of)
    donor, sink = mixed[0:number_of // 2 * 2:2], mixed[1:number_of // 2 * 2:2]
    room = jnp.minimum(tallies[donor] - 1, reach - tallies[sink]) // 2
    room = jnp.where((donor == sequence[0]) | (sink == sequence[0]) | (tallies[sink] == 0), 0, jnp.maximum(room, 0))
    shifted = jax.random.randint(jax.random.fold_in(own, 4), (number_of // 2,), 0, 1 << 20) % (room + 1)
    tallies = tallies.at[donor].add(-shifted).at[sink].add(shifted)
    items = jnp.searchsorted(jnp.cumsum(tallies), jnp.arange(rows * top), side="right").astype(jnp.int32)
    table = items.reshape(top, rows).T
    table = table[jax.random.permutation(jax.random.fold_in(own, 1), rows)]
    turn = jax.random.randint(jax.random.fold_in(own, 2), (rows, 1), 0, top)
    return jnp.take_along_axis(table, (jnp.arange(top)[None, :] + turn) % top, axis=1)


def shares(count, total, bound, lean, full):
    weights = [(1 << 20) // math.isqrt(rank ** lean) + 1 for rank in range(1, count + 1)]
    largest = bound if full else min(bound, max(-(-total // count), total * weights[0] // sum(weights)))
    least = 1 if total - largest >= count - 1 else 0
    counts, spare = [largest] + [least] * (count - 1), total - largest - least * (count - 1)
    while spare > 0:
        candidates = [i for i in range(1, count) if counts[i] < largest] or [i for i in range(1, count) if counts[i] < bound]
        pool, left = sum([weights[i] for i in candidates]), spare
        for i in candidates:
            extra = min(bound - counts[i], max(1, left * weights[i] // pool), spare)
            counts[i] = counts[i] + extra
            spare = spare - extra
    return np.array(counts)


def normal_values(own_key, shape, scale, most, cuts=(), kind=jnp.bfloat16):
    values = jax.random.normal(own_key, shape, jnp.float32) * scale
    if len(cuts) > 0:
        values = block_scale(own_key, shape, cuts, -0.22, 0.18) * values
    return jnp.clip(values, min=-most, max=most).astype(kind)


def gaussian_with(own_key, shape, width, most, pieces, heavy, kind=jnp.bfloat16):
    values = width * jax.random.normal(own_key, shape, jnp.float32)
    if pieces:
        values = values * block_scale(own_key, shape, pieces, -0.22, 0.18)
    return jnp.clip(spiked(values, jax.random.fold_in(own_key, 3), *heavy), -most, most).astype(kind)


def setup_inputs(seed: int = 0) -> dict:
    key_of = jax.random.split(jax.random.key(seed), 16)
    tokens = normal_values(key_of[0], (TOKEN_SLOTS, MODEL_DIM), 1.0, 6.0, ((0, 32),))
    cotangent = gaussian_with(key_of[1], (TOKEN_SLOTS, MODEL_DIM), 1.0, 6.0, ((0, 32),), (0, 1, 32, 2.75))
    query_weight = normal_values(key_of[2], (MODEL_DIM, MODEL_DIM), MODEL_DIM ** -0.5, 0.21875, ((0, 16), (1, 2)))
    key_weight = normal_values(key_of[3], (MODEL_DIM, MODEL_DIM), MODEL_DIM ** -0.5, 0.21875, ((0, 16), (1, 2)))
    value_weight = normal_values(key_of[4], (MODEL_DIM, MODEL_DIM), MODEL_DIM ** -0.5, 0.21875, ((0, 16), (1, 2)))
    output_weight = normal_values(key_of[5], (MODEL_DIM, MODEL_DIM), (MODEL_DIM // 16) ** -0.5, 0.875, ((0, 16), (1, 2)))
    attention_scale = jnp.clip(1.0 + 0.1 * jax.random.normal(key_of[6], (MODEL_DIM,), jnp.float32), 0.5, 1.5).astype(jnp.bfloat16)
    expert_scale = jnp.clip(1.0 + 0.1 * jax.random.normal(key_of[7], (MODEL_DIM,), jnp.float32), 0.5, 1.5).astype(jnp.bfloat16)
    router = normal_values(key_of[8], (MODEL_DIM, EXPERTS), (2 * MODEL_DIM) ** -0.5, 0.15625, ((0, 16),))
    bucket_bias = normal_values(key_of[9], (BUCKETS, HEADS), 1.0, 4.0, ((1, 2),), jnp.float32)
    expert_up_weight = normal_values(key_of[10], (MODEL_DIM, EXPERTS * FF), MODEL_DIM ** -0.5, 0.21875, ((1, 32),))
    expert_down_weight = normal_values(key_of[11], (MODEL_DIM, EXPERTS * FF), (max(1, FF * 2 // (5 * EXPERTS * EXPERTS))) ** -0.5, 0.625, ((1, 32),))
    routes_keys = jax.random.split(jax.random.fold_in(key_of[12], 1), TOKEN_SLOTS // TOKEN_SLOTS_PART)
    routes_turns = jax.random.permutation(jax.random.fold_in(key_of[12], 3), TOKEN_SLOTS // TOKEN_SLOTS_PART)
    routes = jax.vmap(lambda own, number: routed_block(jax.random.fold_in(key_of[12], 2), own, number, TOKEN_SLOTS_PART, EXPERTS, 1, CAP, 1))(routes_keys, routes_turns).reshape((TOKEN_SLOTS, 1))
    lengths = draw_lengths(jax.random.fold_in(key_of[15], 71), 0)
    buckets = place_ends(jax.random.randint(key_of[14], (2 * TOKEN_SLOTS_PART - 1,), 0, BUCKETS), jax.random.fold_in(key_of[14], 1), 0, BUCKETS - 1).astype(jnp.int32)
    return {"tokens": tokens, "cotangent": cotangent, "query_weight": query_weight, "key_weight": key_weight, "value_weight": value_weight, "output_weight": output_weight, "attention_scale": attention_scale, "expert_scale": expert_scale, "router": router, "bucket_bias": bucket_bias, "expert_up_weight": expert_up_weight, "expert_down_weight": expert_down_weight, "routes": routes, "lengths": lengths, "buckets": buckets}


@jax.custom_vjp
def lower_precision(v):
    return lax.optimization_barrier(v.astype(jnp.bfloat16)).astype(jnp.float32)

@jax.custom_vjp
def lower_backward(v):
    return v

def low_keep(v):
    return (lower_precision(v), None)

def low_pass(kept, grad):
    return (grad,)

def back_keep(v):
    return (v, None)

def back_low(kept, grad):
    return (lower_precision(grad),)
lower_precision.defvjp(low_keep, low_pass)
lower_backward.defvjp(back_keep, back_low)
EPSILON = 1e-06
MASKED_SCORE = -1e+30
HIGHEST = lax.Precision.HIGHEST

def rms_norm(values, gain_vec):
    return values * lax.rsqrt(lax.optimization_barrier(jnp.mean(values * values, axis=-1, keepdims=True)) + EPSILON) * gain_vec

def token_layout(lengths):
    token_position = jnp.arange(TOKEN_SLOTS_PART, dtype=jnp.int32)[None, :]
    first_len = lengths[:, 0:1]
    active_count = first_len + lengths[:, 1:2]
    segment_ids = jnp.where(token_position < first_len, 0, jnp.where(token_position < active_count, 1, 2)).astype(jnp.int32)
    active_mask = (token_position < active_count).astype(jnp.float32)
    return (segment_ids, active_mask)

def expert_slots(expert_routing):
    onehot = (expert_routing[:, :, None] == jnp.arange(EXPERTS, dtype=jnp.int32)[None, None, :]).astype(jnp.int32)
    filled = jnp.cumsum(onehot, axis=1) - 1
    return lax.optimization_barrier(jnp.sum(filled * onehot, axis=2)).astype(jnp.int32)

def attention_block(input_tokens, query_weight, key_weight, value_weight, output_weight, rel_table):
    normalized, segment_ids, active_mask = input_tokens

    def split_heads(weight):
        projected = jnp.dot(normalized, weight, precision=HIGHEST)
        return lower_backward(lower_precision(projected)).reshape(TOKEN_SLOTS_PART, HEADS, HEAD_DIM)
    queries = split_heads(query_weight)
    key_rows = split_heads(key_weight)
    value_rows = split_heads(value_weight)
    token_position = jnp.arange(TOKEN_SLOTS_PART, dtype=jnp.int32)
    offset = token_position[None, :] - token_position[:, None] + TOKEN_SLOTS_PART - 1
    rel_bias = jnp.transpose(jnp.take(rel_table, offset, axis=0), (2, 0, 1))
    scores = jnp.einsum('qhd,khd->hqk', queries, key_rows, precision=HIGHEST) * HEAD_DIM ** (-0.5) + rel_bias
    scores = lower_backward(scores)
    allowed = segment_ids[:, None] == segment_ids[None, :]
    scores = jnp.where(allowed[None], scores, MASKED_SCORE)
    weights = jax.nn.softmax(scores, axis=-1)
    context_rows = jnp.einsum('hqk,khd->qhd', lower_precision(weights), value_rows, precision=HIGHEST)
    context_rows = context_rows.reshape(TOKEN_SLOTS_PART, HEADS * HEAD_DIM)
    context_rows = lower_backward(lower_precision(context_rows * active_mask[:, None]))
    return lower_backward(jnp.dot(context_rows, output_weight.T, precision=HIGHEST))

def expert_block(input_tokens):
    row_block, weight_in, weight_out = input_tokens
    pre_act = lower_backward(jnp.dot(row_block, weight_in, precision=HIGHEST))
    hidden = lower_precision(jax.nn.gelu(pre_act, approximate=True))
    return jnp.dot(hidden, weight_out.T, precision=HIGHEST)

def forward_pass(tokens, query_weight, key_weight, value_weight, output_weight, attention_scale, expert_scale, router, bucket_bias, expert_up_weight, expert_down_weight, expert_routing, capacity_index, segment_ids, active_mask, buckets):
    normalized = lower_precision(rms_norm(tokens, attention_scale))
    bucket_pick = (buckets[:, None] == jnp.arange(BUCKETS, dtype=jnp.int32)[None, :]).astype(jnp.float32)
    rel_table = jnp.dot(bucket_pick, bucket_bias, precision=HIGHEST)
    attend_rows = jax.checkpoint(partial(attention_block, query_weight=query_weight, key_weight=key_weight, value_weight=value_weight, output_weight=output_weight, rel_table=rel_table))
    attention_layer = lax.map(attend_rows, (normalized.reshape(N_DP, TOKEN_SLOTS_PART, MODEL_DIM), segment_ids, active_mask)).reshape(TOKEN_SLOTS, MODEL_DIM)
    residual = tokens + attention_layer
    mixture = lower_precision(rms_norm(residual, expert_scale)).reshape(N_DP, TOKEN_SLOTS_PART, MODEL_DIM)
    logits = jnp.einsum('btd,de->bte', mixture, router, precision=HIGHEST)
    router_probs = jax.nn.softmax(logits, axis=-1)
    gate_chance = jnp.take_along_axis(router_probs, expert_routing[:, :, None], axis=2)[:, :, 0]
    block_id = jnp.broadcast_to(jnp.arange(N_DP, dtype=jnp.int32)[:, None], (N_DP, TOKEN_SLOTS_PART))
    buffer = jnp.zeros((N_DP, EXPERTS, CAP, MODEL_DIM), jnp.float32).at[block_id, expert_routing, capacity_index].set(mixture)
    stacked = jnp.transpose(buffer, (1, 0, 2, 3)).reshape(EXPERTS, N_DP * CAP, MODEL_DIM)
    weight_in = jnp.transpose(expert_up_weight.reshape(MODEL_DIM, EXPERTS, FF), (1, 0, 2))
    weight_out = jnp.transpose(expert_down_weight.reshape(MODEL_DIM, EXPERTS, FF), (1, 0, 2))
    outputs = lax.map(jax.checkpoint(expert_block), (stacked, weight_in, weight_out))
    outputs = jnp.transpose(outputs.reshape(EXPERTS, N_DP, CAP, MODEL_DIM), (1, 0, 2, 3))
    expert_overall = lower_backward(outputs[block_id, expert_routing, capacity_index])
    expert_blend = gate_chance[:, :, None] * expert_overall * active_mask[:, :, None]
    return residual + expert_blend.reshape(TOKEN_SLOTS, MODEL_DIM)

def reference(tokens, cotangent, query_weight, key_weight, value_weight, output_weight, attention_scale, expert_scale, router, bucket_bias, expert_up_weight, expert_down_weight, routes, lengths, buckets):
    segment_ids, active_mask = token_layout(lengths)
    expert_routing = routes.reshape(N_DP, TOKEN_SLOTS_PART).astype(jnp.int32)
    capacity_index = expert_slots(expert_routing)
    floats = tuple((array.astype(jnp.float32) for array in (tokens, query_weight, key_weight, value_weight, output_weight, attention_scale, expert_scale, router, bucket_bias, expert_up_weight, expert_down_weight)))

    def forward_fn(*array_list):
        return forward_pass(*array_list, expert_routing, capacity_index, segment_ids, active_mask, buckets)
    layer_out, pullback = jax.vjp(forward_fn, *floats)
    gradients = pullback(cotangent.astype(jnp.float32))
    return (layer_out.astype(jnp.bfloat16), gradients[0].astype(jnp.bfloat16), gradients[1], gradients[2], gradients[3], gradients[4], gradients[5], gradients[6], gradients[7], gradients[8], gradients[9], gradients[10])
```

```python
import jax
import jax.numpy as jnp
from jax import lax
from jax.experimental import pallas as pl
from jax.experimental.pallas import tpu as pltpu
from jax.sharding import PartitionSpec as P

HEAD_DIM = 64
SPLIT = 4
EPSILON = 1e-06
MASKED_SCORE = -1e30
LANES = 128
SCORE_SCALE = HEAD_DIM ** (-0.5)
HIGHEST = lax.Precision.HIGHEST
VMEM_BYTES = 50 * 1024 * 1024
F32 = jnp.float32
BF16 = jnp.bfloat16

Z_AT, X_AT, C_AT, Y_AT, FIRST_AT, SECOND_AT = range(6)


def matmul(left, right, precision=None):
    return jnp.dot(left, right, precision=precision, preferred_element_type=F32)


def matmul_nt(left, right, precision=None):
    return lax.dot_general(
        left, right, (((1,), (1,)), ((), ())), precision=precision, preferred_element_type=F32
    )


def matmul_tn(left, right, precision=None):
    return lax.dot_general(
        left, right, (((0,), (0,)), ((), ())), precision=precision, preferred_element_type=F32
    )


def iota(shape, dim):
    return lax.broadcasted_iota(jnp.int32, shape, dim)


def shape_of(shape, dtype):
    return jax.ShapeDtypeStruct(shape, dtype)


def run(kernel, scalars, operands, outs, scratch=(), flops=0):
    moved = sum(x.size * x.dtype.itemsize for x in list(operands) + list(outs))
    return pl.pallas_call(
        kernel,
        out_shape=list(outs),
        in_specs=[pl.BlockSpec(memory_space=pltpu.SMEM)]
        + [pl.BlockSpec(memory_space=pltpu.VMEM)] * len(operands),
        out_specs=[pl.BlockSpec(memory_space=pltpu.VMEM)] * len(outs),
        scratch_shapes=list(scratch),
        compiler_params=pltpu.CompilerParams(vmem_limit_bytes=VMEM_BYTES),
        cost_estimate=pl.CostEstimate(flops=flops, bytes_accessed=moved, transcendentals=0),
    )(scalars, *operands)


def inverse_rms(values):
    return lax.rsqrt(jnp.mean(values * values, axis=-1, keepdims=True) + EPSILON)


def router_softmax(rows, router, expert_count):
    logits = matmul(rows, router)
    logits = jnp.where(iota(logits.shape, 1) < expert_count, logits, MASKED_SCORE)
    weights = jnp.exp(logits - jnp.max(logits, axis=-1, keepdims=True))
    return weights / jnp.sum(weights, axis=-1, keepdims=True)


def swap(values, axis, mask):
    count = lax.axis_size(axis)
    return lax.ppermute(values, axis, [(i, i ^ mask) for i in range(count)])


def stacked(pieces):
    parts = [piece[...].astype(F32) for piece in pieces]
    return parts[0] if len(parts) == 1 else jnp.concatenate(parts, axis=0)


def store_pieces(refs, values):
    rows = values.shape[0] // len(refs)
    for number, ref in enumerate(refs):
        ref[...] = values[number * rows : (number + 1) * rows].astype(ref.dtype)


def body(
    tokens,
    cotangent,
    query_weight,
    key_weight,
    value_weight,
    output_weight,
    attention_scale,
    expert_scale,
    router,
    bucket_bias,
    expert_up_weight,
    expert_down_weight,
    routes,
    lengths,
    buckets,
):
    row_count, width = tokens.shape
    block_len = routes.shape[0]
    expert_count = router.shape[1]
    bucket_count, local_heads = bucket_bias.shape
    head_width = local_heads * HEAD_DIM
    capacity = max(2, block_len * 5 // (4 * expert_count))
    half = (capacity + 1) // 2
    slot_rows = expert_count * half
    data_count = lax.axis_size("dp")
    shard_rows = width // data_count
    hidden_local = expert_up_weight.shape[1]
    tensor_count = lax.axis_size("tensor")
    span = 2 * block_len

    data_index = lax.axis_index("dp")
    z_index = data_index // SPLIT
    x_index = (data_index // 2) % 2
    c_index = data_index % 2
    y_index = lax.axis_index("tensor")
    scalars = jnp.stack(
        [z_index, x_index, c_index, y_index, lengths[0, 0], lengths[0, 1]]
    ).astype(jnp.int32)

    staged = shard_rows % 16 == 0
    slot_pieces = expert_count if half % 8 == 0 else 1
    z_masks = [j * SPLIT for j in range(expert_count)]

    def over_z(pieces):
        if len(pieces) == 1:
            stack = pieces[0].reshape((expert_count, half) + pieces[0].shape[1:])
            moved = [stack[0]] + [swap(stack[j], "dp", z_masks[j]) for j in range(1, expert_count)]
            return [jnp.concatenate(moved, axis=0)]
        return [pieces[0]] + [swap(pieces[j], "dp", z_masks[j]) for j in range(1, expert_count)]

    small_columns = -(-(expert_count + 2) // LANES) * LANES
    weight_columns = 4 * head_width
    packed = jnp.concatenate(
        [
            query_weight,
            key_weight,
            value_weight,
            output_weight,
            router,
            attention_scale[:, None],
            expert_scale[:, None],
            jnp.zeros((shard_rows, small_columns - expert_count - 2), BF16),
        ],
        axis=1,
    )
    if staged:
        gathered = [packed] + [swap(packed, "dp", mask) for mask in z_masks[1:]]
        gathered = gathered + [swap(piece, "dp", 2) for piece in gathered]
        gathered = gathered + [swap(piece, "dp", 1) for piece in gathered]
    else:
        gathered = [lax.all_gather(packed, "dp", axis=0, tiled=True)]

    def piece_offset(idx, number):
        j_z = number % expert_count
        j_x = (number // expert_count) % 2
        j_c = number // (2 * expert_count)
        index = (idx[Z_AT] ^ j_z) * SPLIT + (idx[X_AT] ^ j_x) * 2 + (idx[C_AT] ^ j_c)
        return pl.multiple_of(index * shard_rows, 16)

    tokens_other = swap(tokens, "tensor", 1)
    cotangent_other = swap(cotangent, "tensor", 1)

    def spread(weight):
        over_y = swap(weight, "tensor", 1)
        return [weight, over_y, swap(weight, "dp", 1), swap(over_y, "dp", 1)]

    up_parts = spread(expert_up_weight)
    down_parts = spread(expert_down_weight)

    bucket_row = jnp.pad(buckets, (0, span - buckets.shape[0]), constant_values=-1)[None, :]
    bucket_back = jnp.pad(buckets[::-1], (0, span - buckets.shape[0]), constant_values=-1)[None, :]
    table_rows = jnp.pad(bucket_bias.T, ((0, 8 - local_heads), (0, 0)))
    route_row = routes.reshape(1, block_len)

    def live_row(idx):
        position = iota((1, block_len), 1)
        return (position < idx[FIRST_AT] + idx[SECOND_AT]).astype(F32)

    def live_column(idx):
        position = iota((block_len, 1), 0)
        return (position < idx[FIRST_AT] + idx[SECOND_AT]).astype(F32)

    def prepare(idx, bucket_ref, table_ref, route_ref, tok, tok_other, cot, cot_other, *refs):
        x_ref, bias_ref, own_ref, other_ref, xs_ref, gs_ref, live_ref, pick_ref = refs[:8]
        live_parts = refs[8:-1]
        cot_full = refs[-1]
        own_at = pl.multiple_of(idx[Y_AT] * row_count, row_count)
        other_at = pl.multiple_of((1 - idx[Y_AT]) * row_count, row_count)
        x_ref[pl.ds(own_at, row_count), :] = tok[...]
        x_ref[pl.ds(other_at, row_count), :] = tok_other[...]
        cot_full[pl.ds(own_at, row_count), :] = cot[...]
        cot_full[pl.ds(other_at, row_count), :] = cot_other[...]

        first, active = idx[FIRST_AT], idx[FIRST_AT] + idx[SECOND_AT]

        def segment(position):
            return jnp.where(position < first, 0, jnp.where(position < active, 1, 2))

        allowed = segment(iota((block_len, block_len), 0)) == segment(
            iota((block_len, block_len), 1)
        )
        pick = (bucket_ref[...] == iota((bucket_count, span), 0)).astype(F32)
        head_table = matmul(table_ref[...], pick, HIGHEST)
        for head in range(local_heads):
            line = jnp.broadcast_to(head_table[head : head + 1, :], (block_len, span))
            turned = pltpu.roll(line, block_len + 1, 1, stride=1, stride_axis=0)
            bias_ref[head] = jnp.where(allowed, turned[:, :block_len], MASKED_SCORE)

        route = route_ref[...]
        chosen = (route == iota((LANES, block_len), 0)).astype(F32)
        earlier = (iota((block_len, block_len), 0) < iota((block_len, block_len), 1)).astype(F32)
        counts = matmul(chosen.astype(BF16), earlier.astype(BF16))
        slot = jnp.sum(chosen * counts, axis=0, keepdims=True).astype(jnp.int32)
        row_id = iota((slot_rows, block_len), 0)

        def selection(which):
            place = slot - half * which
            code = (route ^ idx[Z_AT]) * half + place
            code = jnp.where((place >= 0) & (place < half), code, -1)
            return (row_id == code).astype(F32)

        own_select = selection(idx[Y_AT])
        own_bf = own_select.astype(BF16)
        own_ref[...] = own_bf
        other_ref[...] = selection(1 - idx[Y_AT]).astype(BF16)
        xs_ref[...] = matmul(own_bf, x_ref[...]).astype(BF16)
        gs_ref[...] = matmul(own_bf, cot_full[...]).astype(BF16)
        live_select = own_select * live_row(idx)
        live_ref[...] = jnp.broadcast_to(
            jnp.sum(live_select, axis=1, keepdims=True), live_ref.shape
        )
        pick_ref[...] = matmul_nt(own_bf, chosen.astype(BF16))
        store_pieces(live_parts, matmul(live_select.astype(BF16), cot_full[...]))

    piece_shape = shape_of((slot_rows // slot_pieces, width), BF16)
    prepared = run(
        prepare,
        scalars,
        [bucket_row, table_rows, route_row, tokens, tokens_other, cotangent, cotangent_other],
        [
            shape_of((block_len, width), BF16),
            shape_of((local_heads, block_len, block_len), F32),
            shape_of((slot_rows, block_len), BF16),
            shape_of((slot_rows, block_len), BF16),
            shape_of((slot_rows, width), BF16),
            shape_of((slot_rows, width), BF16),
            shape_of((slot_rows, LANES), F32),
            shape_of((slot_rows, LANES), F32),
        ]
        + [piece_shape] * slot_pieces,
        [pltpu.VMEM((block_len, width), BF16)],
        flops=10**9,
    )
    x_full, bias, own_select, other_select, x_slot, g_slot, live_slot, pick_slot = prepared[:8]
    g_home = prepared[8:]

    def to_experts(pieces):
        arrived = over_z(list(pieces))
        return arrived + [swap(piece, "dp", 2) for piece in arrived]

    g_rows = to_experts(g_home)

    qkv_width = 3 * head_width
    piece_count = len(gathered)

    def attend(idx, x_ref, bias_ref, own_ref, other_ref, xs_ref, *refs):
        pieces = refs[:piece_count]
        (
            send_ref,
            keep_ref,
            normed_ref,
            qkv_ref,
            probs_ref,
            context_ref,
            weight_ref,
            small_ref,
            gain_ref,
        ) = refs[piece_count:]
        if piece_count == 1:
            weight_ref[...] = pieces[0][:, :weight_columns]
            small_ref[...] = pieces[0][:, weight_columns:]
        else:
            for number, piece in enumerate(pieces):
                at = piece_offset(idx, number)
                weight_ref[pl.ds(at, shard_rows), :] = piece[:, :weight_columns]
                small_ref[pl.ds(at, shard_rows), :] = piece[:, weight_columns:]
        turned = small_ref[...].astype(F32).T
        gain = turned[expert_count : expert_count + 1, :]
        gain_ref[...] = jnp.broadcast_to(gain, gain_ref.shape)
        gain_ref[1:2, :] = turned[expert_count + 1 : expert_count + 2, :]
        x = x_ref[...].astype(F32)
        normed = (x * inverse_rms(x) * gain).astype(BF16)
        normed_ref[...] = normed
        qkv_ref[...] = matmul(normed, weight_ref[:, :qkv_width]).astype(BF16)
        live = live_column(idx)
        for head in range(local_heads):
            at = head * HEAD_DIM
            query = qkv_ref[:, at : at + HEAD_DIM]
            key = qkv_ref[:, head_width + at : head_width + at + HEAD_DIM]
            value = qkv_ref[:, 2 * head_width + at : 2 * head_width + at + HEAD_DIM]
            scores = matmul_nt(query, key) * SCORE_SCALE + bias_ref[head]
            weights = jnp.exp(scores - jnp.max(scores, axis=-1, keepdims=True))
            probs = weights / jnp.sum(weights, axis=-1, keepdims=True)
            probs_ref[head] = probs
            context = matmul(probs.astype(BF16), value) * live
            context_ref[:, at : at + HEAD_DIM] = context.astype(BF16)
        out = matmul_nt(context_ref[...], weight_ref[:, qkv_width:]).astype(BF16)
        send_ref[...] = matmul(other_ref[...], out).astype(BF16)
        keep_ref[...] = matmul(own_ref[...], out) + xs_ref[...].astype(F32)

    send, keep, normed, qkv, probs, context, weights, router_small, gains = run(
        attend,
        scalars,
        [x_full, bias, own_select, other_select, x_slot] + gathered,
        [
            shape_of((slot_rows, width), BF16),
            shape_of((slot_rows, width), F32),
            shape_of((block_len, width), BF16),
            shape_of((block_len, qkv_width), BF16),
            shape_of((local_heads, block_len, block_len), F32),
            shape_of((block_len, head_width), BF16),
            shape_of((width, weight_columns), BF16),
            shape_of((width, small_columns), BF16),
            shape_of((8, width), F32),
        ],
        flops=10**9,
    )
    arrived = swap(send, "tensor", 1)

    def second_norm(idx, keep_ref, arrived_ref, gain_ref, residual_ref, scale_ref, nm_ref, *parts):
        residual = keep_ref[...] + arrived_ref[...].astype(F32)
        scale = inverse_rms(residual)
        residual_ref[...] = residual
        scale_ref[...] = jnp.broadcast_to(scale, scale_ref.shape)
        rows = residual * scale * gain_ref[1:2, :]
        nm_ref[...] = rows.astype(BF16)
        store_pieces(parts, rows)

    residual, scale_moe, normed_moe, *row_home = run(
        second_norm,
        scalars,
        [keep, arrived, gains],
        [
            shape_of((slot_rows, width), F32),
            shape_of((slot_rows, LANES), F32),
            shape_of((slot_rows, width), BF16),
        ]
        + [piece_shape] * slot_pieces,
        flops=10**6,
    )
    expert_rows = to_experts(row_home)

    expert_in = 2 * slot_rows
    parts = len(up_parts)

    def experts(idx, router_ref, *refs):
        count = 2 * slot_pieces
        row_parts, refs = refs[:count], refs[count:]
        g_parts, refs = refs[:count], refs[count:]
        up, refs = refs[:parts], refs[parts:]
        down, refs = refs[:parts], refs[parts:]
        send_ref, keep_ref, rows_ref, total_ref, hidden_ref, pre_ref = refs
        rows = stacked(row_parts).astype(BF16)
        rows_ref[...] = rows
        routed = router_softmax(rows, router_ref[...], expert_count)
        mine = (iota(routed.shape, 1) == idx[Z_AT]).astype(F32)
        gate = jnp.sum(routed * mine, axis=1, keepdims=True)
        total = (stacked(g_parts) * gate).astype(BF16)
        total_ref[...] = total
        forward = jnp.zeros((expert_in, width), F32)
        backward = jnp.zeros((expert_in, width), F32)
        for part in range(parts):
            at = part * hidden_local
            pre = matmul(rows, up[part][...])
            square = pre * pre
            inner = 0.7978845608028654 * pre * (1.0 + 0.044715 * square)
            tanh = jnp.tanh(inner)
            hidden = (0.5 * pre * (1.0 + tanh)).astype(BF16)
            slope = 0.5 * (1.0 + tanh) + 0.5 * pre * (1.0 - tanh * tanh) * (
                0.7978845608028654 * (1.0 + 3.0 * 0.044715 * square)
            )
            hidden_ref[:, at : at + hidden_local] = hidden
            grad_pre = (matmul(total, down[part][...]) * slope).astype(BF16)
            pre_ref[:, at : at + hidden_local] = grad_pre
            forward += matmul_nt(hidden, down[part][...])
            backward += matmul_nt(grad_pre, up[part][...])
        keep_ref[:, :width] = forward[:slot_rows]
        keep_ref[:, width:] = backward[:slot_rows]
        send_ref[:, :width] = forward[slot_rows:].astype(BF16)
        send_ref[:, width:] = backward[slot_rows:].astype(BF16)

    send, keep, rows_in, total_in, hidden, grad_pre = run(
        experts,
        scalars,
        [router_small] + expert_rows + g_rows + up_parts + down_parts,
        [
            shape_of((slot_rows, 2 * width), BF16),
            shape_of((slot_rows, 2 * width), F32),
            shape_of((expert_in, width), BF16),
            shape_of((expert_in, width), BF16),
            shape_of((expert_in, parts * hidden_local), BF16),
            shape_of((expert_in, parts * hidden_local), BF16),
        ],
        flops=3 * 10**9,
    )
    arrived = swap(send, "dp", 2)

    def add_x(idx, keep_ref, arrived_ref, *parts_out):
        store_pieces(parts_out, keep_ref[...] + arrived_ref[...].astype(F32))

    both_shape = shape_of((slot_rows // slot_pieces, 2 * width), BF16)
    back = run(add_x, scalars, [keep, arrived], [both_shape] * slot_pieces, flops=10**6)
    home = over_z(list(back))

    def expert_grads(idx, rows_ref, total_ref, hidden_ref, pre_ref, *outs):
        for part in range(parts):
            at = part * hidden_local
            up_grad, down_grad = outs[2 * part : 2 * part + 2]
            up_grad[...] = matmul_tn(rows_ref[...], pre_ref[:, at : at + hidden_local]).astype(
                up_grad.dtype
            )
            down_grad[...] = matmul_tn(
                total_ref[...], hidden_ref[:, at : at + hidden_local]
            ).astype(down_grad.dtype)

    weight_shape = (width, hidden_local)
    weight_grads = run(
        expert_grads,
        scalars,
        [rows_in, total_in, hidden, grad_pre],
        [shape_of(weight_shape, F32)] * 2 + [shape_of(weight_shape, BF16)] * (2 * parts - 2),
        flops=2 * 10**9,
    )

    def scatter_expert(own, over_y, over_c, over_yc):
        from_c = swap(over_c, "dp", 1)
        from_yc = swap(over_yc, "dp", 1)
        passed = (over_y.astype(F32) + from_yc.astype(F32)).astype(BF16)
        return own + from_c.astype(F32) + swap(passed, "tensor", 1).astype(F32)

    grad_w_in = scatter_expert(*weight_grads[0::2])
    grad_w_out = scatter_expert(*weight_grads[1::2])

    expert_pad = -(-expert_count // 8) * 8

    def at_home(idx, *refs):
        pieces, refs = refs[:slot_pieces], refs[slot_pieces:]
        (
            residual_ref,
            scale_ref,
            nm_ref,
            g_ref,
            live_ref,
            pick_ref,
            gain_ref,
            router_ref,
            mid_ref,
            layer_ref,
            gain_out,
            router_out,
        ) = refs
        returned = stacked(pieces)
        total, back_rows = returned[:, :width], returned[:, width:]
        residual = residual_ref[...]
        scale = scale_ref[:, :1]
        live = live_ref[:, :1]
        pick = pick_ref[...]
        gain = gain_ref[1:2, :]
        g = g_ref[...].astype(F32)
        routed = router_softmax(nm_ref[...], router_ref[...], expert_count)
        gate = jnp.sum(routed * pick, axis=1, keepdims=True)
        layer_ref[...] = (residual + gate * total * live).astype(BF16)
        grad_gate = jnp.sum(g * total, axis=1, keepdims=True) * live
        grad_logits = grad_gate * gate * (pick - routed)
        upstream = back_rows + matmul_nt(grad_logits, router_ref[...].astype(F32), HIGHEST)
        scaled = upstream * gain
        grad_mid = (
            g
            + scale * scaled
            - residual * scale**3 * jnp.mean(scaled * residual, axis=-1, keepdims=True)
        )
        mid_ref[...] = grad_mid.astype(BF16)
        gain_out[...] = jnp.broadcast_to(
            jnp.sum(upstream * residual * scale, axis=0, keepdims=True), gain_out.shape
        )
        router_grad = matmul_tn(grad_logits, nm_ref[...].astype(F32), HIGHEST)
        router_out[...] = router_grad[:expert_pad]

    mid_own, layer_own, gain_moe, router_part = run(
        at_home,
        scalars,
        home
        + [residual, scale_moe, normed_moe, g_slot, live_slot, pick_slot, gains, router_small],
        [
            shape_of((slot_rows, width), BF16),
            shape_of((slot_rows, width), BF16),
            shape_of((8, width), F32),
            shape_of((expert_pad, width), F32),
        ],
        flops=10**8,
    )
    mid_other = swap(mid_own, "tensor", 1)
    layer_other = swap(layer_own, "tensor", 1)

    half_pieces = 2 * expert_count

    def emit_rows(idx, full_ref, outs):
        if not staged:
            outs[0][...] = full_ref[...].astype(BF16)
            return
        keep_ref, send_ref = outs
        for number in range(half_pieces):
            at = piece_offset(idx, number)
            keep_ref[number] = full_ref[pl.ds(at, shard_rows), :]
            at = piece_offset(idx, number + half_pieces)
            send_ref[number] = full_ref[pl.ds(at, shard_rows), :].astype(BF16)

    def row_shapes(columns):
        if not staged:
            return [shape_of((width, columns), BF16)]
        return [
            shape_of((half_pieces, shard_rows, columns), F32),
            shape_of((half_pieces, shard_rows, columns), BF16),
        ]

    def reduce_rows(outs):
        if not staged:
            return lax.psum_scatter(
                outs[0].astype(F32), "dp", scatter_dimension=0, tiled=True
            )
        held, send = outs
        held = held + swap(send, "dp", 1).astype(F32)
        held = held[:expert_count] + swap(
            held[expert_count:].astype(BF16), "dp", 2
        ).astype(F32)
        total = held[0]
        for j in range(1, expert_count):
            total = total + swap(held[j].astype(BF16), "dp", z_masks[j]).astype(F32)
        return total

    def output_grad(idx, own_ref, other_ref, mid_ref, mid_other_ref, context_ref, ga_ref, *refs):
        full = refs[-1]
        grad = matmul_tn(own_ref[...], mid_ref[...]) + matmul_tn(
            other_ref[...], mid_other_ref[...]
        )
        grad = grad.astype(BF16)
        ga_ref[...] = grad
        full[...] = matmul_tn(grad, context_ref[...])
        emit_rows(idx, full, refs[:-1])

    grad_attention, *output_rows = run(
        output_grad,
        scalars,
        [own_select, other_select, mid_own, mid_other, context],
        [shape_of((block_len, width), BF16)] + row_shapes(head_width),
        [pltpu.VMEM((width, head_width), F32)],
        flops=4 * 10**8,
    )
    grad_wo = reduce_rows(output_rows)

    def attend_back(
        idx, ga_ref, weight_ref, qkv_ref, probs_ref, normed_ref, x_ref, bucket_ref, *refs
    ):
        keep_ref, send_ref, gain_ref, table_ref = refs[:4]
        outs = refs[4:-3]
        grads, full, upstream = refs[-3:]
        live = live_column(idx)
        grad_context = matmul(ga_ref[...], weight_ref[:, qkv_width:]) * live
        grad_context = grad_context.astype(BF16)
        mirror = (
            iota((block_len, block_len), 0) + iota((block_len, block_len), 1) == block_len - 1
        ).astype(BF16)
        lines = []
        for head in range(local_heads):
            at = head * HEAD_DIM
            query = qkv_ref[:, at : at + HEAD_DIM]
            key = qkv_ref[:, head_width + at : head_width + at + HEAD_DIM]
            value = qkv_ref[:, 2 * head_width + at : 2 * head_width + at + HEAD_DIM]
            back = grad_context[:, at : at + HEAD_DIM]
            probs = probs_ref[head]
            grad_value = matmul_tn(probs.astype(BF16), back)
            grad_probs = matmul_nt(back, value)
            grad_scores = probs * (
                grad_probs - jnp.sum(probs * grad_probs, axis=-1, keepdims=True)
            )
            grad_scores = grad_scores.astype(BF16)
            grad_query = matmul(grad_scores, key) * SCORE_SCALE
            grad_key = matmul_tn(grad_scores, query) * SCORE_SCALE
            grads[:, at : at + HEAD_DIM] = grad_query.astype(BF16)
            grads[:, head_width + at : head_width + at + HEAD_DIM] = grad_key.astype(BF16)
            grads[:, 2 * head_width + at : 2 * head_width + at + HEAD_DIM] = grad_value.astype(
                BF16
            )
            lines_left = jnp.concatenate(
                [matmul(grad_scores, mirror), jnp.zeros((block_len, span - block_len), F32)], axis=1
            )
            rows = block_len
            while rows > 8:
                rows //= 2
                lines_left = lines_left[:rows] + pltpu.roll(lines_left[rows:], rows, 1)
            lines_left = pltpu.roll(lines_left, 0, 1, stride=1, stride_axis=0)
            lines.append(jnp.sum(lines_left, axis=0, keepdims=True))
        lines.append(jnp.zeros((8 - local_heads, span), F32))
        diagonal = jnp.concatenate(lines, axis=0)
        pick = (bucket_ref[...] == iota((LANES, span), 0)).astype(F32)
        table = matmul_nt(diagonal, pick, HIGHEST)
        table_ref[...] = jnp.zeros(table_ref.shape, F32)
        for head in range(local_heads):
            table_ref[:1, head * LANES : (head + 1) * LANES] = table[head : head + 1, :]
        all_grads = grads[...]
        grad_normed = matmul_nt(all_grads, weight_ref[:, :qkv_width])
        upstream[...] = grad_normed
        x = x_ref[...].astype(F32)
        gain_ref[...] = jnp.broadcast_to(
            jnp.sum(grad_normed * x * inverse_rms(x), axis=0, keepdims=True), gain_ref.shape
        )
        own_at = pl.multiple_of(idx[Y_AT] * row_count, row_count)
        other_at = pl.multiple_of((1 - idx[Y_AT]) * row_count, row_count)
        keep_ref[...] = upstream[pl.ds(own_at, row_count), :]
        send_ref[...] = upstream[pl.ds(other_at, row_count), :].astype(BF16)
        full[...] = matmul_tn(normed_ref[...], all_grads)
        emit_rows(idx, full, outs)

    up_keep, up_send, gain_attn, table_part, *qkv_rows = run(
        attend_back,
        scalars,
        [grad_attention, weights, qkv, probs, normed, x_full, bucket_back],
        [
            shape_of((row_count, width), F32),
            shape_of((row_count, width), BF16),
            shape_of((8, width), F32),
            shape_of((8, local_heads * LANES), F32),
        ]
        + row_shapes(qkv_width),
        [
            pltpu.VMEM((block_len, qkv_width), BF16),
            pltpu.VMEM((width, qkv_width), F32),
            pltpu.VMEM((block_len, width), F32),
        ],
        flops=2 * 10**9,
    )
    up_other = swap(up_send, "tensor", 1)
    grad_qkv = reduce_rows(qkv_rows)

    table_line = jnp.pad(table_part[0], (0, width - local_heads * LANES))
    table_lines = jnp.where(
        jnp.arange(tensor_count)[:, None] == y_index, table_line[None, :], 0.0
    )
    small = jnp.concatenate(
        [gain_attn[:1], gain_moe[:1], router_part[:expert_count], table_lines], axis=0
    )
    small = jnp.pad(small, ((0, -small.shape[0] % 8), (0, 0)))
    small = small + swap(small, "tensor", 1)
    if staged:
        small = small + swap(small, "dp", 1)
        small = small + swap(small, "dp", 2)
        moved = [swap(small, "dp", mask) for mask in z_masks[1:]]
        for piece in moved:
            small = small + piece
    else:
        small = lax.psum(small, "dp")
    shard = lax.dynamic_slice_in_dim(small, data_index * shard_rows, shard_rows, 1)
    table = lax.dynamic_slice_in_dim(small, 2 + expert_count + y_index, 1, 0)
    table = table[0, : local_heads * LANES].reshape(local_heads, LANES)[:, :bucket_count].T

    def finish(
        idx, own_ref, other_ref, layer_ref, layer_other_ref, ga_ref, keep_ref, arrived_ref,
        tok_ref, gain_ref, layer_out, tokens_out, full
    ):
        own_at = pl.multiple_of(idx[Y_AT] * row_count, row_count)
        full[...] = matmul_tn(own_ref[...], layer_ref[...]) + matmul_tn(
            other_ref[...], layer_other_ref[...]
        )
        layer_out[...] = full[pl.ds(own_at, row_count), :].astype(BF16)
        x = tok_ref[...].astype(F32)
        scale = inverse_rms(x)
        scaled = (keep_ref[...] + arrived_ref[...].astype(F32)) * gain_ref[:1, :]
        grad = scale * scaled - x * scale**3 * jnp.mean(scaled * x, axis=-1, keepdims=True)
        grad = grad + ga_ref[pl.ds(own_at, row_count), :].astype(F32)
        tokens_out[...] = grad.astype(BF16)

    layer_out, grad_tokens = run(
        finish,
        scalars,
        [
            own_select, other_select, layer_own, layer_other, grad_attention, up_keep, up_other,
            tokens, gains,
        ],
        [shape_of((row_count, width), BF16)] * 2,
        [pltpu.VMEM((block_len, width), F32)],
        flops=10**8,
    )

    return (
        layer_out,
        grad_tokens,
        grad_qkv[:, :head_width],
        grad_qkv[:, head_width : 2 * head_width],
        grad_qkv[:, 2 * head_width :],
        grad_wo,
        shard[0],
        shard[1],
        shard[2 : 2 + expert_count].T,
        table,
        grad_w_in,
        grad_w_out,
    )


def solution(mesh):
    in_specs = (
        P(("dp", "tensor"), None),
        P(("dp", "tensor"), None),
        P("dp", "tensor"),
        P("dp", "tensor"),
        P("dp", "tensor"),
        P("dp", "tensor"),
        P("dp"),
        P("dp"),
        P("dp", None),
        P(None, "tensor"),
        P(None, ("dp", "tensor")),
        P(None, ("dp", "tensor")),
        P("dp", None),
        P("dp", None),
        P(),
    )
    out_specs = (
        P(("dp", "tensor"), None),
        P(("dp", "tensor"), None),
        P("dp", "tensor"),
        P("dp", "tensor"),
        P("dp", "tensor"),
        P("dp", "tensor"),
        P("dp"),
        P("dp"),
        P("dp", None),
        P(None, "tensor"),
        P(None, ("dp", "tensor")),
        P(None, ("dp", "tensor")),
    )
    return jax.shard_map(body, mesh=mesh, in_specs=in_specs, out_specs=out_specs, check_vma=False)
```

```python
import jax
import jax.numpy as jnp
from jax import lax
from jax.experimental import pallas as pl
from jax.experimental.pallas import tpu as pltpu
from jax.sharding import PartitionSpec as P

HEAD_DIM = 64
SPLIT = 4
EPSILON = 1e-06
MASKED_SCORE = -1e30
LANES = 128
SCORE_SCALE = HEAD_DIM ** (-0.5)
HIGHEST = lax.Precision.HIGHEST
VMEM_BYTES = 20 * 1024 * 1024
VMEM_MOST = 60 * 1024 * 1024
F32 = jnp.float32
BF16 = jnp.bfloat16

Z_AT, X_AT, C_AT, Y_AT, DATA_AT = range(5)


class Place:
    def __init__(self, ref):
        self.ref = ref

    def __getitem__(self, which):
        place = self.ref[0]
        return {
            Z_AT: place // (2 * SPLIT),
            X_AT: (place // 4) % 2,
            C_AT: (place // 2) % 2,
            Y_AT: place % 2,
            DATA_AT: place // 2,
        }[which]


def matmul(left, right, precision=None):
    return jnp.dot(left, right, precision=precision, preferred_element_type=F32)


def matmul_nt(left, right, precision=None):
    return lax.dot_general(
        left, right, (((1,), (1,)), ((), ())), precision=precision, preferred_element_type=F32
    )


def matmul_tn(left, right, precision=None):
    return lax.dot_general(
        left, right, (((0,), (0,)), ((), ())), precision=precision, preferred_element_type=F32
    )


def iota(shape, dim):
    return lax.broadcasted_iota(jnp.int32, shape, dim)


def shape_of(shape, dtype):
    return jax.ShapeDtypeStruct(shape, dtype)


def run(kernel, scalars, operands, outs, scratch=(), flops=1, after=(), far=0, far_outs=0, vmem=VMEM_BYTES):
    waits = len(after)

    def wrapped(place_ref, *refs):
        kernel(Place(place_ref), *refs[waits:])

    return pl.pallas_call(
        wrapped,
        out_shape=list(outs),
        in_specs=[pl.BlockSpec(memory_space=pltpu.SMEM)]
        + [pl.BlockSpec(memory_space=pl.ANY)] * waits
        + [pl.BlockSpec(memory_space=pltpu.HBM)] * far
        + [pl.BlockSpec(memory_space=pltpu.VMEM)] * (len(operands) - far),
        out_specs=[pl.BlockSpec(memory_space=pltpu.HBM)] * far_outs
        + [pl.BlockSpec(memory_space=pltpu.VMEM)] * (len(outs) - far_outs),
        scratch_shapes=list(scratch),
        compiler_params=pltpu.CompilerParams(vmem_limit_bytes=vmem),
        cost_estimate=pl.CostEstimate(flops=flops, bytes_accessed=1, transcendentals=0),
    )(scalars, *after, *operands)


def inverse_rms(values):
    return lax.rsqrt(jnp.mean(values * values, axis=-1, keepdims=True) + EPSILON)


def router_softmax(rows, router, expert_count):
    logits = matmul(rows, router)
    logits = jnp.where(iota(logits.shape, 1) < expert_count, logits, MASKED_SCORE)
    weights = jnp.exp(logits - jnp.max(logits, axis=-1, keepdims=True))
    return weights / jnp.sum(weights, axis=-1, keepdims=True)


def swap(values, axis, mask):
    count = lax.axis_size(axis)
    return lax.ppermute(values, axis, [(i, i ^ mask) for i in range(count)])


def stacked(pieces):
    parts = [piece[...].astype(F32) for piece in pieces]
    return parts[0] if len(parts) == 1 else jnp.concatenate(parts, axis=0)


def store_pieces(refs, values):
    rows = values.shape[0] // len(refs)
    for number, ref in enumerate(refs):
        ref[...] = values[number * rows : (number + 1) * rows].astype(ref.dtype)


def body(
    tokens,
    cotangent,
    query_weight,
    key_weight,
    value_weight,
    output_weight,
    attention_scale,
    expert_scale,
    router,
    bucket_bias,
    expert_up_weight,
    expert_down_weight,
    routes,
    lengths,
    buckets,
):
    row_count, width = tokens.shape
    block_len = routes.shape[0]
    expert_count = router.shape[1]
    bucket_count, local_heads = bucket_bias.shape
    head_width = local_heads * HEAD_DIM
    capacity = max(2, block_len * 5 // (4 * expert_count))
    half = (capacity + 1) // 2
    slot_rows = expert_count * half
    data_count = lax.axis_size("dp")
    shard_rows = width // data_count
    hidden_local = expert_up_weight.shape[1]
    tensor_count = lax.axis_size("tensor")
    span = 2 * block_len
    distances = buckets.shape[0]

    data_index = lax.axis_index("dp")
    y_index = lax.axis_index("tensor")
    scalars = (data_index * 2 + y_index).astype(jnp.int32).reshape(1)

    staged = shard_rows % 16 == 0
    slot_pieces = expert_count if half % 8 == 0 else 1
    z_masks = [j * SPLIT for j in range(expert_count)]

    def over_z(pieces):
        if len(pieces) == 1:
            stack = pieces[0].reshape((expert_count, half) + pieces[0].shape[1:])
            moved = [stack[0]] + [swap(stack[j], "dp", z_masks[j]) for j in range(1, expert_count)]
            return [jnp.concatenate(moved, axis=0)]
        return [pieces[0]] + [swap(pieces[j], "dp", z_masks[j]) for j in range(1, expert_count)]

    small_columns = -(-(expert_count + 2) // LANES) * LANES
    weight_columns = 4 * head_width
    def pack(idx, *refs):
        sources, refs = refs[:15], refs[15:]
        (both_ref, out_ref, rows_ref, *small_refs), refs = refs[:7], refs[7:]
        router_ref, attn_ref, moe_ref, sems = refs
        targets = (
            [out_ref.at[:, pl.ds(number * head_width, head_width)] for number in range(4)]
            + [router_ref, attn_ref, moe_ref]
            + [rows_ref.at[pl.ds(number * row_count, row_count), :] for number in range(2)]
            + small_refs
            + [both_ref.at[number] for number in range(2)]
        )
        copies = [
            pltpu.make_async_copy(source, target, sems.at[number])
            for number, (source, target) in enumerate(zip(sources, targets))
        ]
        for copy in copies:
            copy.start()
        for copy in copies[4:7]:
            copy.wait()
        diagonal = iota((shard_rows, shard_rows), 0) == iota((shard_rows, shard_rows), 1)
        lane = iota((shard_rows, small_columns), 1)

        def column(row_ref):
            row = row_ref[...].astype(F32)
            return jnp.sum(jnp.where(diagonal, row, 0.0), axis=1, keepdims=True)

        spread_router = matmul_tn(
            router_ref[...],
            (iota((expert_count, small_columns), 0) == iota((expert_count, small_columns), 1))
            .astype(F32)
            .astype(BF16),
        )
        small = jnp.where(lane == expert_count, column(attn_ref), spread_router)
        small = jnp.where(lane == expert_count + 1, column(moe_ref), small)
        out_ref[:, weight_columns:] = small.astype(BF16)
        for copy in copies[:4] + copies[7:]:
            copy.wait()

    expert_own, packed, rows_own, length_row, bucket_row, table_rows, route_row = run(
        pack,
        scalars,
        [
            query_weight,
            key_weight,
            value_weight,
            output_weight,
            router.T,
            attention_scale[None, :],
            expert_scale[None, :],
            tokens,
            cotangent,
            lengths,
            buckets[None, :],
            bucket_bias.T,
            routes.reshape(1, block_len),
            expert_up_weight,
            expert_down_weight,
        ],
        [
            shape_of((2, width, hidden_local), BF16),
            shape_of((shard_rows, weight_columns + small_columns), BF16),
            shape_of((2 * row_count, width), BF16),
            shape_of(lengths.shape, jnp.int32),
            shape_of((1, distances), jnp.int32),
            shape_of((local_heads, bucket_count), F32),
            shape_of((1, block_len), jnp.int32),
        ],
        [
            pltpu.VMEM((expert_count, shard_rows), BF16),
            pltpu.VMEM((1, shard_rows), BF16),
            pltpu.VMEM((1, shard_rows), BF16),
            pltpu.SemaphoreType.DMA((15,)),
        ],
        far=15,
        vmem=VMEM_MOST,
    )
    if staged:
        gathered = [packed] + [swap(packed, "dp", mask) for mask in z_masks[1:]]
        gathered = gathered + [swap(piece, "dp", 2) for piece in gathered]
        gathered = gathered + [swap(piece, "dp", 1) for piece in gathered]
    else:
        gathered = [lax.all_gather(packed, "dp", axis=0, tiled=True)]

    def piece_offset(idx, number):
        j_z = number % expert_count
        j_x = (number // expert_count) % 2
        j_c = number // (2 * expert_count)
        index = (idx[Z_AT] ^ j_z) * SPLIT + (idx[X_AT] ^ j_x) * 2 + (idx[C_AT] ^ j_c)
        return pl.multiple_of(index * shard_rows, 16)

    rows_other = swap(rows_own, "tensor", 1)

    def prepare(idx, length_ref, bucket_ref, table_ref, route_ref, mine, others, *refs):
        x_ref, bias_ref, own_ref, other_ref, xs_ref, gs_ref, live_ref = refs[:7]
        pick_ref, back_ref, live_rows_ref = refs[7:10]
        live_parts = refs[10:-2]
        cot_full, head_table = refs[-2:]
        own_at = pl.multiple_of(idx[Y_AT] * row_count, row_count)
        other_at = pl.multiple_of((1 - idx[Y_AT]) * row_count, row_count)
        for at, rows in ((own_at, mine), (other_at, others)):
            x_ref[pl.ds(at, row_count), :] = rows[:row_count, :]
            cot_full[pl.ds(at, row_count), :] = rows[row_count:, :]

        first = length_ref[:, 0:1]
        active = first + length_ref[:, 1:2]
        live_rows_ref[...] = jnp.broadcast_to(
            (iota((block_len, 1), 0) < active).astype(F32), live_rows_ref.shape
        )

        def segment(position):
            return jnp.where(position < first, 0, jnp.where(position < active, 1, 2))

        allowed = segment(iota((block_len, block_len), 0)) == segment(
            iota((block_len, block_len), 1)
        )
        pick = (bucket_ref[...] == iota((LANES, distances), 0)).astype(F32)
        head_table[...] = jnp.zeros(head_table.shape, F32)
        head_table[:local_heads, :distances] = matmul(
            table_ref[...], pick[:bucket_count], HIGHEST
        )
        mirror = (
            iota((distances, span), 0) + iota((distances, span), 1) == distances - 1
        ).astype(F32)
        back_ref[...] = matmul(pick.astype(BF16), mirror.astype(BF16)).astype(BF16)
        for head in range(local_heads):
            line = jnp.broadcast_to(head_table[head : head + 1, :], (block_len, span))
            turned = pltpu.roll(line, block_len + 1, 1, stride=1, stride_axis=0)
            bias_ref[head] = jnp.where(allowed, turned[:, :block_len], MASKED_SCORE)

        route = route_ref[...]
        chosen = (route == iota((LANES, block_len), 0)).astype(F32)
        earlier = (iota((block_len, block_len), 0) < iota((block_len, block_len), 1)).astype(F32)
        counts = matmul(chosen.astype(BF16), earlier.astype(BF16))
        slot = jnp.sum(chosen * counts, axis=0, keepdims=True).astype(jnp.int32)
        row_id = iota((slot_rows, block_len), 0)

        def selection(which):
            place = slot - half * which
            code = (route ^ idx[Z_AT]) * half + place
            code = jnp.where((place >= 0) & (place < half), code, -1)
            return (row_id == code).astype(F32)

        own_select = selection(idx[Y_AT])
        own_bf = own_select.astype(BF16)
        own_ref[...] = own_bf
        other_ref[...] = selection(1 - idx[Y_AT]).astype(BF16)
        xs_ref[...] = matmul(own_bf, x_ref[...]).astype(BF16)
        gs_ref[...] = matmul(own_bf, cot_full[...]).astype(BF16)
        live_select = own_select * (iota((1, block_len), 1) < active).astype(F32)
        live_ref[...] = jnp.broadcast_to(
            jnp.sum(live_select, axis=1, keepdims=True), live_ref.shape
        )
        pick_ref[...] = matmul_nt(own_bf, chosen.astype(BF16))
        store_pieces(live_parts, matmul(live_select.astype(BF16), cot_full[...]))

    piece_shape = shape_of((slot_rows // slot_pieces, width), BF16)
    prepared = run(
        prepare,
        scalars,
        [length_row, bucket_row, table_rows, route_row, rows_own, rows_other],
        [
            shape_of((block_len, width), BF16),
            shape_of((local_heads, block_len, block_len), F32),
            shape_of((slot_rows, block_len), BF16),
            shape_of((slot_rows, block_len), BF16),
            shape_of((slot_rows, width), BF16),
            shape_of((slot_rows, width), BF16),
            shape_of((slot_rows, LANES), F32),
            shape_of((slot_rows, LANES), F32),
            shape_of((LANES, span), BF16),
            shape_of((block_len, LANES), F32),
        ]
        + [piece_shape] * slot_pieces,
        [pltpu.VMEM((block_len, width), BF16), pltpu.VMEM((8, span), F32)],
    )
    x_full, bias, own_select, other_select, x_slot, g_slot = prepared[:6]
    live_slot, pick_slot, pick_back, live_rows = prepared[6:10]
    g_home = prepared[10:]
    if staged:
        g_home = lax.optimization_barrier((*g_home, *gathered[expert_count : 2 * expert_count]))
        g_home = g_home[:slot_pieces]
    expert_y = swap(expert_own, "tensor", 1)
    expert_c = swap(expert_own, "dp", 1)

    def to_experts(pieces):
        arrived = over_z(list(pieces))
        return arrived + [swap(piece, "dp", 2) for piece in arrived]

    g_rows = over_z(list(g_home))
    g_rows = g_rows + [swap(jnp.concatenate(g_rows, axis=0), "dp", 2)]

    qkv_width = 3 * head_width
    piece_count = len(gathered)

    def attend(idx, live_ref, x_ref, bias_ref, own_ref, other_ref, xs_ref, *refs):
        pieces = refs[:piece_count]
        (
            send_ref,
            keep_ref,
            normed_ref,
            qkv_ref,
            probs_ref,
            context_ref,
            weight_ref,
            small_ref,
            gain_ref,
        ) = refs[piece_count:]
        if piece_count == 1:
            weight_ref[...] = pieces[0][:, :weight_columns]
            small_ref[...] = pieces[0][:, weight_columns:]
        else:
            for number, piece in enumerate(pieces):
                at = piece_offset(idx, number)
                weight_ref[pl.ds(at, shard_rows), :] = piece[:, :weight_columns]
                small_ref[pl.ds(at, shard_rows), :] = piece[:, weight_columns:]
        turned = small_ref[...].astype(F32).T
        gain = turned[expert_count : expert_count + 1, :]
        gain_ref[...] = jnp.broadcast_to(gain, gain_ref.shape)
        gain_ref[1:2, :] = turned[expert_count + 1 : expert_count + 2, :]
        x = x_ref[...].astype(F32)
        normed = (x * inverse_rms(x) * gain).astype(BF16)
        normed_ref[...] = normed
        qkv_ref[...] = matmul(normed, weight_ref[:, :qkv_width]).astype(BF16)
        live = live_ref[:, :1]
        for head in range(local_heads):
            at = head * HEAD_DIM
            query = qkv_ref[:, at : at + HEAD_DIM]
            key = qkv_ref[:, head_width + at : head_width + at + HEAD_DIM]
            value = qkv_ref[:, 2 * head_width + at : 2 * head_width + at + HEAD_DIM]
            scores = matmul_nt(query, key) * SCORE_SCALE + bias_ref[head]
            weights = jnp.exp(scores - jnp.max(scores, axis=-1, keepdims=True))
            probs = weights / jnp.sum(weights, axis=-1, keepdims=True)
            probs_ref[head] = probs
            context = matmul(probs.astype(BF16), value) * live
            context_ref[:, at : at + HEAD_DIM] = context.astype(BF16)
        out = matmul_nt(context_ref[...], weight_ref[:, qkv_width:]).astype(BF16)
        send_ref[...] = matmul(other_ref[...], out).astype(BF16)
        keep_ref[...] = matmul(own_ref[...], out) + xs_ref[...].astype(F32)

    send, keep, normed, qkv, probs, context, weights, router_small, gains = run(
        attend,
        scalars,
        [live_rows, x_full, bias, own_select, other_select, x_slot] + gathered,
        [
            shape_of((slot_rows, width), BF16),
            shape_of((slot_rows, width), F32),
            shape_of((block_len, width), BF16),
            shape_of((block_len, qkv_width), BF16),
            shape_of((local_heads, block_len, block_len), F32),
            shape_of((block_len, head_width), BF16),
            shape_of((width, weight_columns), BF16),
            shape_of((width, small_columns), BF16),
            shape_of((8, width), F32),
        ],
    )
    arrived = swap(send, "tensor", 1)
    expert_y, _ = lax.optimization_barrier((expert_y, send))
    expert_parts = [expert_own, expert_y, expert_c, swap(expert_y, "dp", 1)]

    def second_norm(idx, keep_ref, arrived_ref, gain_ref, residual_ref, scale_ref, nm_ref, *parts):
        residual = keep_ref[...] + arrived_ref[...].astype(F32)
        scale = inverse_rms(residual)
        residual_ref[...] = residual
        scale_ref[...] = jnp.broadcast_to(scale, scale_ref.shape)
        rows = residual * scale * gain_ref[1:2, :]
        nm_ref[...] = rows.astype(BF16)
        store_pieces(parts, rows)

    residual, scale_moe, normed_moe, *row_home = run(
        second_norm,
        scalars,
        [keep, arrived, gains],
        [
            shape_of((slot_rows, width), F32),
            shape_of((slot_rows, LANES), F32),
            shape_of((slot_rows, width), BF16),
        ]
        + [piece_shape] * slot_pieces,
    )
    expert_rows = to_experts(row_home)

    expert_in = 2 * slot_rows
    parts = len(expert_parts)

    def experts(idx, router_ref, *refs):
        count = 2 * slot_pieces
        row_parts, refs = refs[:count], refs[count:]
        g_parts, refs = refs[: slot_pieces + 1], refs[slot_pieces + 1 :]
        both, refs = refs[:parts], refs[parts:]
        send_ref, keep_ref, rows_ref, total_ref, hidden_ref, pre_ref = refs
        rows = stacked(row_parts).astype(BF16)
        rows_ref[...] = rows
        routed = router_softmax(rows, router_ref[...], expert_count)
        mine = (iota(routed.shape, 1) == idx[Z_AT]).astype(F32)
        gate = jnp.sum(routed * mine, axis=1, keepdims=True)
        total = (stacked(g_parts) * gate).astype(BF16)
        total_ref[...] = total
        forward = jnp.zeros((expert_in, width), F32)
        backward = jnp.zeros((expert_in, width), F32)
        for part in range(parts):
            at = part * hidden_local
            pre = matmul(rows, both[part][0])
            square = pre * pre
            inner = 0.7978845608028654 * pre * (1.0 + 0.044715 * square)
            tanh = jnp.tanh(inner)
            hidden = (0.5 * pre * (1.0 + tanh)).astype(BF16)
            slope = 0.5 * (1.0 + tanh) + 0.5 * pre * (1.0 - tanh * tanh) * (
                0.7978845608028654 * (1.0 + 3.0 * 0.044715 * square)
            )
            hidden_ref[:, at : at + hidden_local] = hidden
            grad_pre = (matmul(total, both[part][1]) * slope).astype(BF16)
            pre_ref[:, at : at + hidden_local] = grad_pre
            forward += matmul_nt(hidden, both[part][1])
            backward += matmul_nt(grad_pre, both[part][0])
        keep_ref[:, :width] = forward[:slot_rows]
        keep_ref[:, width:] = backward[:slot_rows]
        send_ref[:, :width] = forward[slot_rows:].astype(BF16)
        send_ref[:, width:] = backward[slot_rows:].astype(BF16)

    send, keep, rows_in, total_in, hidden, grad_pre = run(
        experts,
        scalars,
        [router_small] + expert_rows + g_rows + expert_parts,
        [
            shape_of((slot_rows, 2 * width), BF16),
            shape_of((slot_rows, 2 * width), F32),
            shape_of((expert_in, width), BF16),
            shape_of((expert_in, width), BF16),
            shape_of((expert_in, parts * hidden_local), BF16),
            shape_of((expert_in, parts * hidden_local), BF16),
        ],
    )
    arrived = swap(send, "dp", 2)

    def expert_grads(idx, rows_ref, total_ref, hidden_ref, pre_ref, own_ref, y_ref, c_ref):
        for part in range(parts):
            at = part * hidden_local
            up_grad = matmul_tn(rows_ref[...], pre_ref[:, at : at + hidden_local])
            down_grad = matmul_tn(total_ref[...], hidden_ref[:, at : at + hidden_local])
            ref, first = ((own_ref, 0), (y_ref, 0), (c_ref, 0), (c_ref, 2))[part]
            ref[first] = up_grad.astype(ref.dtype)
            ref[first + 1] = down_grad.astype(ref.dtype)

    weight_shape = (width, hidden_local)
    grads_own, grads_y, grads_c = run(
        expert_grads,
        scalars,
        [rows_in, total_in, hidden, grad_pre],
        [
            shape_of((2,) + weight_shape, F32),
            shape_of((2,) + weight_shape, BF16),
            shape_of((4,) + weight_shape, BF16),
        ],
    )
    from_c = swap(grads_c, "dp", 1)

    def fold_y(idx, y_ref, c_ref, up_ref, down_ref):
        for number, ref in enumerate((up_ref, down_ref)):
            ref[...] = (y_ref[number].astype(F32) + c_ref[2 + number].astype(F32)).astype(BF16)

    up_passed, down_passed = run(
        fold_y, scalars, [grads_y, from_c], [shape_of(weight_shape, BF16)] * 2
    )
    up_from_y = swap(up_passed, "tensor", 1)

    def add_x(idx, keep_ref, arrived_ref, *parts_out):
        store_pieces(parts_out, keep_ref[...] + arrived_ref[...].astype(F32))

    both_shape = shape_of((slot_rows // slot_pieces, 2 * width), BF16)
    back = run(add_x, scalars, [keep, arrived], [both_shape] * slot_pieces)
    home = over_z(list(back))

    def fold_grad(number):
        def fold(idx, own_ref, c_ref, y_ref, out_ref):
            out_ref[...] = own_ref[number] + c_ref[number].astype(F32) + y_ref[...].astype(F32)

        return fold

    (grad_w_in,) = run(
        fold_grad(0),
        scalars,
        [grads_own, from_c, up_from_y],
        [shape_of(weight_shape, F32)],
        after=[back[0]],
    )

    expert_pad = -(-expert_count // 8) * 8

    def at_home(idx, *refs):
        pieces, refs = refs[:slot_pieces], refs[slot_pieces:]
        (
            residual_ref,
            scale_ref,
            nm_ref,
            g_ref,
            live_ref,
            pick_ref,
            gain_ref,
            router_ref,
            mid_ref,
            layer_ref,
            gain_out,
            router_out,
        ) = refs
        returned = stacked(pieces)
        total, back_rows = returned[:, :width], returned[:, width:]
        residual = residual_ref[...]
        scale = scale_ref[:, :1]
        live = live_ref[:, :1]
        pick = pick_ref[...]
        gain = gain_ref[1:2, :]
        g = g_ref[...].astype(F32)
        routed = router_softmax(nm_ref[...], router_ref[...], expert_count)
        gate = jnp.sum(routed * pick, axis=1, keepdims=True)
        layer_ref[...] = (residual + gate * total * live).astype(BF16)
        grad_gate = jnp.sum(g * total, axis=1, keepdims=True) * live
        grad_logits = grad_gate * gate * (pick - routed)
        upstream = back_rows + matmul_nt(grad_logits, router_ref[...].astype(F32), HIGHEST)
        scaled = upstream * gain
        grad_mid = (
            g
            + scale * scaled
            - residual * scale**3 * jnp.mean(scaled * residual, axis=-1, keepdims=True)
        )
        mid_ref[...] = grad_mid.astype(BF16)
        gain_out[...] = jnp.broadcast_to(
            jnp.sum(upstream * residual * scale, axis=0, keepdims=True), gain_out.shape
        )
        router_grad = matmul_tn(grad_logits, nm_ref[...].astype(F32), HIGHEST)
        router_out[...] = router_grad[:expert_pad]

    mid_own, layer_own, gain_moe, router_part = run(
        at_home,
        scalars,
        home
        + [residual, scale_moe, normed_moe, g_slot, live_slot, pick_slot, gains, router_small],
        [
            shape_of((slot_rows, width), BF16),
            shape_of((slot_rows, width), BF16),
            shape_of((8, width), F32),
            shape_of((expert_pad, width), F32),
        ],
        after=[grad_w_in],
    )
    mid_other = swap(mid_own, "tensor", 1)

    half_pieces = 2 * expert_count
    first_part = weight_columns * 2 // 3 // LANES * LANES

    def emit_rows(idx, full_ref, outs):
        if not staged:
            outs[0][...] = full_ref[...]
            return
        keep_ref, send_ref = outs
        for number in range(half_pieces):
            at = piece_offset(idx, number)
            keep_ref[number] = full_ref[pl.ds(at, shard_rows), :]
            at = piece_offset(idx, number + half_pieces)
            send_ref[number] = full_ref[pl.ds(at, shard_rows), :].astype(BF16)

    if staged:
        row_shapes = [
            shape_of((half_pieces, shard_rows, weight_columns), F32),
            shape_of((half_pieces, shard_rows, weight_columns), BF16),
        ]
    else:
        row_shapes = [shape_of((width, weight_columns), F32)]

    small_rows = -(-(expert_count + 2 + tensor_count) // 8) * 8

    def store_halves(ref, at, values):
        high = values.astype(BF16)
        ref[at : at + 2 * small_rows, :width] = jnp.concatenate(
            [high.astype(F32), values - high.astype(F32)], axis=0
        ).astype(BF16)

    def load_halves(ref, at):
        both = ref[at : at + 2 * small_rows, :width].astype(F32)
        return both[:small_rows] + both[small_rows:]

    def attend_back(
        idx,
        own_ref,
        other_ref,
        mid_ref,
        mid_other_ref,
        context_ref,
        weight_ref,
        qkv_ref,
        probs_ref,
        normed_ref,
        x_ref,
        back_ref,
        live_ref,
        moe_ref,
        router_ref,
        *refs,
    ):
        ga_ref, keep_ref, send_ref, small_ref = refs[:4]
        outs = refs[4:-3]
        grads, full, upstream = refs[-3:]
        live = live_ref[:, :1]
        grad_attention = matmul_tn(own_ref[...], mid_ref[...]) + matmul_tn(
            other_ref[...], mid_other_ref[...]
        )
        ga_ref[...] = grad_attention.astype(BF16)
        full[:, qkv_width:] = matmul_tn(ga_ref[...], context_ref[...])
        grad_context = matmul(ga_ref[...], weight_ref[:, qkv_width:]) * live
        grad_context = grad_context.astype(BF16)
        mirror = (
            iota((block_len, block_len), 0) + iota((block_len, block_len), 1) == block_len - 1
        ).astype(BF16)
        lines = []
        for head in range(local_heads):
            at = head * HEAD_DIM
            query = qkv_ref[:, at : at + HEAD_DIM]
            key = qkv_ref[:, head_width + at : head_width + at + HEAD_DIM]
            value = qkv_ref[:, 2 * head_width + at : 2 * head_width + at + HEAD_DIM]
            back = grad_context[:, at : at + HEAD_DIM]
            probs = probs_ref[head]
            grad_value = matmul_tn(probs.astype(BF16), back)
            grad_probs = matmul_nt(back, value)
            grad_scores = probs * (
                grad_probs - jnp.sum(probs * grad_probs, axis=-1, keepdims=True)
            )
            grad_scores = grad_scores.astype(BF16)
            grad_query = matmul(grad_scores, key) * SCORE_SCALE
            grad_key = matmul_tn(grad_scores, query) * SCORE_SCALE
            grads[:, at : at + HEAD_DIM] = grad_query.astype(BF16)
            grads[:, head_width + at : head_width + at + HEAD_DIM] = grad_key.astype(BF16)
            grads[:, 2 * head_width + at : 2 * head_width + at + HEAD_DIM] = grad_value.astype(
                BF16
            )
            lines_left = jnp.concatenate(
                [matmul(grad_scores, mirror), jnp.zeros((block_len, span - block_len), F32)], axis=1
            )
            rows = block_len
            while rows > 8:
                rows //= 2
                lines_left = lines_left[:rows] + pltpu.roll(lines_left[rows:], rows, 1)
            lines_left = pltpu.roll(lines_left, 0, 1, stride=1, stride_axis=0)
            lines.append(jnp.sum(lines_left, axis=0, keepdims=True))
        lines.append(jnp.zeros((8 - local_heads, span), F32))
        diagonal = jnp.concatenate(lines, axis=0)
        table = matmul_nt(diagonal, back_ref[...].astype(F32), HIGHEST)
        line = [table[head : head + 1, :] for head in range(local_heads)]
        line.append(jnp.zeros((1, width - local_heads * LANES), F32))
        line = jnp.concatenate(line[: local_heads + (width > local_heads * LANES)], axis=1)
        all_grads = grads[...]
        grad_normed = matmul_nt(all_grads, weight_ref[:, :qkv_width])
        upstream[...] = grad_normed
        x = x_ref[...].astype(F32)
        gain = jnp.sum(grad_normed * x * inverse_rms(x), axis=0, keepdims=True)
        row = iota((small_rows, width), 0)
        small = jnp.where(row == expert_count, gain, 0.0)
        small = jnp.where(row == expert_count + 1, moe_ref[:1, :], small)
        small_ref[...] = jnp.where(row == expert_count + 2 + idx[Y_AT], line, small)
        small_ref[:expert_count, :] = router_ref[:expert_count, :]
        own_at = pl.multiple_of(idx[Y_AT] * row_count, row_count)
        other_at = pl.multiple_of((1 - idx[Y_AT]) * row_count, row_count)
        keep_ref[...] = upstream[pl.ds(own_at, row_count), :]
        send_ref[:row_count, :] = upstream[pl.ds(other_at, row_count), :].astype(BF16)
        store_halves(send_ref, row_count, small_ref[...])
        full[:, :qkv_width] = matmul_tn(normed_ref[...], all_grads)
        emit_rows(idx, full, outs)

    grad_attention, up_keep, up_send, small, *partial_rows = run(
        attend_back,
        scalars,
        [
            own_select,
            other_select,
            mid_own,
            mid_other,
            context,
            weights,
            qkv,
            probs,
            normed,
            x_full,
            pick_back,
            live_rows,
            gain_moe,
            router_part,
        ],
        [
            shape_of((block_len, width), BF16),
            shape_of((row_count, width), F32),
            shape_of((row_count + 2 * small_rows, width), BF16),
            shape_of((small_rows, width), F32),
        ]
        + row_shapes,
        [
            pltpu.VMEM((block_len, qkv_width), BF16),
            pltpu.VMEM((width, weight_columns), F32),
            pltpu.VMEM((block_len, width), F32),
        ],
    )
    up_other = swap(up_send, "tensor", 1)
    down_passed, _ = lax.optimization_barrier((down_passed, up_other))
    down_from_y = swap(down_passed, "tensor", 1)

    def small_over_y(idx, small_ref, other_ref, out_ref):
        out_ref[...] = small_ref[...] + load_halves(other_ref, row_count)

    (small,) = run(
        small_over_y, scalars, [small, up_other], [shape_of((small_rows, width), F32)]
    )

    out_shapes = [shape_of((shard_rows, head_width), F32)] * 4
    if staged:
        held, outgoing = partial_rows
        from_core = swap(outgoing, "dp", 1)

        def after_core(idx, held_ref, from_ref, x_send, x_keep, *z_refs):
            z_sends, z_keep = z_refs[:-1], z_refs[-1]

            def total(number, columns):
                return held_ref[number, :, columns] + from_ref[number, :, columns].astype(F32)

            front, rest = slice(0, first_part), slice(first_part, weight_columns)
            for j in range(expert_count):
                x_keep[j] = total(j, front)
                x_send[j] = total(expert_count + j, front).astype(BF16)
                for x in range(2):
                    piece = total(x * expert_count + j, rest)
                    if j == 0:
                        z_keep[x] = piece
                    else:
                        z_sends[j - 1][x] = piece.astype(BF16)

        rest_part = weight_columns - first_part
        x_send, x_keep, *z_sends, z_keep = run(
            after_core,
            scalars,
            [held, from_core],
            [
                shape_of((expert_count, shard_rows, first_part), BF16),
                shape_of((expert_count, shard_rows, first_part), F32),
            ]
            + [shape_of((2, shard_rows, rest_part), BF16)] * (expert_count - 1)
            + [shape_of((2, shard_rows, rest_part), F32)],
        )
        from_x = swap(x_send, "dp", 2)
        from_z = [swap(piece, "dp", z_masks[j + 1]) for j, piece in enumerate(z_sends)]

        small = small + swap(small, "dp", 1)
        small_x = swap(small, "dp", 2)

        def after_first(idx, small_ref, small_x_ref, x_keep, from_x, z_keep, *refs):
            from_z, refs = refs[: expert_count - 1], refs[expert_count - 1 :]
            z_sends, (front_keep, x_send, rest_keep, small_keep) = refs[:-4], refs[-4:]
            small = small_ref[...] + small_x_ref[...]
            small_keep[...] = small
            front_keep[...] = x_keep[0] + from_x[0].astype(F32)
            for j in range(1, expert_count):
                z_sends[j - 1][...] = jnp.zeros(z_sends[j - 1].shape, BF16)
                z_sends[j - 1][:shard_rows, :] = (x_keep[j] + from_x[j].astype(F32)).astype(BF16)
                store_halves(z_sends[j - 1], shard_rows, small)
            rest = z_keep[...]
            for ref in from_z:
                rest = rest + ref[...].astype(F32)
            rest_keep[...] = rest[0]
            x_send[...] = rest[1].astype(BF16)

        *z_sends, front_keep, x_send, rest_keep, small = run(
            after_first,
            scalars,
            [small, small_x, x_keep, from_x, z_keep] + from_z,
            [shape_of((shard_rows + 2 * small_rows, first_part), BF16)] * (expert_count - 1)
            + [
                shape_of((shard_rows, first_part), F32),
                shape_of((shard_rows, rest_part), BF16),
                shape_of((shard_rows, rest_part), F32),
                shape_of((small_rows, width), F32),
            ],
        )
        from_z = [swap(piece, "dp", z_masks[j + 1]) for j, piece in enumerate(z_sends)]
        from_x = swap(x_send, "dp", 2)
        late = [front_keep]

        def last_sum(idx, small_ref, front_keep, rest_keep, from_x, *refs):
            from_z, refs = refs[: expert_count - 1], refs[expert_count - 1 :]
            outs, (attn_out, moe_out, router_out, table_out, full) = refs[:-5], refs[-5:]
            front = front_keep[...]
            small = small_ref[...]
            for ref in from_z:
                front = front + ref[:shard_rows, :].astype(F32)
                small = small + load_halves(ref, shard_rows)
            column = iota((LANES, width), 1) - idx[DATA_AT] * shard_rows
            select = (column == iota((LANES, width), 0)).astype(F32)
            shard = matmul_nt(small, select, HIGHEST)
            attn_out[...] = shard[expert_count : expert_count + 1, :shard_rows]
            moe_out[...] = shard[expert_count + 1 : expert_count + 2, :shard_rows]
            router_out[...] = shard[:expert_count, :shard_rows]
            mine = iota((small_rows, width), 0) == expert_count + 2 + idx[Y_AT]
            line = jnp.sum(jnp.where(mine, small, 0.0), axis=0, keepdims=True)
            lines = [line[:, head * LANES : (head + 1) * LANES] for head in range(local_heads)]
            table_out[...] = jnp.concatenate(lines, axis=0)[:, :bucket_count]
            full[:, :first_part] = front
            full[:, first_part:] = rest_keep[...] + from_x[...].astype(F32)
            for number, out in enumerate(outs):
                out[...] = full[:, number * head_width : (number + 1) * head_width]

        *grad_matrices, grad_attn_scale, grad_moe_scale, grad_router, table = run(
            last_sum,
            scalars,
            [small, front_keep, rest_keep, from_x] + from_z,
            out_shapes
            + [
                shape_of((1, shard_rows), F32),
                shape_of((1, shard_rows), F32),
                shape_of((expert_count, shard_rows), F32),
                shape_of((local_heads, bucket_count), F32),
            ],
            [pltpu.VMEM((shard_rows, weight_columns), F32)],
        )
        grad_attn_scale, grad_moe_scale = grad_attn_scale[0], grad_moe_scale[0]
        grad_router, table = grad_router.T, table.T
    else:
        late = []
        summed = lax.psum_scatter(partial_rows[0], "dp", scatter_dimension=0, tiled=True)
        grad_matrices = [
            summed[:, number * head_width : (number + 1) * head_width] for number in range(4)
        ]
        small = lax.psum(small, "dp")
        shard = lax.dynamic_slice_in_dim(small, data_index * shard_rows, shard_rows, 1)
        grad_router = shard[:expert_count].T
        grad_attn_scale, grad_moe_scale = shard[expert_count], shard[expert_count + 1]
        table = lax.dynamic_slice_in_dim(small, expert_count + 2 + y_index, 1, 0)
        table = table[0, : local_heads * LANES].reshape(local_heads, LANES)[:, :bucket_count].T

    (grad_w_out,) = run(
        fold_grad(1),
        scalars,
        [grads_own, from_c, down_from_y],
        [shape_of(weight_shape, F32)],
        after=late,
    )
    if late:
        layer_own, _ = lax.optimization_barrier((layer_own, late[0]))
    layer_other = swap(layer_own, "tensor", 1)

    def finish(
        idx, own_ref, other_ref, layer_ref, layer_other_ref, ga_ref, keep_ref, arrived_ref,
        tok_ref, gain_ref, layer_out, tokens_out, full
    ):
        own_at = pl.multiple_of(idx[Y_AT] * row_count, row_count)
        full[...] = matmul_tn(own_ref[...], layer_ref[...]) + matmul_tn(
            other_ref[...], layer_other_ref[...]
        )
        layer_out[...] = full[pl.ds(own_at, row_count), :].astype(BF16)
        x = tok_ref[...].astype(F32)
        scale = inverse_rms(x)
        scaled = (keep_ref[...] + arrived_ref[:row_count, :].astype(F32)) * gain_ref[:1, :]
        grad = scale * scaled - x * scale**3 * jnp.mean(scaled * x, axis=-1, keepdims=True)
        grad = grad + ga_ref[pl.ds(own_at, row_count), :].astype(F32)
        tokens_out[...] = grad.astype(BF16)

    layer_out, grad_tokens = run(
        finish,
        scalars,
        [
            own_select, other_select, layer_own, layer_other, grad_attention, up_keep, up_other,
            tokens, gains,
        ],
        [shape_of((row_count, width), BF16)] * 2,
        [pltpu.VMEM((block_len, width), F32)],
        after=late,
    )

    return (
        layer_out,
        grad_tokens,
        *grad_matrices,
        grad_attn_scale,
        grad_moe_scale,
        grad_router,
        table,
        grad_w_in,
        grad_w_out,
    )


def solution(mesh):
    in_specs = (
        P(("dp", "tensor"), None),
        P(("dp", "tensor"), None),
        P("dp", "tensor"),
        P("dp", "tensor"),
        P("dp", "tensor"),
        P("dp", "tensor"),
        P("dp"),
        P("dp"),
        P("dp", None),
        P(None, "tensor"),
        P(None, ("dp", "tensor")),
        P(None, ("dp", "tensor")),
        P("dp", None),
        P("dp", None),
        P(),
    )
    out_specs = (
        P(("dp", "tensor"), None),
        P(("dp", "tensor"), None),
        P("dp", "tensor"),
        P("dp", "tensor"),
        P("dp", "tensor"),
        P("dp", "tensor"),
        P("dp"),
        P("dp"),
        P("dp", None),
        P(None, "tensor"),
        P(None, ("dp", "tensor")),
        P(None, ("dp", "tensor")),
    )
    return jax.shard_map(body, mesh=mesh, in_specs=in_specs, out_specs=out_specs, check_vma=False)
```

```python
import jax
import jax.numpy as jnp
from jax import lax
from jax.experimental import pallas as pl
from jax.experimental.pallas import tpu as pltpu
from jax.sharding import PartitionSpec as P

HEAD_DIM = 64
SPLIT = 4
EPSILON = 1e-06
MASKED_SCORE = -1e30
LANES = 128
SCORE_SCALE = HEAD_DIM ** (-0.5)
HIGHEST = lax.Precision.HIGHEST
VMEM_BYTES = 20 * 1024 * 1024
VMEM_MOST = 60 * 1024 * 1024
F32 = jnp.float32
BF16 = jnp.bfloat16

Z_AT, X_AT, C_AT, Y_AT, DATA_AT = range(5)


class Place:
    def __init__(self, ref):
        self.ref = ref

    def __getitem__(self, which):
        place = self.ref[0]
        return {
            Z_AT: place // (2 * SPLIT),
            X_AT: (place // 4) % 2,
            C_AT: (place // 2) % 2,
            Y_AT: place % 2,
            DATA_AT: place // 2,
        }[which]


def matmul(left, right, precision=None):
    return jnp.dot(left, right, precision=precision, preferred_element_type=F32)


def matmul_nt(left, right, precision=None):
    return lax.dot_general(
        left, right, (((1,), (1,)), ((), ())), precision=precision, preferred_element_type=F32
    )


def matmul_tn(left, right, precision=None):
    return lax.dot_general(
        left, right, (((0,), (0,)), ((), ())), precision=precision, preferred_element_type=F32
    )


def iota(shape, dim):
    return lax.broadcasted_iota(jnp.int32, shape, dim)


def shape_of(shape, dtype):
    return jax.ShapeDtypeStruct(shape, dtype)


def run(kernel, scalars, operands, outs, scratch=(), flops=1, after=(), far=0, far_outs=0, vmem=VMEM_BYTES):
    waits = len(after)

    def wrapped(place_ref, *refs):
        kernel(Place(place_ref), *refs[waits:])

    return pl.pallas_call(
        wrapped,
        out_shape=list(outs),
        in_specs=[pl.BlockSpec(memory_space=pltpu.SMEM)]
        + [pl.BlockSpec(memory_space=pl.ANY)] * waits
        + [pl.BlockSpec(memory_space=pltpu.HBM)] * far
        + [pl.BlockSpec(memory_space=pltpu.VMEM)] * (len(operands) - far),
        out_specs=[pl.BlockSpec(memory_space=pltpu.HBM)] * far_outs
        + [pl.BlockSpec(memory_space=pltpu.VMEM)] * (len(outs) - far_outs),
        scratch_shapes=list(scratch),
        compiler_params=pltpu.CompilerParams(vmem_limit_bytes=vmem),
        cost_estimate=pl.CostEstimate(flops=flops, bytes_accessed=1, transcendentals=0),
    )(scalars, *after, *operands)


def inverse_rms(values):
    return lax.rsqrt(jnp.mean(values * values, axis=-1, keepdims=True) + EPSILON)


def router_softmax(rows, router, expert_count):
    logits = matmul(rows, router)
    logits = jnp.where(iota(logits.shape, 1) < expert_count, logits, MASKED_SCORE)
    weights = jnp.exp(logits - jnp.max(logits, axis=-1, keepdims=True))
    return weights / jnp.sum(weights, axis=-1, keepdims=True)


def swap(values, axis, mask):
    count = lax.axis_size(axis)
    return lax.ppermute(values, axis, [(i, i ^ mask) for i in range(count)])


def stacked(pieces):
    parts = [piece[...].astype(F32) for piece in pieces]
    return parts[0] if len(parts) == 1 else jnp.concatenate(parts, axis=0)


def store_pieces(refs, values):
    rows = values.shape[0] // len(refs)
    for number, ref in enumerate(refs):
        ref[...] = values[number * rows : (number + 1) * rows].astype(ref.dtype)


def body(
    tokens,
    cotangent,
    query_weight,
    key_weight,
    value_weight,
    output_weight,
    attention_scale,
    expert_scale,
    router,
    bucket_bias,
    expert_up_weight,
    expert_down_weight,
    routes,
    lengths,
    buckets,
):
    row_count, width = tokens.shape
    block_len = routes.shape[0]
    expert_count = router.shape[1]
    bucket_count, local_heads = bucket_bias.shape
    head_width = local_heads * HEAD_DIM
    capacity = max(2, block_len * 5 // (4 * expert_count))
    half = (capacity + 1) // 2
    slot_rows = expert_count * half
    data_count = lax.axis_size("dp")
    shard_rows = width // data_count
    hidden_local = expert_up_weight.shape[1]
    tensor_count = lax.axis_size("tensor")
    span = 2 * block_len
    distances = buckets.shape[0]
    cut = width // 3

    data_index = lax.axis_index("dp")
    y_index = lax.axis_index("tensor")
    scalars = (data_index * 2 + y_index).astype(jnp.int32).reshape(1)

    staged = shard_rows % 16 == 0
    slot_pieces = expert_count if half % 8 == 0 else 1
    z_masks = [j * SPLIT for j in range(expert_count)]

    def over_z(pieces):
        if len(pieces) == 1:
            stack = pieces[0].reshape((expert_count, half) + pieces[0].shape[1:])
            moved = [stack[0]] + [swap(stack[j], "dp", z_masks[j]) for j in range(1, expert_count)]
            return [jnp.concatenate(moved, axis=0)]
        return [pieces[0]] + [swap(pieces[j], "dp", z_masks[j]) for j in range(1, expert_count)]

    small_columns = -(-(expert_count + 2) // LANES) * LANES
    weight_columns = 4 * head_width
    def pack(idx, *refs):
        sources, refs = refs[:15], refs[15:]
        (out_ref, rows_ref, rest_ref, facts_ref), refs = refs[:4], refs[4:]
        router_ref, attn_ref, moe_ref, *small_refs, sems = refs
        targets = (
            [out_ref.at[:, pl.ds(number * head_width, head_width)] for number in range(4)]
            + [router_ref, attn_ref, moe_ref]
            + [rows_ref.at[pl.ds(number * row_count, row_count), :] for number in range(2)]
            + small_refs
            + [
                ref.at[pl.ds(at, rows), pl.ds(number * hidden_local, hidden_local)]
                for number in range(2)
                for ref, at, rows in (
                    (rows_ref, 2 * row_count, cut),
                    (rest_ref, 0, width - cut),
                )
            ]
        )
        sources = list(sources[:13]) + [
            source.at[pl.ds(at, rows), :]
            for source in sources[13:]
            for at, rows in ((0, cut), (cut, width - cut))
        ]
        copies = [
            pltpu.make_async_copy(source, target, sems.at[number])
            for number, (source, target) in enumerate(zip(sources, targets))
        ]
        for copy in copies:
            copy.start()
        for copy in copies[4:7]:
            copy.wait()
        diagonal = iota((shard_rows, shard_rows), 0) == iota((shard_rows, shard_rows), 1)
        lane = iota((shard_rows, small_columns), 1)

        def column(row_ref):
            row = row_ref[...].astype(F32)
            return jnp.sum(jnp.where(diagonal, row, 0.0), axis=1, keepdims=True)

        spread_router = matmul_tn(
            router_ref[...],
            (iota((expert_count, small_columns), 0) == iota((expert_count, small_columns), 1))
            .astype(F32)
            .astype(BF16),
        )
        small = jnp.where(lane == expert_count, column(attn_ref), spread_router)
        small = jnp.where(lane == expert_count + 1, column(moe_ref), small)
        out_ref[:, weight_columns:] = small.astype(BF16)
        for copy in copies[:4] + copies[7:]:
            copy.wait()
        length_ref, bucket_ref, table_ref, route_ref = small_refs
        facts_ref[...] = jnp.zeros(facts_ref.shape, F32)
        facts_ref[0:1, :2] = length_ref[...].astype(F32)
        facts_ref[1:2, :distances] = bucket_ref[...].astype(F32)
        facts_ref[2:3, :block_len] = route_ref[...].astype(F32)
        facts_ref[8 : 8 + local_heads, :bucket_count] = table_ref[...]

    packed, rows_own, rest_own, facts = run(
        pack,
        scalars,
        [
            query_weight,
            key_weight,
            value_weight,
            output_weight,
            router.T,
            attention_scale[None, :],
            expert_scale[None, :],
            tokens,
            cotangent,
            lengths,
            buckets[None, :],
            bucket_bias.T,
            routes.reshape(1, block_len),
            expert_up_weight,
            expert_down_weight,
        ],
        [
            shape_of((shard_rows, weight_columns + small_columns), BF16),
            shape_of((2 * row_count + cut, 2 * hidden_local), BF16),
            shape_of((width - cut, 2 * hidden_local), BF16),
            shape_of((16, span), F32),
        ],
        [
            pltpu.VMEM((expert_count, shard_rows), BF16),
            pltpu.VMEM((1, shard_rows), BF16),
            pltpu.VMEM((1, shard_rows), BF16),
            pltpu.VMEM(lengths.shape, jnp.int32),
            pltpu.VMEM((1, distances), jnp.int32),
            pltpu.VMEM((local_heads, bucket_count), F32),
            pltpu.VMEM((1, block_len), jnp.int32),
            pltpu.SemaphoreType.DMA((17,)),
        ],
        far=15,
        vmem=VMEM_MOST,
    )
    if staged:
        gathered = [packed] + [swap(packed, "dp", mask) for mask in z_masks[1:]]
    else:
        gathered = [lax.all_gather(packed, "dp", axis=0, tiled=True)]

    def piece_offset(idx, number):
        j_z = number % expert_count
        j_x = (number // expert_count) % 2
        j_c = number // (2 * expert_count)
        index = (idx[Z_AT] ^ j_z) * SPLIT + (idx[X_AT] ^ j_x) * 2 + (idx[C_AT] ^ j_c)
        return pl.multiple_of(index * shard_rows, 16)

    rows_other = swap(rows_own, "tensor", 1)

    def prepare(idx, facts_ref, mine, others, *refs):
        x_ref, bias_ref, own_ref, other_ref, xs_ref, gs_ref, live_ref = refs[:7]
        pick_ref, back_ref, live_rows_ref = refs[7:10]
        live_parts = refs[10:-2]
        cot_full, head_table = refs[-2:]
        own_at = pl.multiple_of(idx[Y_AT] * row_count, row_count)
        other_at = pl.multiple_of((1 - idx[Y_AT]) * row_count, row_count)
        for at, rows in ((own_at, mine), (other_at, others)):
            x_ref[pl.ds(at, row_count), :] = rows[:row_count, :]
            cot_full[pl.ds(at, row_count), :] = rows[row_count : 2 * row_count, :]

        first = facts_ref[0:1, 0:1].astype(jnp.int32)
        active = first + facts_ref[0:1, 1:2].astype(jnp.int32)
        live_rows_ref[...] = jnp.broadcast_to(
            (iota((block_len, 1), 0) < active).astype(F32), live_rows_ref.shape
        )

        def segment(position):
            return jnp.where(position < first, 0, jnp.where(position < active, 1, 2))

        allowed = segment(iota((block_len, block_len), 0)) == segment(
            iota((block_len, block_len), 1)
        )
        pick = facts_ref[1:2, :distances].astype(jnp.int32) == iota((LANES, distances), 0)
        pick = pick.astype(F32)
        head_table[...] = jnp.zeros(head_table.shape, F32)
        head_table[:local_heads, :distances] = matmul(
            facts_ref[8 : 8 + local_heads, :bucket_count], pick[:bucket_count], HIGHEST
        )
        mirror = (
            iota((distances, span), 0) + iota((distances, span), 1) == distances - 1
        ).astype(F32)
        back_ref[...] = matmul(pick.astype(BF16), mirror.astype(BF16)).astype(BF16)
        for head in range(local_heads):
            line = jnp.broadcast_to(head_table[head : head + 1, :], (block_len, span))
            turned = pltpu.roll(line, block_len + 1, 1, stride=1, stride_axis=0)
            bias_ref[head] = jnp.where(allowed, turned[:, :block_len], MASKED_SCORE)

        route = facts_ref[2:3, :block_len].astype(jnp.int32)
        chosen = (route == iota((LANES, block_len), 0)).astype(F32)
        earlier = (iota((block_len, block_len), 0) < iota((block_len, block_len), 1)).astype(F32)
        counts = matmul(chosen.astype(BF16), earlier.astype(BF16))
        slot = jnp.sum(chosen * counts, axis=0, keepdims=True).astype(jnp.int32)
        row_id = iota((slot_rows, block_len), 0)

        def selection(which):
            place = slot - half * which
            code = (route ^ idx[Z_AT]) * half + place
            code = jnp.where((place >= 0) & (place < half), code, -1)
            return (row_id == code).astype(F32)

        own_select = selection(idx[Y_AT])
        own_bf = own_select.astype(BF16)
        own_ref[...] = own_bf
        other_ref[...] = selection(1 - idx[Y_AT]).astype(BF16)
        xs_ref[...] = matmul(own_bf, x_ref[...]).astype(BF16)
        gs_ref[...] = matmul(own_bf, cot_full[...]).astype(BF16)
        live_select = own_select * (iota((1, block_len), 1) < active).astype(F32)
        live_ref[...] = jnp.broadcast_to(
            jnp.sum(live_select, axis=1, keepdims=True), live_ref.shape
        )
        pick_ref[...] = matmul_nt(own_bf, chosen.astype(BF16))
        store_pieces(live_parts, matmul(live_select.astype(BF16), cot_full[...]))

    piece_shape = shape_of((slot_rows // slot_pieces, width), BF16)
    prepared = run(
        prepare,
        scalars,
        [facts, rows_own, rows_other],
        [
            shape_of((block_len, width), BF16),
            shape_of((local_heads, block_len, block_len), F32),
            shape_of((slot_rows, block_len), BF16),
            shape_of((slot_rows, block_len), BF16),
            shape_of((slot_rows, width), BF16),
            shape_of((slot_rows, width), BF16),
            shape_of((slot_rows, LANES), F32),
            shape_of((slot_rows, LANES), F32),
            shape_of((LANES, span), BF16),
            shape_of((block_len, LANES), F32),
        ]
        + [piece_shape] * slot_pieces,
        [pltpu.VMEM((block_len, width), BF16), pltpu.VMEM((8, span), F32)],
    )
    x_full, bias, own_select, other_select, x_slot, g_slot = prepared[:6]
    live_slot, pick_slot, pick_back, live_rows = prepared[6:10]
    g_home = prepared[10:]
    g_wait = []
    if staged:
        g_home = lax.optimization_barrier((*g_home, *gathered[1:expert_count]))[:slot_pieces]
        gathered = gathered + [swap(piece, "dp", 2) for piece in gathered]
        *gathered, _ = lax.optimization_barrier((*gathered, x_full))
        gathered = gathered + [swap(piece, "dp", 1) for piece in gathered]
    g_rows = over_z(list(g_home))
    if staged:
        g_wait = g_rows[1:]
    g_rows = g_rows + [swap(jnp.concatenate(g_rows, axis=0), "dp", 2)]
    rest_send, _ = lax.optimization_barrier((rest_own, rows_other))
    rest_y = swap(rest_send, "tensor", 1)
    expert_parts = [rows_own, rest_own, rows_other, rest_y]
    expert_parts += [swap(rows_own, "dp", 1), swap(rest_own, "dp", 1), swap(rows_other, "dp", 1)]

    def to_experts(pieces):
        arrived = over_z(list(pieces))
        return arrived + [swap(piece, "dp", 2) for piece in arrived]


    qkv_width = 3 * head_width
    piece_count = len(gathered)

    def attend(idx, live_ref, x_ref, bias_ref, own_ref, other_ref, xs_ref, *refs):
        pieces = refs[:piece_count]
        (
            send_ref,
            keep_ref,
            normed_ref,
            qkv_ref,
            probs_ref,
            context_ref,
            weight_ref,
            small_ref,
            gain_ref,
        ) = refs[piece_count:]
        if piece_count == 1:
            weight_ref[...] = pieces[0][:, :weight_columns]
            small_ref[...] = pieces[0][:, weight_columns:]
        else:
            for number, piece in enumerate(pieces):
                at = piece_offset(idx, number)
                weight_ref[pl.ds(at, shard_rows), :] = piece[:, :weight_columns]
                small_ref[pl.ds(at, shard_rows), :] = piece[:, weight_columns:]
        turned = small_ref[...].astype(F32).T
        gain = turned[expert_count : expert_count + 1, :]
        gain_ref[...] = jnp.broadcast_to(gain, gain_ref.shape)
        gain_ref[1:2, :] = turned[expert_count + 1 : expert_count + 2, :]
        x = x_ref[...].astype(F32)
        normed = (x * inverse_rms(x) * gain).astype(BF16)
        normed_ref[...] = normed
        qkv_ref[...] = matmul(normed, weight_ref[:, :qkv_width]).astype(BF16)
        live = live_ref[:, :1]
        for head in range(local_heads):
            at = head * HEAD_DIM
            query = qkv_ref[:, at : at + HEAD_DIM]
            key = qkv_ref[:, head_width + at : head_width + at + HEAD_DIM]
            value = qkv_ref[:, 2 * head_width + at : 2 * head_width + at + HEAD_DIM]
            scores = matmul_nt(query, key) * SCORE_SCALE + bias_ref[head]
            weights = jnp.exp(scores - jnp.max(scores, axis=-1, keepdims=True))
            probs = weights / jnp.sum(weights, axis=-1, keepdims=True)
            probs_ref[head] = probs
            context = matmul(probs.astype(BF16), value) * live
            context_ref[:, at : at + HEAD_DIM] = context.astype(BF16)
        out = matmul_nt(context_ref[...], weight_ref[:, qkv_width:]).astype(BF16)
        send_ref[...] = matmul(other_ref[...], out).astype(BF16)
        keep_ref[...] = matmul(own_ref[...], out) + xs_ref[...].astype(F32)

    send, keep, normed, qkv, probs, context, weights, router_small, gains = run(
        attend,
        scalars,
        [live_rows, x_full, bias, own_select, other_select, x_slot] + gathered,
        [
            shape_of((slot_rows, width), BF16),
            shape_of((slot_rows, width), F32),
            shape_of((block_len, width), BF16),
            shape_of((block_len, qkv_width), BF16),
            shape_of((local_heads, block_len, block_len), F32),
            shape_of((block_len, head_width), BF16),
            shape_of((width, weight_columns), BF16),
            shape_of((width, small_columns), BF16),
            shape_of((8, width), F32),
        ],
        after=g_wait,
    )
    arrived = swap(send, "tensor", 1)
    rest_y, _ = lax.optimization_barrier((rest_y, arrived))
    expert_parts.append(swap(rest_y, "dp", 1))

    def second_norm(idx, keep_ref, arrived_ref, gain_ref, residual_ref, scale_ref, nm_ref, *parts):
        residual = keep_ref[...] + arrived_ref[...].astype(F32)
        scale = inverse_rms(residual)
        residual_ref[...] = residual
        scale_ref[...] = jnp.broadcast_to(scale, scale_ref.shape)
        rows = residual * scale * gain_ref[1:2, :]
        nm_ref[...] = rows.astype(BF16)
        store_pieces(parts, rows)

    residual, scale_moe, normed_moe, *row_home = run(
        second_norm,
        scalars,
        [keep, arrived, gains],
        [
            shape_of((slot_rows, width), F32),
            shape_of((slot_rows, LANES), F32),
            shape_of((slot_rows, width), BF16),
        ]
        + [piece_shape] * slot_pieces,
        after=expert_parts[4:7],
    )
    expert_rows = to_experts(row_home)

    expert_in = 2 * slot_rows
    parts = 4

    def experts(idx, router_ref, *refs):
        count = 2 * slot_pieces
        row_parts, refs = refs[:count], refs[count:]
        g_parts, refs = refs[: slot_pieces + 1], refs[slot_pieces + 1 :]
        weights, refs = refs[: 2 * parts], refs[2 * parts :]
        send_ref, keep_ref, rows_ref, total_ref, hidden_ref, pre_ref = refs
        rows = stacked(row_parts).astype(BF16)
        rows_ref[...] = rows
        routed = router_softmax(rows, router_ref[...], expert_count)
        mine = (iota(routed.shape, 1) == idx[Z_AT]).astype(F32)
        gate = jnp.sum(routed * mine, axis=1, keepdims=True)
        total = (stacked(g_parts) * gate).astype(BF16)
        total_ref[...] = total
        forward = jnp.zeros((expert_in, width), F32)
        backward = jnp.zeros((expert_in, width), F32)
        for part in range(parts):
            at = part * hidden_local
            head, rest = weights[2 * part : 2 * part + 2]
            up, down = [
                jnp.concatenate(
                    [
                        head[2 * row_count :, number * hidden_local : (number + 1) * hidden_local],
                        rest[:, number * hidden_local : (number + 1) * hidden_local],
                    ],
                    axis=0,
                )
                for number in range(2)
            ]
            pre = matmul(rows, up)
            square = pre * pre
            inner = 0.7978845608028654 * pre * (1.0 + 0.044715 * square)
            tanh = jnp.tanh(inner)
            hidden = (0.5 * pre * (1.0 + tanh)).astype(BF16)
            slope = 0.5 * (1.0 + tanh) + 0.5 * pre * (1.0 - tanh * tanh) * (
                0.7978845608028654 * (1.0 + 3.0 * 0.044715 * square)
            )
            hidden_ref[:, at : at + hidden_local] = hidden
            grad_pre = (matmul(total, down) * slope).astype(BF16)
            pre_ref[:, at : at + hidden_local] = grad_pre
            forward += matmul_nt(hidden, down)
            backward += matmul_nt(grad_pre, up)
        keep_ref[:, :width] = forward[:slot_rows]
        keep_ref[:, width:] = backward[:slot_rows]
        send_ref[:, :width] = forward[slot_rows:].astype(BF16)
        send_ref[:, width:] = backward[slot_rows:].astype(BF16)

    send, keep, rows_in, total_in, hidden, grad_pre = run(
        experts,
        scalars,
        [router_small] + expert_rows + g_rows + expert_parts,
        [
            shape_of((slot_rows, 2 * width), BF16),
            shape_of((slot_rows, 2 * width), F32),
            shape_of((expert_in, width), BF16),
            shape_of((expert_in, width), BF16),
            shape_of((expert_in, parts * hidden_local), BF16),
            shape_of((expert_in, parts * hidden_local), BF16),
        ],
    )
    arrived = swap(send, "dp", 2)

    def expert_grads(first):
        def grads(idx, rows_ref, total_ref, hidden_ref, pre_ref, *outs):
            for part in range(2):
                at = (first + part) * hidden_local
                up_grad = matmul_tn(rows_ref[...], pre_ref[:, at : at + hidden_local])
                down_grad = matmul_tn(total_ref[...], hidden_ref[:, at : at + hidden_local])
                ref, place = (outs[0], 2 * part) if len(outs) == 1 else (outs[part], 0)
                ref[place] = up_grad.astype(ref.dtype)
                ref[place + 1] = down_grad.astype(ref.dtype)

        return grads

    weight_shape = (width, hidden_local)
    grad_inputs = [rows_in, total_in, hidden, grad_pre]
    (grads_c,) = run(
        expert_grads(2), scalars, grad_inputs, [shape_of((4,) + weight_shape, BF16)]
    )
    grads_own, grads_y = run(
        expert_grads(0),
        scalars,
        grad_inputs,
        [shape_of((2,) + weight_shape, F32), shape_of((2,) + weight_shape, BF16)],
    )
    from_c = swap(grads_c, "dp", 1)

    def fold_y(idx, y_ref, c_ref, up_ref, down_ref):
        for number, ref in enumerate((up_ref, down_ref)):
            total = y_ref[number].astype(F32) + c_ref[2 + number].astype(F32)
            if number == 0:
                ref[...] = total.astype(BF16)
            else:
                ref[:, :hidden_local] = total[: width // 2].astype(BF16)
                ref[:, hidden_local:] = total[width // 2 :].astype(BF16)

    up_passed, down_passed = run(
        fold_y,
        scalars,
        [grads_y, from_c],
        [shape_of(weight_shape, BF16), shape_of((width // 2, 2 * hidden_local), BF16)],
    )
    up_from_y = swap(up_passed, "tensor", 1)

    def add_x(idx, keep_ref, arrived_ref, *parts_out):
        store_pieces(parts_out, keep_ref[...] + arrived_ref[...].astype(F32))

    both_shape = shape_of((slot_rows // slot_pieces, 2 * width), BF16)
    back = run(add_x, scalars, [keep, arrived], [both_shape] * slot_pieces)
    home = over_z(list(back))

    def fold_grad(number):
        def fold(idx, own_ref, c_ref, y_ref, out_ref, done_ref):
            done_ref[...] = jnp.zeros(done_ref.shape, F32)
            if number == 0:
                out_ref[...] = own_ref[0] + c_ref[0].astype(F32) + y_ref[...].astype(F32)
                return
            for part in range(2):
                rows = slice(part * (width // 2), (part + 1) * (width // 2))
                columns = slice(part * hidden_local, (part + 1) * hidden_local)
                out_ref[rows, :] = (
                    own_ref[1, rows, :]
                    + c_ref[1, rows, :].astype(F32)
                    + y_ref[slot_rows + row_count :, columns].astype(F32)
                )

        return fold

    grad_w_in, up_done = run(
        fold_grad(0),
        scalars,
        [grads_own, from_c, up_from_y],
        [shape_of(weight_shape, F32), shape_of((8, LANES), F32)],
        after=[back[0]],
    )

    expert_pad = -(-expert_count // 8) * 8

    def at_home(idx, *refs):
        pieces, refs = refs[:slot_pieces], refs[slot_pieces:]
        (
            residual_ref,
            scale_ref,
            nm_ref,
            g_ref,
            live_ref,
            pick_ref,
            gain_ref,
            router_ref,
            mid_ref,
            layer_ref,
            gain_out,
            router_out,
        ) = refs
        returned = stacked(pieces)
        total, back_rows = returned[:, :width], returned[:, width:]
        residual = residual_ref[...]
        scale = scale_ref[:, :1]
        live = live_ref[:, :1]
        pick = pick_ref[...]
        gain = gain_ref[1:2, :]
        g = g_ref[...].astype(F32)
        routed = router_softmax(nm_ref[...], router_ref[...], expert_count)
        gate = jnp.sum(routed * pick, axis=1, keepdims=True)
        layer_ref[...] = (residual + gate * total * live).astype(BF16)
        grad_gate = jnp.sum(g * total, axis=1, keepdims=True) * live
        grad_logits = grad_gate * gate * (pick - routed)
        upstream = back_rows + matmul_nt(grad_logits, router_ref[...].astype(F32), HIGHEST)
        scaled = upstream * gain
        grad_mid = (
            g
            + scale * scaled
            - residual * scale**3 * jnp.mean(scaled * residual, axis=-1, keepdims=True)
        )
        mid_ref[...] = grad_mid.astype(BF16)
        gain_out[...] = jnp.broadcast_to(
            jnp.sum(upstream * residual * scale, axis=0, keepdims=True), gain_out.shape
        )
        router_grad = matmul_tn(grad_logits, nm_ref[...].astype(F32), HIGHEST)
        router_out[...] = router_grad[:expert_pad]

    mid_own, layer_own, gain_moe, router_part = run(
        at_home,
        scalars,
        home
        + [residual, scale_moe, normed_moe, g_slot, live_slot, pick_slot, gains, router_small],
        [
            shape_of((slot_rows, width), BF16),
            shape_of((slot_rows, width), BF16),
            shape_of((8, width), F32),
            shape_of((expert_pad, width), F32),
        ],
        after=[up_done],
    )
    mid_other = swap(mid_own, "tensor", 1)

    half_pieces = 2 * expert_count
    first_part = weight_columns * 3 // 4 // LANES * LANES

    def emit_rows(idx, full_ref, outs):
        if not staged:
            outs[0][...] = full_ref[...]
            return
        keep_ref, send_ref = outs
        for number in range(half_pieces):
            at = piece_offset(idx, number)
            keep_ref[number] = full_ref[pl.ds(at, shard_rows), :]
            at = piece_offset(idx, number + half_pieces)
            send_ref[number] = full_ref[pl.ds(at, shard_rows), :].astype(BF16)

    if staged:
        row_shapes = [
            shape_of((half_pieces, shard_rows, weight_columns), F32),
            shape_of((half_pieces, shard_rows, weight_columns), BF16),
        ]
    else:
        row_shapes = [shape_of((width, weight_columns), F32)]

    small_rows = -(-(expert_count + 2 + tensor_count) // 8) * 8

    def store_halves(ref, at, values):
        high = values.astype(BF16)
        ref[at : at + 2 * small_rows, :width] = jnp.concatenate(
            [high.astype(F32), values - high.astype(F32)], axis=0
        ).astype(BF16)

    def load_halves(ref, at):
        both = ref[at : at + 2 * small_rows, :width].astype(F32)
        return both[:small_rows] + both[small_rows:]

    def attend_back(
        idx,
        own_ref,
        other_ref,
        mid_ref,
        mid_other_ref,
        context_ref,
        weight_ref,
        qkv_ref,
        probs_ref,
        normed_ref,
        x_ref,
        back_ref,
        live_ref,
        moe_ref,
        router_ref,
        layer_ref,
        down_ref,
        *refs,
    ):
        ga_ref, keep_ref, send_ref, small_ref = refs[:4]
        outs = refs[4:-3]
        grads, full, upstream = refs[-3:]
        live = live_ref[:, :1]
        grad_attention = matmul_tn(own_ref[...], mid_ref[...]) + matmul_tn(
            other_ref[...], mid_other_ref[...]
        )
        ga_ref[...] = grad_attention.astype(BF16)
        full[:, qkv_width:] = matmul_tn(ga_ref[...], context_ref[...])
        grad_context = matmul(ga_ref[...], weight_ref[:, qkv_width:]) * live
        grad_context = grad_context.astype(BF16)
        mirror = (
            iota((block_len, block_len), 0) + iota((block_len, block_len), 1) == block_len - 1
        ).astype(BF16)
        lines = []
        for head in range(local_heads):
            at = head * HEAD_DIM
            query = qkv_ref[:, at : at + HEAD_DIM]
            key = qkv_ref[:, head_width + at : head_width + at + HEAD_DIM]
            value = qkv_ref[:, 2 * head_width + at : 2 * head_width + at + HEAD_DIM]
            back = grad_context[:, at : at + HEAD_DIM]
            probs = probs_ref[head]
            grad_value = matmul_tn(probs.astype(BF16), back)
            grad_probs = matmul_nt(back, value)
            grad_scores = probs * (
                grad_probs - jnp.sum(probs * grad_probs, axis=-1, keepdims=True)
            )
            grad_scores = grad_scores.astype(BF16)
            grad_query = matmul(grad_scores, key) * SCORE_SCALE
            grad_key = matmul_tn(grad_scores, query) * SCORE_SCALE
            grads[:, at : at + HEAD_DIM] = grad_query.astype(BF16)
            grads[:, head_width + at : head_width + at + HEAD_DIM] = grad_key.astype(BF16)
            grads[:, 2 * head_width + at : 2 * head_width + at + HEAD_DIM] = grad_value.astype(
                BF16
            )
            lines_left = jnp.concatenate(
                [matmul(grad_scores, mirror), jnp.zeros((block_len, span - block_len), F32)], axis=1
            )
            rows = block_len
            while rows > 8:
                rows //= 2
                lines_left = lines_left[:rows] + pltpu.roll(lines_left[rows:], rows, 1)
            lines_left = pltpu.roll(lines_left, 0, 1, stride=1, stride_axis=0)
            lines.append(jnp.sum(lines_left, axis=0, keepdims=True))
        lines.append(jnp.zeros((8 - local_heads, span), F32))
        diagonal = jnp.concatenate(lines, axis=0)
        table = matmul_nt(diagonal, back_ref[...].astype(F32), HIGHEST)
        line = [table[head : head + 1, :] for head in range(local_heads)]
        line.append(jnp.zeros((1, width - local_heads * LANES), F32))
        line = jnp.concatenate(line[: local_heads + (width > local_heads * LANES)], axis=1)
        all_grads = grads[...]
        grad_normed = matmul_nt(all_grads, weight_ref[:, :qkv_width])
        upstream[...] = grad_normed
        x = x_ref[...].astype(F32)
        gain = jnp.sum(grad_normed * x * inverse_rms(x), axis=0, keepdims=True)
        row = iota((small_rows, width), 0)
        small = jnp.where(row == expert_count, gain, 0.0)
        small = jnp.where(row == expert_count + 1, moe_ref[:1, :], small)
        small_ref[...] = jnp.where(row == expert_count + 2 + idx[Y_AT], line, small)
        small_ref[:expert_count, :] = router_ref[:expert_count, :]
        own_at = pl.multiple_of(idx[Y_AT] * row_count, row_count)
        other_at = pl.multiple_of((1 - idx[Y_AT]) * row_count, row_count)
        keep_ref[...] = upstream[pl.ds(own_at, row_count), :]
        send_ref[slot_rows : slot_rows + row_count, :] = upstream[
            pl.ds(other_at, row_count), :
        ].astype(BF16)
        send_ref[:slot_rows, :] = layer_ref[...]
        send_ref[slot_rows + row_count :, :] = down_ref[...]
        full[:, :qkv_width] = matmul_tn(normed_ref[...], all_grads)
        emit_rows(idx, full, outs)

    grad_attention, up_keep, up_send, small, *partial_rows = run(
        attend_back,
        scalars,
        [
            own_select,
            other_select,
            mid_own,
            mid_other,
            context,
            weights,
            qkv,
            probs,
            normed,
            x_full,
            pick_back,
            live_rows,
            gain_moe,
            router_part,
            layer_own,
            down_passed,
        ],
        [
            shape_of((block_len, width), BF16),
            shape_of((row_count, width), F32),
            shape_of((slot_rows + row_count + width // 2, width), BF16),
            shape_of((small_rows, width), F32),
        ]
        + row_shapes,
        [
            pltpu.VMEM((block_len, qkv_width), BF16),
            pltpu.VMEM((width, weight_columns), F32),
            pltpu.VMEM((block_len, width), F32),
        ],
    )
    def small_over_y(idx, small_ref, other_ref, out_ref):
        out_ref[...] = small_ref[...] + other_ref[...]

    (small,) = run(
        small_over_y,
        scalars,
        [small, swap(small, "tensor", 1)],
        [shape_of((small_rows, width), F32)],
    )
    up_send, _ = lax.optimization_barrier((up_send, small))
    up_other = swap(up_send, "tensor", 1)

    out_shapes = [shape_of((shard_rows, head_width), F32)] * 4
    if staged:
        held, outgoing = partial_rows
        from_core = swap(outgoing, "dp", 1)

        small_core = swap(small, "dp", 1)
        x_rows = expert_count * shard_rows

        def after_core(idx, small_ref, small_core, held_ref, from_ref, x_send, x_keep, *z_refs):
            z_sends, z_keep, small_keep = z_refs[:-2], z_refs[-2], z_refs[-1]
            small = small_ref[...] + small_core[...]
            small_keep[...] = small
            x_send[x_rows:, :] = jnp.zeros((2 * small_rows, first_part), BF16)
            store_halves(x_send, x_rows, small)

            def total(number, columns):
                return held_ref[number, :, columns] + from_ref[number, :, columns].astype(F32)

            front, rest = slice(0, first_part), slice(first_part, weight_columns)
            for j in range(expert_count):
                x_keep[j] = total(j, front)
                x_send[j * shard_rows : (j + 1) * shard_rows, :] = total(
                    expert_count + j, front
                ).astype(BF16)
                for x in range(2):
                    piece = total(x * expert_count + j, rest)
                    if j == 0:
                        z_keep[x] = piece
                    else:
                        z_sends[j - 1][x] = piece.astype(BF16)

        rest_part = weight_columns - first_part
        x_send, x_keep, *z_sends, z_keep, small = run(
            after_core,
            scalars,
            [small, small_core, held, from_core],
            [
                shape_of((x_rows + 2 * small_rows, first_part), BF16),
                shape_of((expert_count, shard_rows, first_part), F32),
            ]
            + [shape_of((2, shard_rows, rest_part), BF16)] * (expert_count - 1)
            + [shape_of((2, shard_rows, rest_part), F32), shape_of((small_rows, width), F32)],
        )
        from_x = swap(x_send, "dp", 2)
        from_z = [swap(piece, "dp", z_masks[j + 1]) for j, piece in enumerate(z_sends)]


        def after_first(idx, small_ref, x_keep, from_x, z_keep, *refs):
            from_z, refs = refs[: expert_count - 1], refs[expert_count - 1 :]
            z_sends, (front_keep, x_send, rest_keep, small_keep) = refs[:-4], refs[-4:]
            small = small_ref[...] + load_halves(from_x, x_rows)
            small_keep[...] = small
            front_keep[...] = x_keep[0] + from_x[:shard_rows, :].astype(F32)
            for j in range(1, expert_count):
                z_sends[j - 1][...] = jnp.zeros(z_sends[j - 1].shape, BF16)
                z_sends[j - 1][:shard_rows, :] = (
                    x_keep[j] + from_x[j * shard_rows : (j + 1) * shard_rows, :].astype(F32)
                ).astype(BF16)
                store_halves(z_sends[j - 1], shard_rows, small)
            rest = z_keep[...]
            for ref in from_z:
                rest = rest + ref[...].astype(F32)
            rest_keep[...] = rest[0]
            x_send[...] = rest[1].astype(BF16)

        *z_sends, front_keep, x_send, rest_keep, small = run(
            after_first,
            scalars,
            [small, x_keep, from_x, z_keep] + from_z,
            [shape_of((shard_rows + 2 * small_rows, first_part), BF16)] * (expert_count - 1)
            + [
                shape_of((shard_rows, first_part), F32),
                shape_of((shard_rows, rest_part), BF16),
                shape_of((shard_rows, rest_part), F32),
                shape_of((small_rows, width), F32),
            ],
        )
        from_z = [swap(piece, "dp", z_masks[j + 1]) for j, piece in enumerate(z_sends)]
        from_x = swap(x_send, "dp", 2)
        late = [front_keep]

        def last_sum(idx, small_ref, front_keep, rest_keep, from_x, *refs):
            from_z, refs = refs[: expert_count - 1], refs[expert_count - 1 :]
            outs, (attn_out, moe_out, router_out, table_out, full) = refs[:-5], refs[-5:]
            front = front_keep[...]
            small = small_ref[...]
            for ref in from_z:
                front = front + ref[:shard_rows, :].astype(F32)
                small = small + load_halves(ref, shard_rows)
            column = iota((LANES, width), 1) - idx[DATA_AT] * shard_rows
            select = (column == iota((LANES, width), 0)).astype(F32)
            shard = matmul_nt(small, select, HIGHEST)
            attn_out[...] = shard[expert_count : expert_count + 1, :shard_rows]
            moe_out[...] = shard[expert_count + 1 : expert_count + 2, :shard_rows]
            router_out[...] = shard[:expert_count, :shard_rows]
            mine = iota((small_rows, width), 0) == expert_count + 2 + idx[Y_AT]
            line = jnp.sum(jnp.where(mine, small, 0.0), axis=0, keepdims=True)
            lines = [line[:, head * LANES : (head + 1) * LANES] for head in range(local_heads)]
            table_out[...] = jnp.concatenate(lines, axis=0)[:, :bucket_count]
            full[:, :first_part] = front
            full[:, first_part:] = rest_keep[...] + from_x[...].astype(F32)
            for number, out in enumerate(outs):
                out[...] = full[:, number * head_width : (number + 1) * head_width]

        *grad_matrices, grad_attn_scale, grad_moe_scale, grad_router, table = run(
            last_sum,
            scalars,
            [small, front_keep, rest_keep, from_x] + from_z,
            out_shapes
            + [
                shape_of((1, shard_rows), F32),
                shape_of((1, shard_rows), F32),
                shape_of((expert_count, shard_rows), F32),
                shape_of((local_heads, bucket_count), F32),
            ],
            [pltpu.VMEM((shard_rows, weight_columns), F32)],
        )
        grad_attn_scale, grad_moe_scale = grad_attn_scale[0], grad_moe_scale[0]
        grad_router, table = grad_router.T, table.T
    else:
        late = []
        summed = lax.psum_scatter(partial_rows[0], "dp", scatter_dimension=0, tiled=True)
        grad_matrices = [
            summed[:, number * head_width : (number + 1) * head_width] for number in range(4)
        ]
        small = lax.psum(small, "dp")
        shard = lax.dynamic_slice_in_dim(small, data_index * shard_rows, shard_rows, 1)
        grad_router = shard[:expert_count].T
        grad_attn_scale, grad_moe_scale = shard[expert_count], shard[expert_count + 1]
        table = lax.dynamic_slice_in_dim(small, expert_count + 2 + y_index, 1, 0)
        table = table[0, : local_heads * LANES].reshape(local_heads, LANES)[:, :bucket_count].T

    grad_w_out, _ = run(
        fold_grad(1),
        scalars,
        [grads_own, from_c, up_other],
        [shape_of(weight_shape, F32), shape_of((8, LANES), F32)],
        after=late,
    )
    def finish(
        idx, own_ref, other_ref, layer_ref, arrived_ref, ga_ref, keep_ref, tok_ref, gain_ref,
        layer_out, tokens_out, full
    ):
        own_at = pl.multiple_of(idx[Y_AT] * row_count, row_count)
        full[...] = matmul_tn(own_ref[...], layer_ref[...]) + matmul_tn(
            other_ref[...], arrived_ref[:slot_rows, :]
        )
        layer_out[...] = full[pl.ds(own_at, row_count), :].astype(BF16)
        x = tok_ref[...].astype(F32)
        scale = inverse_rms(x)
        scaled = keep_ref[...] + arrived_ref[slot_rows : slot_rows + row_count, :].astype(F32)
        scaled = scaled * gain_ref[:1, :]
        grad = scale * scaled - x * scale**3 * jnp.mean(scaled * x, axis=-1, keepdims=True)
        grad = grad + ga_ref[pl.ds(own_at, row_count), :].astype(F32)
        tokens_out[...] = grad.astype(BF16)

    layer_out, grad_tokens = run(
        finish,
        scalars,
        [
            own_select, other_select, layer_own, up_other, grad_attention, up_keep, tokens, gains,
        ],
        [shape_of((row_count, width), BF16)] * 2,
        [pltpu.VMEM((block_len, width), F32)],
        after=late,
    )

    return (
        layer_out,
        grad_tokens,
        *grad_matrices,
        grad_attn_scale,
        grad_moe_scale,
        grad_router,
        table,
        grad_w_in,
        grad_w_out,
    )


def solution(mesh):
    in_specs = (
        P(("dp", "tensor"), None),
        P(("dp", "tensor"), None),
        P("dp", "tensor"),
        P("dp", "tensor"),
        P("dp", "tensor"),
        P("dp", "tensor"),
        P("dp"),
        P("dp"),
        P("dp", None),
        P(None, "tensor"),
        P(None, ("dp", "tensor")),
        P(None, ("dp", "tensor")),
        P("dp", None),
        P("dp", None),
        P(),
    )
    out_specs = (
        P(("dp", "tensor"), None),
        P(("dp", "tensor"), None),
        P("dp", "tensor"),
        P("dp", "tensor"),
        P("dp", "tensor"),
        P("dp", "tensor"),
        P("dp"),
        P("dp"),
        P("dp", None),
        P(None, "tensor"),
        P(None, ("dp", "tensor")),
        P(None, ("dp", "tensor")),
    )
    return jax.shard_map(body, mesh=mesh, in_specs=in_specs, out_specs=out_specs, check_vma=False)
```

```python
import jax
import jax.numpy as jnp
from jax import lax
from jax.experimental import pallas as pl
from jax.experimental.pallas import tpu as pltpu
from jax.sharding import PartitionSpec as P

HEAD_DIM = 64
SPLIT = 4
EPSILON = 1e-06
MASKED_SCORE = -1e30
LANES = 128
SCORE_SCALE = HEAD_DIM ** (-0.5)
HIGHEST = lax.Precision.HIGHEST
VMEM_BYTES = 20 * 1024 * 1024
VMEM_MOST = 60 * 1024 * 1024
F32 = jnp.float32
BF16 = jnp.bfloat16

Z_AT, X_AT, C_AT, Y_AT, DATA_AT = range(5)


class Place:
    def __init__(self, ref):
        self.ref = ref

    def __getitem__(self, which):
        place = self.ref[0]
        return {
            Z_AT: place // (2 * SPLIT),
            X_AT: (place // 4) % 2,
            C_AT: (place // 2) % 2,
            Y_AT: place % 2,
            DATA_AT: place // 2,
        }[which]


def matmul(left, right, precision=None):
    return jnp.dot(left, right, precision=precision, preferred_element_type=F32)


def matmul_nt(left, right, precision=None):
    return lax.dot_general(
        left, right, (((1,), (1,)), ((), ())), precision=precision, preferred_element_type=F32
    )


def matmul_tn(left, right, precision=None):
    return lax.dot_general(
        left, right, (((0,), (0,)), ((), ())), precision=precision, preferred_element_type=F32
    )


def iota(shape, dim):
    return lax.broadcasted_iota(jnp.int32, shape, dim)


def shape_of(shape, dtype):
    return jax.ShapeDtypeStruct(shape, dtype)


def run(kernel, scalars, operands, outs, scratch=(), flops=1, after=(), far=0, far_outs=0, vmem=VMEM_BYTES):
    waits = len(after)

    def wrapped(place_ref, *refs):
        kernel(Place(place_ref), *refs[waits:])

    return pl.pallas_call(
        wrapped,
        out_shape=list(outs),
        in_specs=[pl.BlockSpec(memory_space=pltpu.SMEM)]
        + [pl.BlockSpec(memory_space=pl.ANY)] * waits
        + [pl.BlockSpec(memory_space=pltpu.HBM)] * far
        + [pl.BlockSpec(memory_space=pltpu.VMEM)] * (len(operands) - far),
        out_specs=[pl.BlockSpec(memory_space=pltpu.HBM)] * far_outs
        + [pl.BlockSpec(memory_space=pltpu.VMEM)] * (len(outs) - far_outs),
        scratch_shapes=list(scratch),
        compiler_params=pltpu.CompilerParams(vmem_limit_bytes=vmem),
        cost_estimate=pl.CostEstimate(flops=flops, bytes_accessed=1, transcendentals=0),
    )(scalars, *after, *operands)


def inverse_rms(values):
    return lax.rsqrt(jnp.mean(values * values, axis=-1, keepdims=True) + EPSILON)


def router_softmax(rows, router, expert_count):
    logits = matmul(rows, router)
    logits = jnp.where(iota(logits.shape, 1) < expert_count, logits, MASKED_SCORE)
    weights = jnp.exp(logits - jnp.max(logits, axis=-1, keepdims=True))
    return weights / jnp.sum(weights, axis=-1, keepdims=True)


def swap(values, axis, mask):
    count = lax.axis_size(axis)
    return lax.ppermute(values, axis, [(i, i ^ mask) for i in range(count)])


def stacked(pieces):
    parts = [piece[...].astype(F32) for piece in pieces]
    return parts[0] if len(parts) == 1 else jnp.concatenate(parts, axis=0)


def store_pieces(refs, values):
    rows = values.shape[0] // len(refs)
    for number, ref in enumerate(refs):
        ref[...] = values[number * rows : (number + 1) * rows].astype(ref.dtype)


def body(
    tokens,
    cotangent,
    query_weight,
    key_weight,
    value_weight,
    output_weight,
    attention_scale,
    expert_scale,
    router,
    bucket_bias,
    expert_up_weight,
    expert_down_weight,
    routes,
    lengths,
    buckets,
):
    row_count, width = tokens.shape
    block_len = routes.shape[0]
    expert_count = router.shape[1]
    bucket_count, local_heads = bucket_bias.shape
    head_width = local_heads * HEAD_DIM
    capacity = max(2, block_len * 5 // (4 * expert_count))
    half = (capacity + 1) // 2
    slot_rows = expert_count * half
    data_count = lax.axis_size("dp")
    shard_rows = width // data_count
    hidden_local = expert_up_weight.shape[1]
    tensor_count = lax.axis_size("tensor")
    span = 2 * block_len
    distances = buckets.shape[0]
    cut = width // 3

    data_index = lax.axis_index("dp")
    y_index = lax.axis_index("tensor")
    scalars = (data_index * 2 + y_index).astype(jnp.int32).reshape(1)

    staged = shard_rows % 16 == 0
    slot_pieces = expert_count if half % 8 == 0 else 1
    z_masks = [j * SPLIT for j in range(expert_count)]

    def over_z(pieces):
        if len(pieces) == 1:
            stack = pieces[0].reshape((expert_count, half) + pieces[0].shape[1:])
            moved = [stack[0]] + [swap(stack[j], "dp", z_masks[j]) for j in range(1, expert_count)]
            return [jnp.concatenate(moved, axis=0)]
        return [pieces[0]] + [swap(pieces[j], "dp", z_masks[j]) for j in range(1, expert_count)]

    small_columns = -(-(expert_count + 2) // LANES) * LANES
    weight_columns = 4 * head_width
    def pack(idx, *refs):
        sources, refs = refs[:15], refs[15:]
        (out_ref, rows_ref, rest_ref, facts_ref), refs = refs[:4], refs[4:]
        router_ref, attn_ref, moe_ref, *small_refs, sems = refs
        targets = (
            [out_ref.at[:, pl.ds(number * head_width, head_width)] for number in range(4)]
            + [router_ref, attn_ref, moe_ref]
            + [rows_ref.at[pl.ds(number * row_count, row_count), :] for number in range(2)]
            + small_refs
            + [
                ref.at[pl.ds(at, rows), pl.ds(number * hidden_local, hidden_local)]
                for number in range(2)
                for ref, at, rows in (
                    (rows_ref, 2 * row_count, cut),
                    (rest_ref, 0, width - cut),
                )
            ]
        )
        sources = list(sources[:13]) + [
            source.at[pl.ds(at, rows), :]
            for source in sources[13:]
            for at, rows in ((0, cut), (cut, width - cut))
        ]
        copies = [
            pltpu.make_async_copy(source, target, sems.at[number])
            for number, (source, target) in enumerate(zip(sources, targets))
        ]
        for copy in copies:
            copy.start()
        for copy in copies[4:7]:
            copy.wait()
        diagonal = iota((shard_rows, shard_rows), 0) == iota((shard_rows, shard_rows), 1)
        lane = iota((shard_rows, small_columns), 1)

        def column(row_ref):
            row = row_ref[...].astype(F32)
            return jnp.sum(jnp.where(diagonal, row, 0.0), axis=1, keepdims=True)

        spread_router = matmul_tn(
            router_ref[...],
            (iota((expert_count, small_columns), 0) == iota((expert_count, small_columns), 1))
            .astype(F32)
            .astype(BF16),
        )
        small = jnp.where(lane == expert_count, column(attn_ref), spread_router)
        small = jnp.where(lane == expert_count + 1, column(moe_ref), small)
        out_ref[:, weight_columns:] = small.astype(BF16)
        for copy in copies[:4] + copies[7:]:
            copy.wait()
        length_ref, bucket_ref, table_ref, route_ref = small_refs
        facts_ref[...] = jnp.zeros(facts_ref.shape, F32)
        facts_ref[0:1, :2] = length_ref[...].astype(F32)
        facts_ref[1:2, :distances] = bucket_ref[...].astype(F32)
        facts_ref[2:3, :block_len] = route_ref[...].astype(F32)
        facts_ref[8 : 8 + local_heads, :bucket_count] = table_ref[...]

    packed, rows_own, rest_own, facts = run(
        pack,
        scalars,
        [
            query_weight,
            key_weight,
            value_weight,
            output_weight,
            router.T,
            attention_scale[None, :],
            expert_scale[None, :],
            tokens,
            cotangent,
            lengths,
            buckets[None, :],
            bucket_bias.T,
            routes.reshape(1, block_len),
            expert_up_weight,
            expert_down_weight,
        ],
        [
            shape_of((shard_rows, weight_columns + small_columns), BF16),
            shape_of((2 * row_count + cut, 2 * hidden_local), BF16),
            shape_of((width - cut, 2 * hidden_local), BF16),
            shape_of((16, span), F32),
        ],
        [
            pltpu.VMEM((expert_count, shard_rows), BF16),
            pltpu.VMEM((1, shard_rows), BF16),
            pltpu.VMEM((1, shard_rows), BF16),
            pltpu.VMEM(lengths.shape, jnp.int32),
            pltpu.VMEM((1, distances), jnp.int32),
            pltpu.VMEM((local_heads, bucket_count), F32),
            pltpu.VMEM((1, block_len), jnp.int32),
            pltpu.SemaphoreType.DMA((17,)),
        ],
        far=15,
        vmem=VMEM_MOST,
    )
    if staged:
        gathered = [packed] + [swap(packed, "dp", mask) for mask in z_masks[1:]]
    else:
        gathered = [lax.all_gather(packed, "dp", axis=0, tiled=True)]

    def piece_offset(idx, number):
        j_z = number % expert_count
        j_x = (number // expert_count) % 2
        j_c = number // (2 * expert_count)
        index = (idx[Z_AT] ^ j_z) * SPLIT + (idx[X_AT] ^ j_x) * 2 + (idx[C_AT] ^ j_c)
        return pl.multiple_of(index * shard_rows, 16)

    rows_other = swap(rows_own, "tensor", 1)

    def prepare(idx, facts_ref, mine, others, *refs):
        x_ref, bias_ref, own_ref, other_ref, xs_ref, gs_ref, live_ref = refs[:7]
        pick_ref, back_ref, live_rows_ref = refs[7:10]
        live_parts = refs[10:-2]
        cot_full, head_table = refs[-2:]
        own_at = pl.multiple_of(idx[Y_AT] * row_count, row_count)
        other_at = pl.multiple_of((1 - idx[Y_AT]) * row_count, row_count)
        for at, rows in ((own_at, mine), (other_at, others)):
            x_ref[pl.ds(at, row_count), :] = rows[:row_count, :]
            cot_full[pl.ds(at, row_count), :] = rows[row_count : 2 * row_count, :]

        first = facts_ref[0:1, 0:1].astype(jnp.int32)
        active = first + facts_ref[0:1, 1:2].astype(jnp.int32)
        live_rows_ref[...] = jnp.broadcast_to(
            (iota((block_len, 1), 0) < active).astype(F32), live_rows_ref.shape
        )

        def segment(position):
            return jnp.where(position < first, 0, jnp.where(position < active, 1, 2))

        allowed = segment(iota((block_len, block_len), 0)) == segment(
            iota((block_len, block_len), 1)
        )
        pick = facts_ref[1:2, :distances].astype(jnp.int32) == iota((LANES, distances), 0)
        pick = pick.astype(F32)
        head_table[...] = jnp.zeros(head_table.shape, F32)
        head_table[:local_heads, :distances] = matmul(
            facts_ref[8 : 8 + local_heads, :bucket_count], pick[:bucket_count], HIGHEST
        )
        mirror = (
            iota((distances, span), 0) + iota((distances, span), 1) == distances - 1
        ).astype(F32)
        back_ref[...] = matmul(pick.astype(BF16), mirror.astype(BF16)).astype(BF16)
        for head in range(local_heads):
            line = jnp.broadcast_to(head_table[head : head + 1, :], (block_len, span))
            turned = pltpu.roll(line, block_len + 1, 1, stride=1, stride_axis=0)
            bias_ref[head] = jnp.where(allowed, turned[:, :block_len], MASKED_SCORE)

        route = facts_ref[2:3, :block_len].astype(jnp.int32)
        chosen = (route == iota((LANES, block_len), 0)).astype(F32)
        earlier = (iota((block_len, block_len), 0) < iota((block_len, block_len), 1)).astype(F32)
        counts = matmul(chosen.astype(BF16), earlier.astype(BF16))
        slot = jnp.sum(chosen * counts, axis=0, keepdims=True).astype(jnp.int32)
        row_id = iota((slot_rows, block_len), 0)

        def selection(which):
            place = slot - half * which
            code = (route ^ idx[Z_AT]) * half + place
            code = jnp.where((place >= 0) & (place < half), code, -1)
            return (row_id == code).astype(F32)

        own_select = selection(idx[Y_AT])
        own_bf = own_select.astype(BF16)
        own_ref[...] = own_bf
        other_ref[...] = selection(1 - idx[Y_AT]).astype(BF16)
        xs_ref[...] = matmul(own_bf, x_ref[...]).astype(BF16)
        gs_ref[...] = matmul(own_bf, cot_full[...]).astype(BF16)
        live_select = own_select * (iota((1, block_len), 1) < active).astype(F32)
        live_ref[...] = jnp.broadcast_to(
            jnp.sum(live_select, axis=1, keepdims=True), live_ref.shape
        )
        pick_ref[...] = matmul_nt(own_bf, chosen.astype(BF16))
        store_pieces(live_parts, matmul(live_select.astype(BF16), cot_full[...]))

    piece_shape = shape_of((slot_rows // slot_pieces, width), BF16)
    prepared = run(
        prepare,
        scalars,
        [facts, rows_own, rows_other],
        [
            shape_of((block_len, width), BF16),
            shape_of((local_heads, block_len, block_len), F32),
            shape_of((slot_rows, block_len), BF16),
            shape_of((slot_rows, block_len), BF16),
            shape_of((slot_rows, width), BF16),
            shape_of((slot_rows, width), BF16),
            shape_of((slot_rows, LANES), F32),
            shape_of((slot_rows, LANES), F32),
            shape_of((LANES, span), BF16),
            shape_of((block_len, LANES), F32),
        ]
        + [piece_shape] * slot_pieces,
        [pltpu.VMEM((block_len, width), BF16), pltpu.VMEM((8, span), F32)],
    )
    x_full, bias, own_select, other_select, x_slot, g_slot = prepared[:6]
    live_slot, pick_slot, pick_back, live_rows = prepared[6:10]
    g_home = prepared[10:]
    g_wait = []
    if staged:
        g_home = lax.optimization_barrier((*g_home, *gathered[1:expert_count]))[:slot_pieces]
        gathered = gathered + [swap(piece, "dp", 2) for piece in gathered]
        *gathered, _ = lax.optimization_barrier((*gathered, x_full))
        gathered = gathered + [swap(piece, "dp", 1) for piece in gathered]
    g_rows = over_z(list(g_home))
    if staged:
        g_wait = g_rows[1:]
    g_rows = g_rows + [swap(jnp.concatenate(g_rows, axis=0), "dp", 2)]
    rest_send, _ = lax.optimization_barrier((rest_own, rows_other))
    rest_y = swap(rest_send, "tensor", 1)
    expert_parts = [rows_own, rest_own, rows_other, rest_y]
    expert_parts += [swap(rows_own, "dp", 1), swap(rest_own, "dp", 1), swap(rows_other, "dp", 1)]

    def to_experts(pieces):
        arrived = over_z(list(pieces))
        return arrived + [swap(piece, "dp", 2) for piece in arrived]


    qkv_width = 3 * head_width
    piece_count = len(gathered)

    def attend(idx, live_ref, x_ref, bias_ref, own_ref, other_ref, xs_ref, *refs):
        pieces = refs[:piece_count]
        (
            send_ref,
            keep_ref,
            normed_ref,
            qkv_ref,
            probs_ref,
            context_ref,
            weight_ref,
            small_ref,
            gain_ref,
        ) = refs[piece_count:]
        if piece_count == 1:
            weight_ref[...] = pieces[0][:, :weight_columns]
            small_ref[...] = pieces[0][:, weight_columns:]
        else:
            for number, piece in enumerate(pieces):
                at = piece_offset(idx, number)
                weight_ref[pl.ds(at, shard_rows), :] = piece[:, :weight_columns]
                small_ref[pl.ds(at, shard_rows), :] = piece[:, weight_columns:]
        turned = small_ref[...].astype(F32).T
        gain = turned[expert_count : expert_count + 1, :]
        gain_ref[...] = jnp.broadcast_to(gain, gain_ref.shape)
        gain_ref[1:2, :] = turned[expert_count + 1 : expert_count + 2, :]
        x = x_ref[...].astype(F32)
        normed = (x * inverse_rms(x) * gain).astype(BF16)
        normed_ref[...] = normed
        qkv_ref[...] = matmul(normed, weight_ref[:, :qkv_width]).astype(BF16)
        live = live_ref[:, :1]
        for head in range(local_heads):
            at = head * HEAD_DIM
            query = qkv_ref[:, at : at + HEAD_DIM]
            key = qkv_ref[:, head_width + at : head_width + at + HEAD_DIM]
            value = qkv_ref[:, 2 * head_width + at : 2 * head_width + at + HEAD_DIM]
            scores = matmul_nt(query, key) * SCORE_SCALE + bias_ref[head]
            weights = jnp.exp(scores - jnp.max(scores, axis=-1, keepdims=True))
            probs = weights / jnp.sum(weights, axis=-1, keepdims=True)
            probs_ref[head] = probs
            context = matmul(probs.astype(BF16), value) * live
            context_ref[:, at : at + HEAD_DIM] = context.astype(BF16)
        out = matmul_nt(context_ref[...], weight_ref[:, qkv_width:]).astype(BF16)
        send_ref[...] = matmul(other_ref[...], out).astype(BF16)
        keep_ref[...] = matmul(own_ref[...], out) + xs_ref[...].astype(F32)

    send, keep, normed, qkv, probs, context, weights, router_small, gains = run(
        attend,
        scalars,
        [live_rows, x_full, bias, own_select, other_select, x_slot] + gathered,
        [
            shape_of((slot_rows, width), BF16),
            shape_of((slot_rows, width), F32),
            shape_of((block_len, width), BF16),
            shape_of((block_len, qkv_width), BF16),
            shape_of((local_heads, block_len, block_len), F32),
            shape_of((block_len, head_width), BF16),
            shape_of((width, weight_columns), BF16),
            shape_of((width, small_columns), BF16),
            shape_of((8, width), F32),
        ],
        after=g_wait,
    )
    arrived = swap(send, "tensor", 1)
    rest_y, _ = lax.optimization_barrier((rest_y, arrived))
    expert_parts.append(swap(rest_y, "dp", 1))

    def second_norm(idx, keep_ref, arrived_ref, gain_ref, residual_ref, scale_ref, nm_ref, *parts):
        residual = keep_ref[...] + arrived_ref[...].astype(F32)
        scale = inverse_rms(residual)
        residual_ref[...] = residual
        scale_ref[...] = jnp.broadcast_to(scale, scale_ref.shape)
        rows = residual * scale * gain_ref[1:2, :]
        nm_ref[...] = rows.astype(BF16)
        store_pieces(parts, rows)

    residual, scale_moe, normed_moe, *row_home = run(
        second_norm,
        scalars,
        [keep, arrived, gains],
        [
            shape_of((slot_rows, width), F32),
            shape_of((slot_rows, LANES), F32),
            shape_of((slot_rows, width), BF16),
        ]
        + [piece_shape] * slot_pieces,
        after=expert_parts[4:7],
    )
    expert_rows = to_experts(row_home)

    expert_in = 2 * slot_rows
    parts = 4

    def experts(idx, router_ref, *refs):
        count = 2 * slot_pieces
        row_parts, refs = refs[:count], refs[count:]
        g_parts, refs = refs[: slot_pieces + 1], refs[slot_pieces + 1 :]
        weights, refs = refs[: 2 * parts], refs[2 * parts :]
        send_ref, keep_ref, rows_ref, total_ref, hidden_ref, pre_ref = refs
        rows = stacked(row_parts).astype(BF16)
        rows_ref[...] = rows
        routed = router_softmax(rows, router_ref[...], expert_count)
        mine = (iota(routed.shape, 1) == idx[Z_AT]).astype(F32)
        gate = jnp.sum(routed * mine, axis=1, keepdims=True)
        total = (stacked(g_parts) * gate).astype(BF16)
        total_ref[...] = total
        forward = jnp.zeros((expert_in, width), F32)
        backward = jnp.zeros((expert_in, width), F32)
        for part in range(parts):
            at = part * hidden_local
            head, rest = weights[2 * part : 2 * part + 2]
            up, down = [
                jnp.concatenate(
                    [
                        head[2 * row_count :, number * hidden_local : (number + 1) * hidden_local],
                        rest[:, number * hidden_local : (number + 1) * hidden_local],
                    ],
                    axis=0,
                )
                for number in range(2)
            ]
            pre = matmul(rows, up)
            square = pre * pre
            inner = 0.7978845608028654 * pre * (1.0 + 0.044715 * square)
            tanh = jnp.tanh(inner)
            hidden = (0.5 * pre * (1.0 + tanh)).astype(BF16)
            slope = 0.5 * (1.0 + tanh) + 0.5 * pre * (1.0 - tanh * tanh) * (
                0.7978845608028654 * (1.0 + 3.0 * 0.044715 * square)
            )
            hidden_ref[:, at : at + hidden_local] = hidden
            grad_pre = (matmul(total, down) * slope).astype(BF16)
            pre_ref[:, at : at + hidden_local] = grad_pre
            forward += matmul_nt(hidden, down)
            backward += matmul_nt(grad_pre, up)
        keep_ref[:, :width] = forward[:slot_rows]
        keep_ref[:, width:] = backward[:slot_rows]
        send_ref[:, :width] = forward[slot_rows:].astype(BF16)
        send_ref[:, width:] = backward[slot_rows:].astype(BF16)

    send, keep, rows_in, total_in, hidden, grad_pre = run(
        experts,
        scalars,
        [router_small] + expert_rows + g_rows + expert_parts,
        [
            shape_of((slot_rows, 2 * width), BF16),
            shape_of((slot_rows, 2 * width), F32),
            shape_of((expert_in, width), BF16),
            shape_of((expert_in, width), BF16),
            shape_of((expert_in, parts * hidden_local), BF16),
            shape_of((expert_in, parts * hidden_local), BF16),
        ],
    )
    arrived = swap(send, "dp", 2)

    def expert_grads(first):
        def grads(idx, rows_ref, total_ref, hidden_ref, pre_ref, *outs):
            for part in range(2):
                at = (first + part) * hidden_local
                up_grad = matmul_tn(rows_ref[...], pre_ref[:, at : at + hidden_local])
                down_grad = matmul_tn(total_ref[...], hidden_ref[:, at : at + hidden_local])
                ref, place = (outs[0], 2 * part) if len(outs) == 1 else (outs[part], 0)
                ref[place] = up_grad.astype(ref.dtype)
                ref[place + 1] = down_grad.astype(ref.dtype)

        return grads

    weight_shape = (width, hidden_local)
    grad_inputs = [rows_in, total_in, hidden, grad_pre]
    (grads_c,) = run(
        expert_grads(2), scalars, grad_inputs, [shape_of((4,) + weight_shape, BF16)]
    )
    grads_own, grads_y = run(
        expert_grads(0),
        scalars,
        grad_inputs,
        [shape_of((2,) + weight_shape, F32), shape_of((2,) + weight_shape, BF16)],
    )
    from_c = swap(grads_c, "dp", 1)

    def fold_y(idx, y_ref, c_ref, up_ref, down_ref):
        for number, ref in enumerate((up_ref, down_ref)):
            total = y_ref[number].astype(F32) + c_ref[2 + number].astype(F32)
            if number == 0:
                ref[...] = total.astype(BF16)
            else:
                ref[:, :hidden_local] = total[: width // 2].astype(BF16)
                ref[:, hidden_local:] = total[width // 2 :].astype(BF16)

    up_passed, down_passed = run(
        fold_y,
        scalars,
        [grads_y, from_c],
        [shape_of(weight_shape, BF16), shape_of((width // 2, 2 * hidden_local), BF16)],
    )
    up_from_y = swap(up_passed, "tensor", 1)

    def add_x(idx, keep_ref, arrived_ref, *parts_out):
        store_pieces(parts_out, keep_ref[...] + arrived_ref[...].astype(F32))

    both_shape = shape_of((slot_rows // slot_pieces, 2 * width), BF16)
    back = run(add_x, scalars, [keep, arrived], [both_shape] * slot_pieces)
    home = over_z(list(back))

    def fold_grad(number):
        def fold(idx, own_ref, c_ref, y_ref, out_ref, done_ref):
            done_ref[...] = jnp.zeros(done_ref.shape, F32)
            if number == 0:
                out_ref[...] = own_ref[0] + c_ref[0].astype(F32) + y_ref[...].astype(F32)
                return
            for part in range(2):
                rows = slice(part * (width // 2), (part + 1) * (width // 2))
                columns = slice(part * hidden_local, (part + 1) * hidden_local)
                out_ref[rows, :] = (
                    own_ref[1, rows, :]
                    + c_ref[1, rows, :].astype(F32)
                    + y_ref[slot_rows + row_count :, columns].astype(F32)
                )

        return fold

    grad_w_in, up_done = run(
        fold_grad(0),
        scalars,
        [grads_own, from_c, up_from_y],
        [shape_of(weight_shape, F32), shape_of((8, LANES), F32)],
        after=[back[0]],
    )

    expert_pad = -(-expert_count // 8) * 8

    def at_home(idx, *refs):
        pieces, refs = refs[:slot_pieces], refs[slot_pieces:]
        (
            residual_ref,
            scale_ref,
            nm_ref,
            g_ref,
            live_ref,
            pick_ref,
            gain_ref,
            router_ref,
            mid_ref,
            layer_ref,
            gain_out,
            router_out,
        ) = refs
        returned = stacked(pieces)
        total, back_rows = returned[:, :width], returned[:, width:]
        residual = residual_ref[...]
        scale = scale_ref[:, :1]
        live = live_ref[:, :1]
        pick = pick_ref[...]
        gain = gain_ref[1:2, :]
        g = g_ref[...].astype(F32)
        routed = router_softmax(nm_ref[...], router_ref[...], expert_count)
        gate = jnp.sum(routed * pick, axis=1, keepdims=True)
        layer_ref[...] = (residual + gate * total * live).astype(BF16)
        grad_gate = jnp.sum(g * total, axis=1, keepdims=True) * live
        grad_logits = grad_gate * gate * (pick - routed)
        upstream = back_rows + matmul_nt(grad_logits, router_ref[...].astype(F32), HIGHEST)
        scaled = upstream * gain
        grad_mid = (
            g
            + scale * scaled
            - residual * scale**3 * jnp.mean(scaled * residual, axis=-1, keepdims=True)
        )
        mid_ref[...] = grad_mid.astype(BF16)
        gain_out[...] = jnp.broadcast_to(
            jnp.sum(upstream * residual * scale, axis=0, keepdims=True), gain_out.shape
        )
        router_grad = matmul_tn(grad_logits, nm_ref[...].astype(F32), HIGHEST)
        router_out[...] = router_grad[:expert_pad]

    mid_own, layer_own, gain_moe, router_part = run(
        at_home,
        scalars,
        home
        + [residual, scale_moe, normed_moe, g_slot, live_slot, pick_slot, gains, router_small],
        [
            shape_of((slot_rows, width), BF16),
            shape_of((slot_rows, width), BF16),
            shape_of((8, width), F32),
            shape_of((expert_pad, width), F32),
        ],
        after=[up_done],
    )
    mid_other = swap(mid_own, "tensor", 1)

    half_pieces = 2 * expert_count
    rest_part = 2 * LANES
    first_part = weight_columns - rest_part
    small_blocks = width // rest_part

    def emit_rows(idx, full_ref, outs):
        if not staged:
            outs[0][...] = full_ref[...]
            return
        keep_ref, send_ref = outs
        for number in range(half_pieces):
            at = piece_offset(idx, number)
            keep_ref[number] = full_ref[pl.ds(at, shard_rows), :]
            at = piece_offset(idx, number + half_pieces)
            send_ref[number] = full_ref[pl.ds(at, shard_rows), :].astype(BF16)

    if staged:
        row_shapes = [
            shape_of((half_pieces, shard_rows, weight_columns), F32),
            shape_of((half_pieces, shard_rows, weight_columns), BF16),
        ]
    else:
        row_shapes = [shape_of((width, weight_columns), F32)]

    small_rows = -(-(expert_count + 2 + tensor_count) // 8) * 8

    def store_halves(ref, at, values):
        high = values.astype(BF16)
        both = jnp.concatenate([high.astype(F32), values - high.astype(F32)], axis=0).astype(BF16)
        for block in range(small_blocks):
            row = at + 2 * small_rows * block
            ref[row : row + 2 * small_rows, :] = both[
                :, block * rest_part : (block + 1) * rest_part
            ]

    def load_halves(ref, at):
        blocks = []
        for block in range(small_blocks):
            row = at + 2 * small_rows * block
            both = ref[row : row + 2 * small_rows, :].astype(F32)
            blocks.append(both[:small_rows] + both[small_rows:])
        return jnp.concatenate(blocks, axis=1)

    def attend_back(
        idx,
        own_ref,
        other_ref,
        mid_ref,
        mid_other_ref,
        context_ref,
        weight_ref,
        qkv_ref,
        probs_ref,
        normed_ref,
        x_ref,
        back_ref,
        live_ref,
        moe_ref,
        router_ref,
        layer_ref,
        down_ref,
        *refs,
    ):
        ga_ref, keep_ref, send_ref, small_ref = refs[:4]
        outs = refs[4:-3]
        grads, full, upstream = refs[-3:]
        live = live_ref[:, :1]
        grad_attention = matmul_tn(own_ref[...], mid_ref[...]) + matmul_tn(
            other_ref[...], mid_other_ref[...]
        )
        ga_ref[...] = grad_attention.astype(BF16)
        full[:, qkv_width:] = matmul_tn(ga_ref[...], context_ref[...])
        grad_context = matmul(ga_ref[...], weight_ref[:, qkv_width:]) * live
        grad_context = grad_context.astype(BF16)
        mirror = (
            iota((block_len, block_len), 0) + iota((block_len, block_len), 1) == block_len - 1
        ).astype(BF16)
        lines = []
        for head in range(local_heads):
            at = head * HEAD_DIM
            query = qkv_ref[:, at : at + HEAD_DIM]
            key = qkv_ref[:, head_width + at : head_width + at + HEAD_DIM]
            value = qkv_ref[:, 2 * head_width + at : 2 * head_width + at + HEAD_DIM]
            back = grad_context[:, at : at + HEAD_DIM]
            probs = probs_ref[head]
            grad_value = matmul_tn(probs.astype(BF16), back)
            grad_probs = matmul_nt(back, value)
            grad_scores = probs * (
                grad_probs - jnp.sum(probs * grad_probs, axis=-1, keepdims=True)
            )
            grad_scores = grad_scores.astype(BF16)
            grad_query = matmul(grad_scores, key) * SCORE_SCALE
            grad_key = matmul_tn(grad_scores, query) * SCORE_SCALE
            grads[:, at : at + HEAD_DIM] = grad_query.astype(BF16)
            grads[:, head_width + at : head_width + at + HEAD_DIM] = grad_key.astype(BF16)
            grads[:, 2 * head_width + at : 2 * head_width + at + HEAD_DIM] = grad_value.astype(
                BF16
            )
            lines_left = jnp.concatenate(
                [matmul(grad_scores, mirror), jnp.zeros((block_len, span - block_len), F32)], axis=1
            )
            rows = block_len
            while rows > 8:
                rows //= 2
                lines_left = lines_left[:rows] + pltpu.roll(lines_left[rows:], rows, 1)
            lines_left = pltpu.roll(lines_left, 0, 1, stride=1, stride_axis=0)
            lines.append(jnp.sum(lines_left, axis=0, keepdims=True))
        lines.append(jnp.zeros((8 - local_heads, span), F32))
        diagonal = jnp.concatenate(lines, axis=0)
        table = matmul_nt(diagonal, back_ref[...].astype(F32), HIGHEST)
        line = [table[head : head + 1, :] for head in range(local_heads)]
        line.append(jnp.zeros((1, width - local_heads * LANES), F32))
        line = jnp.concatenate(line[: local_heads + (width > local_heads * LANES)], axis=1)
        all_grads = grads[...]
        grad_normed = matmul_nt(all_grads, weight_ref[:, :qkv_width])
        upstream[...] = grad_normed
        x = x_ref[...].astype(F32)
        gain = jnp.sum(grad_normed * x * inverse_rms(x), axis=0, keepdims=True)
        row = iota((small_rows, width), 0)
        small = jnp.where(row == expert_count, gain, 0.0)
        small = jnp.where(row == expert_count + 1, moe_ref[:1, :], small)
        small_ref[...] = jnp.where(row == expert_count + 2 + idx[Y_AT], line, small)
        small_ref[:expert_count, :] = router_ref[:expert_count, :]
        own_at = pl.multiple_of(idx[Y_AT] * row_count, row_count)
        other_at = pl.multiple_of((1 - idx[Y_AT]) * row_count, row_count)
        keep_ref[...] = upstream[pl.ds(own_at, row_count), :]
        send_ref[slot_rows : slot_rows + row_count, :] = upstream[
            pl.ds(other_at, row_count), :
        ].astype(BF16)
        send_ref[:slot_rows, :] = layer_ref[...]
        send_ref[slot_rows + row_count :, :] = down_ref[...]
        full[:, :qkv_width] = matmul_tn(normed_ref[...], all_grads)
        emit_rows(idx, full, outs)

    grad_attention, up_keep, up_send, small, *partial_rows = run(
        attend_back,
        scalars,
        [
            own_select,
            other_select,
            mid_own,
            mid_other,
            context,
            weights,
            qkv,
            probs,
            normed,
            x_full,
            pick_back,
            live_rows,
            gain_moe,
            router_part,
            layer_own,
            down_passed,
        ],
        [
            shape_of((block_len, width), BF16),
            shape_of((row_count, width), F32),
            shape_of((slot_rows + row_count + width // 2, width), BF16),
            shape_of((small_rows, width), F32),
        ]
        + row_shapes,
        [
            pltpu.VMEM((block_len, qkv_width), BF16),
            pltpu.VMEM((width, weight_columns), F32),
            pltpu.VMEM((block_len, width), F32),
        ],
    )
    def small_over_y(idx, small_ref, other_ref, out_ref):
        out_ref[...] = small_ref[...] + other_ref[...]

    (small,) = run(
        small_over_y,
        scalars,
        [small, swap(small, "tensor", 1)],
        [shape_of((small_rows, width), F32)],
    )
    up_send, _ = lax.optimization_barrier((up_send, small))
    up_other = swap(up_send, "tensor", 1)

    out_shapes = [shape_of((shard_rows, head_width), F32)] * 4
    if staged:
        held, outgoing = partial_rows
        from_core = swap(outgoing, "dp", 1)

        small_core = swap(small, "dp", 1)
        extra_rows = 2 * small_rows * small_blocks

        def after_core(idx, small_ref, small_core, held_ref, from_ref, x_send, x_keep, *z_refs):
            z_sends, z_keep, small_keep = z_refs[:-2], z_refs[-2], z_refs[-1]
            small = small_ref[...] + small_core[...]
            small_keep[...] = small

            def total(number, columns):
                return held_ref[number, :, columns] + from_ref[number, :, columns].astype(F32)

            front, rest = slice(0, first_part), slice(first_part, weight_columns)
            for j in range(expert_count):
                x_keep[j] = total(j, front)
                x_send[j] = total(expert_count + j, front).astype(BF16)
                if j > 0:
                    store_halves(z_sends[j - 1], 2 * shard_rows, small)
                for x in range(2):
                    piece = total(x * expert_count + j, rest)
                    if j == 0:
                        z_keep[x] = piece
                    else:
                        z_sends[j - 1][x * shard_rows : (x + 1) * shard_rows, :] = piece.astype(
                            BF16
                        )

        x_send, x_keep, *z_sends, z_keep, small = run(
            after_core,
            scalars,
            [small, small_core, held, from_core],
            [
                shape_of((expert_count, shard_rows, first_part), BF16),
                shape_of((expert_count, shard_rows, first_part), F32),
            ]
            + [shape_of((2 * shard_rows + extra_rows, rest_part), BF16)] * (expert_count - 1)
            + [shape_of((2, shard_rows, rest_part), F32), shape_of((small_rows, width), F32)],
        )
        from_x = swap(x_send, "dp", 2)
        from_z = [swap(piece, "dp", z_masks[j + 1]) for j, piece in enumerate(z_sends)]


        def after_first(idx, small_ref, x_keep, from_x, z_keep, *refs):
            from_z, refs = refs[: expert_count - 1], refs[expert_count - 1 :]
            z_sends, (front_keep, x_send, rest_keep, small_keep) = refs[:-4], refs[-4:]
            front_keep[...] = x_keep[0] + from_x[0].astype(F32)
            for j in range(1, expert_count):
                z_sends[j - 1][...] = (x_keep[j] + from_x[j].astype(F32)).astype(BF16)
            small = small_ref[...]
            rest = [z_keep[0], z_keep[1]]
            for ref in from_z:
                small = small + load_halves(ref, 2 * shard_rows)
                for x in range(2):
                    rest[x] = rest[x] + ref[x * shard_rows : (x + 1) * shard_rows, :].astype(F32)
            small_keep[...] = small
            store_halves(x_send, shard_rows, small)
            rest_keep[...] = rest[0]
            x_send[:shard_rows, :] = rest[1].astype(BF16)

        *z_sends, front_keep, x_send, rest_keep, small = run(
            after_first,
            scalars,
            [small, x_keep, from_x, z_keep] + from_z,
            [shape_of((shard_rows, first_part), BF16)] * (expert_count - 1)
            + [
                shape_of((shard_rows, first_part), F32),
                shape_of((shard_rows + extra_rows, rest_part), BF16),
                shape_of((shard_rows, rest_part), F32),
                shape_of((small_rows, width), F32),
            ],
        )
        from_z = [swap(piece, "dp", z_masks[j + 1]) for j, piece in enumerate(z_sends)]
        from_x = swap(x_send, "dp", 2)
        late = [front_keep]

        def last_sum(idx, small_ref, front_keep, rest_keep, from_x, *refs):
            from_z, refs = refs[: expert_count - 1], refs[expert_count - 1 :]
            outs, (attn_out, moe_out, router_out, table_out, full) = refs[:-5], refs[-5:]
            front = front_keep[...]
            small = small_ref[...] + load_halves(from_x, shard_rows)
            for ref in from_z:
                front = front + ref[...].astype(F32)
            column = iota((LANES, width), 1) - idx[DATA_AT] * shard_rows
            select = (column == iota((LANES, width), 0)).astype(F32)
            shard = matmul_nt(small, select, HIGHEST)
            attn_out[...] = shard[expert_count : expert_count + 1, :shard_rows]
            moe_out[...] = shard[expert_count + 1 : expert_count + 2, :shard_rows]
            router_out[...] = shard[:expert_count, :shard_rows]
            mine = iota((small_rows, width), 0) == expert_count + 2 + idx[Y_AT]
            line = jnp.sum(jnp.where(mine, small, 0.0), axis=0, keepdims=True)
            lines = [line[:, head * LANES : (head + 1) * LANES] for head in range(local_heads)]
            table_out[...] = jnp.concatenate(lines, axis=0)[:, :bucket_count]
            full[:, :first_part] = front
            full[:, first_part:] = rest_keep[...] + from_x[:shard_rows, :].astype(F32)
            for number, out in enumerate(outs):
                out[...] = full[:, number * head_width : (number + 1) * head_width]

        *grad_matrices, grad_attn_scale, grad_moe_scale, grad_router, table = run(
            last_sum,
            scalars,
            [small, front_keep, rest_keep, from_x] + from_z,
            out_shapes
            + [
                shape_of((1, shard_rows), F32),
                shape_of((1, shard_rows), F32),
                shape_of((expert_count, shard_rows), F32),
                shape_of((local_heads, bucket_count), F32),
            ],
            [pltpu.VMEM((shard_rows, weight_columns), F32)],
        )
        grad_attn_scale, grad_moe_scale = grad_attn_scale[0], grad_moe_scale[0]
        grad_router, table = grad_router.T, table.T
    else:
        late = []
        summed = lax.psum_scatter(partial_rows[0], "dp", scatter_dimension=0, tiled=True)
        grad_matrices = [
            summed[:, number * head_width : (number + 1) * head_width] for number in range(4)
        ]
        small = lax.psum(small, "dp")
        shard = lax.dynamic_slice_in_dim(small, data_index * shard_rows, shard_rows, 1)
        grad_router = shard[:expert_count].T
        grad_attn_scale, grad_moe_scale = shard[expert_count], shard[expert_count + 1]
        table = lax.dynamic_slice_in_dim(small, expert_count + 2 + y_index, 1, 0)
        table = table[0, : local_heads * LANES].reshape(local_heads, LANES)[:, :bucket_count].T

    grad_w_out, _ = run(
        fold_grad(1),
        scalars,
        [grads_own, from_c, up_other],
        [shape_of(weight_shape, F32), shape_of((8, LANES), F32)],
        after=late,
    )
    def finish(
        idx, own_ref, other_ref, layer_ref, arrived_ref, ga_ref, keep_ref, tok_ref, gain_ref,
        layer_out, tokens_out, full
    ):
        own_at = pl.multiple_of(idx[Y_AT] * row_count, row_count)
        full[...] = matmul_tn(own_ref[...], layer_ref[...]) + matmul_tn(
            other_ref[...], arrived_ref[:slot_rows, :]
        )
        layer_out[...] = full[pl.ds(own_at, row_count), :].astype(BF16)
        x = tok_ref[...].astype(F32)
        scale = inverse_rms(x)
        scaled = keep_ref[...] + arrived_ref[slot_rows : slot_rows + row_count, :].astype(F32)
        scaled = scaled * gain_ref[:1, :]
        grad = scale * scaled - x * scale**3 * jnp.mean(scaled * x, axis=-1, keepdims=True)
        grad = grad + ga_ref[pl.ds(own_at, row_count), :].astype(F32)
        tokens_out[...] = grad.astype(BF16)

    layer_out, grad_tokens = run(
        finish,
        scalars,
        [
            own_select, other_select, layer_own, up_other, grad_attention, up_keep, tokens, gains,
        ],
        [shape_of((row_count, width), BF16)] * 2,
        [pltpu.VMEM((block_len, width), F32)],
        after=late,
    )

    return (
        layer_out,
        grad_tokens,
        *grad_matrices,
        grad_attn_scale,
        grad_moe_scale,
        grad_router,
        table,
        grad_w_in,
        grad_w_out,
    )


def solution(mesh):
    in_specs = (
        P(("dp", "tensor"), None),
        P(("dp", "tensor"), None),
        P("dp", "tensor"),
        P("dp", "tensor"),
        P("dp", "tensor"),
        P("dp", "tensor"),
        P("dp"),
        P("dp"),
        P("dp", None),
        P(None, "tensor"),
        P(None, ("dp", "tensor")),
        P(None, ("dp", "tensor")),
        P("dp", None),
        P("dp", None),
        P(),
    )
    out_specs = (
        P(("dp", "tensor"), None),
        P(("dp", "tensor"), None),
        P("dp", "tensor"),
        P("dp", "tensor"),
        P("dp", "tensor"),
        P("dp", "tensor"),
        P("dp"),
        P("dp"),
        P("dp", None),
        P(None, "tensor"),
        P(None, ("dp", "tensor")),
        P(None, ("dp", "tensor")),
    )
    return jax.shard_map(body, mesh=mesh, in_specs=in_specs, out_specs=out_specs, check_vma=False)
```

```python
import jax
import jax.numpy as jnp
from jax import lax
from jax.experimental import pallas as pl
from jax.experimental.pallas import tpu as pltpu
from jax.sharding import PartitionSpec as P

HEAD_DIM = 64
SPLIT = 4
EPSILON = 1e-06
MASKED_SCORE = -1e30
LANES = 128
SCORE_SCALE = HEAD_DIM ** (-0.5)
HIGHEST = lax.Precision.HIGHEST
VMEM_BYTES = 20 * 1024 * 1024
VMEM_MOST = 60 * 1024 * 1024
F32 = jnp.float32
BF16 = jnp.bfloat16

Z_AT, X_AT, C_AT, Y_AT, DATA_AT = range(5)


class Place:
    def __init__(self, ref):
        self.ref = ref

    def __getitem__(self, which):
        place = self.ref[0]
        return {
            Z_AT: place // (2 * SPLIT),
            X_AT: (place // 4) % 2,
            C_AT: (place // 2) % 2,
            Y_AT: place % 2,
            DATA_AT: place // 2,
        }[which]


def matmul(left, right, precision=None):
    return jnp.dot(left, right, precision=precision, preferred_element_type=F32)


def matmul_nt(left, right, precision=None):
    return lax.dot_general(
        left, right, (((1,), (1,)), ((), ())), precision=precision, preferred_element_type=F32
    )


def matmul_tn(left, right, precision=None):
    return lax.dot_general(
        left, right, (((0,), (0,)), ((), ())), precision=precision, preferred_element_type=F32
    )


def iota(shape, dim):
    return lax.broadcasted_iota(jnp.int32, shape, dim)


def shape_of(shape, dtype):
    return jax.ShapeDtypeStruct(shape, dtype)


def run(kernel, scalars, operands, outs, scratch=(), flops=1, after=(), far=0, far_outs=0, vmem=VMEM_BYTES):
    waits = len(after)

    def wrapped(place_ref, *refs):
        kernel(Place(place_ref), *refs[waits:])

    return pl.pallas_call(
        wrapped,
        out_shape=list(outs),
        in_specs=[pl.BlockSpec(memory_space=pltpu.SMEM)]
        + [pl.BlockSpec(memory_space=pl.ANY)] * waits
        + [pl.BlockSpec(memory_space=pltpu.HBM)] * far
        + [pl.BlockSpec(memory_space=pltpu.VMEM)] * (len(operands) - far),
        out_specs=[pl.BlockSpec(memory_space=pltpu.HBM)] * far_outs
        + [pl.BlockSpec(memory_space=pltpu.VMEM)] * (len(outs) - far_outs),
        scratch_shapes=list(scratch),
        compiler_params=pltpu.CompilerParams(vmem_limit_bytes=vmem),
        cost_estimate=pl.CostEstimate(flops=flops, bytes_accessed=1, transcendentals=0),
    )(scalars, *after, *operands)


def inverse_rms(values):
    return lax.rsqrt(jnp.mean(values * values, axis=-1, keepdims=True) + EPSILON)


def router_softmax(rows, router, expert_count):
    logits = matmul(rows, router)
    logits = jnp.where(iota(logits.shape, 1) < expert_count, logits, MASKED_SCORE)
    weights = jnp.exp(logits - jnp.max(logits, axis=-1, keepdims=True))
    return weights / jnp.sum(weights, axis=-1, keepdims=True)


def swap(values, axis, mask):
    count = lax.axis_size(axis)
    return lax.ppermute(values, axis, [(i, i ^ mask) for i in range(count)])


def stacked(pieces):
    parts = [piece[...].astype(F32) for piece in pieces]
    return parts[0] if len(parts) == 1 else jnp.concatenate(parts, axis=0)


def store_pieces(refs, values):
    rows = values.shape[0] // len(refs)
    for number, ref in enumerate(refs):
        ref[...] = values[number * rows : (number + 1) * rows].astype(ref.dtype)


def body(
    tokens,
    cotangent,
    query_weight,
    key_weight,
    value_weight,
    output_weight,
    attention_scale,
    expert_scale,
    router,
    bucket_bias,
    expert_up_weight,
    expert_down_weight,
    routes,
    lengths,
    buckets,
):
    row_count, width = tokens.shape
    block_len = routes.shape[0]
    expert_count = router.shape[1]
    bucket_count, local_heads = bucket_bias.shape
    head_width = local_heads * HEAD_DIM
    capacity = max(2, block_len * 5 // (4 * expert_count))
    half = (capacity + 1) // 2
    slot_rows = expert_count * half
    data_count = lax.axis_size("dp")
    shard_rows = width // data_count
    hidden_local = expert_up_weight.shape[1]
    tensor_count = lax.axis_size("tensor")
    span = 2 * block_len
    distances = buckets.shape[0]
    cut = width // 3

    data_index = lax.axis_index("dp")
    y_index = lax.axis_index("tensor")
    scalars = (data_index * 2 + y_index).astype(jnp.int32).reshape(1)

    staged = shard_rows % 16 == 0
    slot_pieces = expert_count if half % 8 == 0 else 1
    z_masks = [j * SPLIT for j in range(expert_count)]

    def over_z(pieces):
        if len(pieces) == 1:
            stack = pieces[0].reshape((expert_count, half) + pieces[0].shape[1:])
            moved = [stack[0]] + [swap(stack[j], "dp", z_masks[j]) for j in range(1, expert_count)]
            return [jnp.concatenate(moved, axis=0)]
        return [pieces[0]] + [swap(pieces[j], "dp", z_masks[j]) for j in range(1, expert_count)]

    small_columns = -(-(expert_count + 2) // LANES) * LANES
    weight_columns = 4 * head_width
    def pack(idx, *refs):
        sources, refs = refs[:15], refs[15:]
        (out_ref, rows_ref, rest_ref, facts_ref), refs = refs[:4], refs[4:]
        router_ref, attn_ref, moe_ref, *small_refs, sems = refs
        targets = (
            [out_ref.at[:, pl.ds(number * head_width, head_width)] for number in range(4)]
            + [router_ref, attn_ref, moe_ref]
            + [rows_ref.at[pl.ds(number * row_count, row_count), :] for number in range(2)]
            + small_refs
            + [
                ref.at[pl.ds(at, rows), pl.ds(number * hidden_local, hidden_local)]
                for number in range(2)
                for ref, at, rows in (
                    (rows_ref, 2 * row_count, cut),
                    (rest_ref, 0, width - cut),
                )
            ]
        )
        sources = list(sources[:13]) + [
            source.at[pl.ds(at, rows), :]
            for source in sources[13:]
            for at, rows in ((0, cut), (cut, width - cut))
        ]
        copies = [
            pltpu.make_async_copy(source, target, sems.at[number])
            for number, (source, target) in enumerate(zip(sources, targets))
        ]
        for copy in copies:
            copy.start()
        for copy in copies[4:7]:
            copy.wait()
        diagonal = iota((shard_rows, shard_rows), 0) == iota((shard_rows, shard_rows), 1)
        lane = iota((shard_rows, small_columns), 1)

        def column(row_ref):
            row = row_ref[...].astype(F32)
            return jnp.sum(jnp.where(diagonal, row, 0.0), axis=1, keepdims=True)

        spread_router = matmul_tn(
            router_ref[...],
            (iota((expert_count, small_columns), 0) == iota((expert_count, small_columns), 1))
            .astype(F32)
            .astype(BF16),
        )
        small = jnp.where(lane == expert_count, column(attn_ref), spread_router)
        small = jnp.where(lane == expert_count + 1, column(moe_ref), small)
        out_ref[:, weight_columns:] = small.astype(BF16)
        for copy in copies[:4] + copies[7:]:
            copy.wait()
        length_ref, bucket_ref, table_ref, route_ref = small_refs
        facts_ref[...] = jnp.zeros(facts_ref.shape, F32)
        facts_ref[0:1, :2] = length_ref[...].astype(F32)
        facts_ref[1:2, :distances] = bucket_ref[...].astype(F32)
        facts_ref[2:3, :block_len] = route_ref[...].astype(F32)
        facts_ref[8 : 8 + local_heads, :bucket_count] = table_ref[...]

    packed, rows_own, rest_own, facts = run(
        pack,
        scalars,
        [
            query_weight,
            key_weight,
            value_weight,
            output_weight,
            router.T,
            attention_scale[None, :],
            expert_scale[None, :],
            tokens,
            cotangent,
            lengths,
            buckets[None, :],
            bucket_bias.T,
            routes.reshape(1, block_len),
            expert_up_weight,
            expert_down_weight,
        ],
        [
            shape_of((shard_rows, weight_columns + small_columns), BF16),
            shape_of((2 * row_count + cut, 2 * hidden_local), BF16),
            shape_of((width - cut, 2 * hidden_local), BF16),
            shape_of((16, span), F32),
        ],
        [
            pltpu.VMEM((expert_count, shard_rows), BF16),
            pltpu.VMEM((1, shard_rows), BF16),
            pltpu.VMEM((1, shard_rows), BF16),
            pltpu.VMEM(lengths.shape, jnp.int32),
            pltpu.VMEM((1, distances), jnp.int32),
            pltpu.VMEM((local_heads, bucket_count), F32),
            pltpu.VMEM((1, block_len), jnp.int32),
            pltpu.SemaphoreType.DMA((17,)),
        ],
        far=15,
        vmem=VMEM_MOST,
    )
    if staged:
        gathered = [packed] + [swap(packed, "dp", mask) for mask in z_masks[1:]]
    else:
        gathered = [lax.all_gather(packed, "dp", axis=0, tiled=True)]

    def piece_offset(idx, number):
        j_z = number % expert_count
        j_x = (number // expert_count) % 2
        j_c = number // (2 * expert_count)
        index = (idx[Z_AT] ^ j_z) * SPLIT + (idx[X_AT] ^ j_x) * 2 + (idx[C_AT] ^ j_c)
        return pl.multiple_of(index * shard_rows, 16)

    rows_other = swap(rows_own, "tensor", 1)

    def prepare(idx, facts_ref, mine, others, *refs):
        x_ref, bias_ref, own_ref, other_ref, xs_ref, gs_ref, live_ref = refs[:7]
        pick_ref, back_ref, live_rows_ref = refs[7:10]
        live_parts = refs[10:-2]
        cot_full, head_table = refs[-2:]
        own_at = pl.multiple_of(idx[Y_AT] * row_count, row_count)
        other_at = pl.multiple_of((1 - idx[Y_AT]) * row_count, row_count)
        for at, rows in ((own_at, mine), (other_at, others)):
            x_ref[pl.ds(at, row_count), :] = rows[:row_count, :]
            cot_full[pl.ds(at, row_count), :] = rows[row_count : 2 * row_count, :]

        first = facts_ref[0:1, 0:1].astype(jnp.int32)
        active = first + facts_ref[0:1, 1:2].astype(jnp.int32)
        live_rows_ref[...] = jnp.broadcast_to(
            (iota((block_len, 1), 0) < active).astype(F32), live_rows_ref.shape
        )

        def segment(position):
            return jnp.where(position < first, 0, jnp.where(position < active, 1, 2))

        allowed = segment(iota((block_len, block_len), 0)) == segment(
            iota((block_len, block_len), 1)
        )
        pick = facts_ref[1:2, :distances].astype(jnp.int32) == iota((LANES, distances), 0)
        pick = pick.astype(F32)
        head_table[...] = jnp.zeros(head_table.shape, F32)
        head_table[:local_heads, :distances] = matmul(
            facts_ref[8 : 8 + local_heads, :bucket_count], pick[:bucket_count], HIGHEST
        )
        mirror = (
            iota((distances, span), 0) + iota((distances, span), 1) == distances - 1
        ).astype(F32)
        back_ref[...] = matmul(pick.astype(BF16), mirror.astype(BF16)).astype(BF16)
        for head in range(local_heads):
            line = jnp.broadcast_to(head_table[head : head + 1, :], (block_len, span))
            turned = pltpu.roll(line, block_len + 1, 1, stride=1, stride_axis=0)
            bias_ref[head] = jnp.where(allowed, turned[:, :block_len], MASKED_SCORE)

        route = facts_ref[2:3, :block_len].astype(jnp.int32)
        chosen = (route == iota((LANES, block_len), 0)).astype(F32)
        earlier = (iota((block_len, block_len), 0) < iota((block_len, block_len), 1)).astype(F32)
        counts = matmul(chosen.astype(BF16), earlier.astype(BF16))
        slot = jnp.sum(chosen * counts, axis=0, keepdims=True).astype(jnp.int32)
        row_id = iota((slot_rows, block_len), 0)

        def selection(which):
            place = slot - half * which
            code = (route ^ idx[Z_AT]) * half + place
            code = jnp.where((place >= 0) & (place < half), code, -1)
            return (row_id == code).astype(F32)

        own_select = selection(idx[Y_AT])
        own_bf = own_select.astype(BF16)
        own_ref[...] = own_bf
        other_ref[...] = selection(1 - idx[Y_AT]).astype(BF16)
        xs_ref[...] = matmul(own_bf, x_ref[...]).astype(BF16)
        gs_ref[...] = matmul(own_bf, cot_full[...]).astype(BF16)
        live_select = own_select * (iota((1, block_len), 1) < active).astype(F32)
        live_ref[...] = jnp.broadcast_to(
            jnp.sum(live_select, axis=1, keepdims=True), live_ref.shape
        )
        pick_ref[...] = matmul_nt(own_bf, chosen.astype(BF16))
        store_pieces(live_parts, matmul(live_select.astype(BF16), cot_full[...]))

    piece_shape = shape_of((slot_rows // slot_pieces, width), BF16)
    prepared = run(
        prepare,
        scalars,
        [facts, rows_own, rows_other],
        [
            shape_of((block_len, width), BF16),
            shape_of((local_heads, block_len, block_len), F32),
            shape_of((slot_rows, block_len), BF16),
            shape_of((slot_rows, block_len), BF16),
            shape_of((slot_rows, width), BF16),
            shape_of((slot_rows, width), BF16),
            shape_of((slot_rows, LANES), F32),
            shape_of((slot_rows, LANES), F32),
            shape_of((LANES, span), BF16),
            shape_of((block_len, LANES), F32),
        ]
        + [piece_shape] * slot_pieces,
        [pltpu.VMEM((block_len, width), BF16), pltpu.VMEM((8, span), F32)],
    )
    x_full, bias, own_select, other_select, x_slot, g_slot = prepared[:6]
    live_slot, pick_slot, pick_back, live_rows = prepared[6:10]
    g_home = prepared[10:]
    g_wait = []
    if staged:
        g_home = lax.optimization_barrier((*g_home, *gathered[1:expert_count]))[:slot_pieces]
        gathered = gathered + [swap(piece, "dp", 2) for piece in gathered]
        *gathered, _ = lax.optimization_barrier((*gathered, x_full))
        gathered = gathered + [swap(piece, "dp", 1) for piece in gathered]
    g_rows = over_z(list(g_home))
    if staged:
        g_wait = g_rows[1:]
    g_rows = g_rows + [swap(jnp.concatenate(g_rows, axis=0), "dp", 2)]
    rest_send, _ = lax.optimization_barrier((rest_own, rows_other))
    rest_y = swap(rest_send, "tensor", 1)
    expert_parts = [rows_own, rest_own, rows_other, rest_y]
    expert_parts += [swap(rows_own, "dp", 1), swap(rest_own, "dp", 1), swap(rows_other, "dp", 1)]

    def to_experts(pieces):
        arrived = over_z(list(pieces))
        return arrived + [swap(piece, "dp", 2) for piece in arrived]


    qkv_width = 3 * head_width
    piece_count = len(gathered)

    def attend(idx, live_ref, x_ref, bias_ref, own_ref, other_ref, xs_ref, *refs):
        pieces = refs[:piece_count]
        (
            send_ref,
            keep_ref,
            normed_ref,
            qkv_ref,
            probs_ref,
            context_ref,
            weight_ref,
            small_ref,
            gain_ref,
        ) = refs[piece_count:]
        if piece_count == 1:
            weight_ref[...] = pieces[0][:, :weight_columns]
            small_ref[...] = pieces[0][:, weight_columns:]
        else:
            for number, piece in enumerate(pieces):
                at = piece_offset(idx, number)
                weight_ref[pl.ds(at, shard_rows), :] = piece[:, :weight_columns]
                small_ref[pl.ds(at, shard_rows), :] = piece[:, weight_columns:]
        turned = small_ref[...].astype(F32).T
        gain = turned[expert_count : expert_count + 1, :]
        gain_ref[...] = jnp.broadcast_to(gain, gain_ref.shape)
        gain_ref[1:2, :] = turned[expert_count + 1 : expert_count + 2, :]
        x = x_ref[...].astype(F32)
        normed = (x * inverse_rms(x) * gain).astype(BF16)
        normed_ref[...] = normed
        qkv_ref[...] = matmul(normed, weight_ref[:, :qkv_width]).astype(BF16)
        live = live_ref[:, :1]
        for head in range(local_heads):
            at = head * HEAD_DIM
            query = qkv_ref[:, at : at + HEAD_DIM]
            key = qkv_ref[:, head_width + at : head_width + at + HEAD_DIM]
            value = qkv_ref[:, 2 * head_width + at : 2 * head_width + at + HEAD_DIM]
            scores = matmul_nt(query, key) * SCORE_SCALE + bias_ref[head]
            weights = jnp.exp(scores - jnp.max(scores, axis=-1, keepdims=True))
            probs = weights / jnp.sum(weights, axis=-1, keepdims=True)
            probs_ref[head] = probs
            context = matmul(probs.astype(BF16), value) * live
            context_ref[:, at : at + HEAD_DIM] = context.astype(BF16)
        out = matmul_nt(context_ref[...], weight_ref[:, qkv_width:]).astype(BF16)
        send_ref[...] = matmul(other_ref[...], out).astype(BF16)
        keep_ref[...] = matmul(own_ref[...], out) + xs_ref[...].astype(F32)

    send, keep, normed, qkv, probs, context, weights, router_small, gains = run(
        attend,
        scalars,
        [live_rows, x_full, bias, own_select, other_select, x_slot] + gathered,
        [
            shape_of((slot_rows, width), BF16),
            shape_of((slot_rows, width), F32),
            shape_of((block_len, width), BF16),
            shape_of((block_len, qkv_width), BF16),
            shape_of((local_heads, block_len, block_len), F32),
            shape_of((block_len, head_width), BF16),
            shape_of((width, weight_columns), BF16),
            shape_of((width, small_columns), BF16),
            shape_of((8, width), F32),
        ],
        after=g_wait,
    )
    arrived = swap(send, "tensor", 1)
    rest_y, _ = lax.optimization_barrier((rest_y, arrived))
    expert_parts.append(swap(rest_y, "dp", 1))

    def second_norm(idx, keep_ref, arrived_ref, gain_ref, residual_ref, scale_ref, nm_ref, *parts):
        residual = keep_ref[...] + arrived_ref[...].astype(F32)
        scale = inverse_rms(residual)
        residual_ref[...] = residual
        scale_ref[...] = jnp.broadcast_to(scale, scale_ref.shape)
        rows = residual * scale * gain_ref[1:2, :]
        nm_ref[...] = rows.astype(BF16)
        store_pieces(parts, rows)

    residual, scale_moe, normed_moe, *row_home = run(
        second_norm,
        scalars,
        [keep, arrived, gains],
        [
            shape_of((slot_rows, width), F32),
            shape_of((slot_rows, LANES), F32),
            shape_of((slot_rows, width), BF16),
        ]
        + [piece_shape] * slot_pieces,
        after=expert_parts[4:7],
    )
    expert_rows = to_experts(row_home)

    expert_in = 2 * slot_rows
    parts = 4

    def experts(idx, router_ref, *refs):
        count = 2 * slot_pieces
        row_parts, refs = refs[:count], refs[count:]
        g_parts, refs = refs[: slot_pieces + 1], refs[slot_pieces + 1 :]
        weights, refs = refs[: 2 * parts], refs[2 * parts :]
        send_ref, keep_ref, rows_ref, total_ref, hidden_ref, pre_ref = refs
        rows = stacked(row_parts).astype(BF16)
        rows_ref[...] = rows
        routed = router_softmax(rows, router_ref[...], expert_count)
        mine = (iota(routed.shape, 1) == idx[Z_AT]).astype(F32)
        gate = jnp.sum(routed * mine, axis=1, keepdims=True)
        total = (stacked(g_parts) * gate).astype(BF16)
        total_ref[...] = total
        forward = jnp.zeros((expert_in, width), F32)
        backward = jnp.zeros((expert_in, width), F32)
        pair_width = 2 * hidden_local
        for pair in range(parts // 2):
            at = pair * pair_width
            up, down = [
                jnp.concatenate(
                    [
                        jnp.concatenate([head[2 * row_count :, columns], rest[:, columns]], axis=0)
                        for head, rest in (
                            weights[4 * pair : 4 * pair + 2],
                            weights[4 * pair + 2 : 4 * pair + 4],
                        )
                    ],
                    axis=1,
                )
                for columns in (slice(0, hidden_local), slice(hidden_local, pair_width))
            ]
            pre = matmul(rows, up)
            square = pre * pre
            inner = 0.7978845608028654 * pre * (1.0 + 0.044715 * square)
            tanh = jnp.tanh(inner)
            hidden = (0.5 * pre * (1.0 + tanh)).astype(BF16)
            slope = 0.5 * (1.0 + tanh) + 0.5 * pre * (1.0 - tanh * tanh) * (
                0.7978845608028654 * (1.0 + 3.0 * 0.044715 * square)
            )
            hidden_ref[:, at : at + pair_width] = hidden
            grad_pre = (matmul(total, down) * slope).astype(BF16)
            pre_ref[:, at : at + pair_width] = grad_pre
            forward += matmul_nt(hidden, down)
            backward += matmul_nt(grad_pre, up)
        keep_ref[:, :width] = forward[:slot_rows]
        keep_ref[:, width:] = backward[:slot_rows]
        send_ref[:, :width] = forward[slot_rows:].astype(BF16)
        send_ref[:, width:] = backward[slot_rows:].astype(BF16)

    send, keep, rows_in, total_in, hidden, grad_pre = run(
        experts,
        scalars,
        [router_small] + expert_rows + g_rows + expert_parts,
        [
            shape_of((slot_rows, 2 * width), BF16),
            shape_of((slot_rows, 2 * width), F32),
            shape_of((expert_in, width), BF16),
            shape_of((expert_in, width), BF16),
            shape_of((expert_in, parts * hidden_local), BF16),
            shape_of((expert_in, parts * hidden_local), BF16),
        ],
    )
    arrived = swap(send, "dp", 2)

    def expert_grads(first):
        def grads(idx, rows_ref, total_ref, hidden_ref, pre_ref, *outs):
            at = first * hidden_local
            both = slice(at, at + 2 * hidden_local)
            up_grads = matmul_tn(rows_ref[...], pre_ref[:, both])
            down_grads = matmul_tn(total_ref[...], hidden_ref[:, both])
            for part in range(2):
                columns = slice(part * hidden_local, (part + 1) * hidden_local)
                up_grad, down_grad = up_grads[:, columns], down_grads[:, columns]
                ref, place = (outs[0], 2 * part) if len(outs) == 1 else (outs[part], 0)
                ref[place] = up_grad.astype(ref.dtype)
                ref[place + 1] = down_grad.astype(ref.dtype)

        return grads

    weight_shape = (width, hidden_local)
    grad_inputs = [rows_in, total_in, hidden, grad_pre]
    (grads_c,) = run(
        expert_grads(2), scalars, grad_inputs, [shape_of((4,) + weight_shape, BF16)]
    )
    grads_own, grads_y = run(
        expert_grads(0),
        scalars,
        grad_inputs,
        [shape_of((2,) + weight_shape, F32), shape_of((2,) + weight_shape, BF16)],
    )
    from_c = swap(grads_c, "dp", 1)

    def fold_y(idx, y_ref, c_ref, up_ref, down_ref):
        for number, ref in enumerate((up_ref, down_ref)):
            total = y_ref[number].astype(F32) + c_ref[2 + number].astype(F32)
            if number == 0:
                ref[...] = total.astype(BF16)
            else:
                ref[:, :hidden_local] = total[: width // 2].astype(BF16)
                ref[:, hidden_local:] = total[width // 2 :].astype(BF16)

    up_passed, down_passed = run(
        fold_y,
        scalars,
        [grads_y, from_c],
        [shape_of(weight_shape, BF16), shape_of((width // 2, 2 * hidden_local), BF16)],
    )
    up_from_y = swap(up_passed, "tensor", 1)

    def add_x(idx, keep_ref, arrived_ref, *parts_out):
        store_pieces(parts_out, keep_ref[...] + arrived_ref[...].astype(F32))

    both_shape = shape_of((slot_rows // slot_pieces, 2 * width), BF16)
    back = run(add_x, scalars, [keep, arrived], [both_shape] * slot_pieces)
    home = over_z(list(back))

    def fold_grad(number):
        def fold(idx, own_ref, c_ref, y_ref, out_ref, done_ref):
            done_ref[...] = jnp.zeros(done_ref.shape, F32)
            if number == 0:
                out_ref[...] = own_ref[0] + c_ref[0].astype(F32) + y_ref[...].astype(F32)
                return
            for part in range(2):
                rows = slice(part * (width // 2), (part + 1) * (width // 2))
                columns = slice(part * hidden_local, (part + 1) * hidden_local)
                out_ref[rows, :] = (
                    own_ref[1, rows, :]
                    + c_ref[1, rows, :].astype(F32)
                    + y_ref[slot_rows + row_count :, columns].astype(F32)
                )

        return fold

    grad_w_in, up_done = run(
        fold_grad(0),
        scalars,
        [grads_own, from_c, up_from_y],
        [shape_of(weight_shape, F32), shape_of((8, LANES), F32)],
        after=[back[0]],
    )

    expert_pad = -(-expert_count // 8) * 8

    def at_home(idx, *refs):
        pieces, refs = refs[:slot_pieces], refs[slot_pieces:]
        (
            residual_ref,
            scale_ref,
            nm_ref,
            g_ref,
            live_ref,
            pick_ref,
            gain_ref,
            router_ref,
            mid_ref,
            layer_ref,
            gain_out,
            router_out,
        ) = refs
        returned = stacked(pieces)
        total, back_rows = returned[:, :width], returned[:, width:]
        residual = residual_ref[...]
        scale = scale_ref[:, :1]
        live = live_ref[:, :1]
        pick = pick_ref[...]
        gain = gain_ref[1:2, :]
        g = g_ref[...].astype(F32)
        routed = router_softmax(nm_ref[...], router_ref[...], expert_count)
        gate = jnp.sum(routed * pick, axis=1, keepdims=True)
        layer_ref[...] = (residual + gate * total * live).astype(BF16)
        grad_gate = jnp.sum(g * total, axis=1, keepdims=True) * live
        grad_logits = grad_gate * gate * (pick - routed)
        upstream = back_rows + matmul_nt(grad_logits, router_ref[...].astype(F32), HIGHEST)
        scaled = upstream * gain
        grad_mid = (
            g
            + scale * scaled
            - residual * scale**3 * jnp.mean(scaled * residual, axis=-1, keepdims=True)
        )
        mid_ref[...] = grad_mid.astype(BF16)
        gain_out[...] = jnp.broadcast_to(
            jnp.sum(upstream * residual * scale, axis=0, keepdims=True), gain_out.shape
        )
        router_grad = matmul_tn(grad_logits, nm_ref[...].astype(F32), HIGHEST)
        router_out[...] = router_grad[:expert_pad]

    mid_own, layer_own, gain_moe, router_part = run(
        at_home,
        scalars,
        home
        + [residual, scale_moe, normed_moe, g_slot, live_slot, pick_slot, gains, router_small],
        [
            shape_of((slot_rows, width), BF16),
            shape_of((slot_rows, width), BF16),
            shape_of((8, width), F32),
            shape_of((expert_pad, width), F32),
        ],
        after=[up_done],
    )
    mid_other = swap(mid_own, "tensor", 1)

    half_pieces = 2 * expert_count
    rest_part = 2 * LANES
    first_part = weight_columns - rest_part
    small_blocks = width // rest_part

    def emit_rows(idx, full_ref, outs):
        if not staged:
            outs[0][...] = full_ref[...]
            return
        keep_ref, send_ref = outs
        for number in range(half_pieces):
            at = piece_offset(idx, number)
            keep_ref[number] = full_ref[pl.ds(at, shard_rows), :]
            at = piece_offset(idx, number + half_pieces)
            send_ref[number] = full_ref[pl.ds(at, shard_rows), :].astype(BF16)

    if staged:
        row_shapes = [
            shape_of((half_pieces, shard_rows, weight_columns), F32),
            shape_of((half_pieces, shard_rows, weight_columns), BF16),
        ]
    else:
        row_shapes = [shape_of((width, weight_columns), F32)]

    small_rows = -(-(expert_count + 2 + tensor_count) // 8) * 8

    def store_halves(ref, at, values):
        high = values.astype(BF16)
        both = jnp.concatenate([high.astype(F32), values - high.astype(F32)], axis=0).astype(BF16)
        for block in range(small_blocks):
            row = at + 2 * small_rows * block
            ref[row : row + 2 * small_rows, :] = both[
                :, block * rest_part : (block + 1) * rest_part
            ]

    def load_halves(ref, at):
        blocks = []
        for block in range(small_blocks):
            row = at + 2 * small_rows * block
            both = ref[row : row + 2 * small_rows, :].astype(F32)
            blocks.append(both[:small_rows] + both[small_rows:])
        return jnp.concatenate(blocks, axis=1)

    def attend_back(
        idx,
        own_ref,
        other_ref,
        mid_ref,
        mid_other_ref,
        context_ref,
        weight_ref,
        qkv_ref,
        probs_ref,
        normed_ref,
        x_ref,
        back_ref,
        live_ref,
        moe_ref,
        router_ref,
        layer_ref,
        down_ref,
        *refs,
    ):
        ga_ref, keep_ref, send_ref, small_ref = refs[:4]
        outs = refs[4:-3]
        grads, full, upstream = refs[-3:]
        live = live_ref[:, :1]
        grad_attention = matmul_tn(own_ref[...], mid_ref[...]) + matmul_tn(
            other_ref[...], mid_other_ref[...]
        )
        ga_ref[...] = grad_attention.astype(BF16)
        full[:, qkv_width:] = matmul_tn(ga_ref[...], context_ref[...])
        grad_context = matmul(ga_ref[...], weight_ref[:, qkv_width:]) * live
        grad_context = grad_context.astype(BF16)
        mirror = (
            iota((block_len, block_len), 0) + iota((block_len, block_len), 1) == block_len - 1
        ).astype(BF16)
        lines = []
        for head in range(local_heads):
            at = head * HEAD_DIM
            query = qkv_ref[:, at : at + HEAD_DIM]
            key = qkv_ref[:, head_width + at : head_width + at + HEAD_DIM]
            value = qkv_ref[:, 2 * head_width + at : 2 * head_width + at + HEAD_DIM]
            back = grad_context[:, at : at + HEAD_DIM]
            probs = probs_ref[head]
            grad_value = matmul_tn(probs.astype(BF16), back)
            grad_probs = matmul_nt(back, value)
            grad_scores = probs * (
                grad_probs - jnp.sum(probs * grad_probs, axis=-1, keepdims=True)
            )
            grad_scores = grad_scores.astype(BF16)
            grad_query = matmul(grad_scores, key) * SCORE_SCALE
            grad_key = matmul_tn(grad_scores, query) * SCORE_SCALE
            grads[:, at : at + HEAD_DIM] = grad_query.astype(BF16)
            grads[:, head_width + at : head_width + at + HEAD_DIM] = grad_key.astype(BF16)
            grads[:, 2 * head_width + at : 2 * head_width + at + HEAD_DIM] = grad_value.astype(
                BF16
            )
            lines_left = jnp.concatenate(
                [matmul(grad_scores, mirror), jnp.zeros((block_len, span - block_len), F32)], axis=1
            )
            rows = block_len
            while rows > 8:
                rows //= 2
                lines_left = lines_left[:rows] + pltpu.roll(lines_left[rows:], rows, 1)
            lines_left = pltpu.roll(lines_left, 0, 1, stride=1, stride_axis=0)
            lines.append(jnp.sum(lines_left, axis=0, keepdims=True))
        lines.append(jnp.zeros((8 - local_heads, span), F32))
        diagonal = jnp.concatenate(lines, axis=0)
        table = matmul_nt(diagonal, back_ref[...].astype(F32), HIGHEST)
        line = [table[head : head + 1, :] for head in range(local_heads)]
        line.append(jnp.zeros((1, width - local_heads * LANES), F32))
        line = jnp.concatenate(line[: local_heads + (width > local_heads * LANES)], axis=1)
        all_grads = grads[...]
        grad_normed = matmul_nt(all_grads, weight_ref[:, :qkv_width])
        upstream[...] = grad_normed
        x = x_ref[...].astype(F32)
        gain = jnp.sum(grad_normed * x * inverse_rms(x), axis=0, keepdims=True)
        row = iota((small_rows, width), 0)
        small = jnp.where(row == expert_count, gain, 0.0)
        small = jnp.where(row == expert_count + 1, moe_ref[:1, :], small)
        small_ref[...] = jnp.where(row == expert_count + 2 + idx[Y_AT], line, small)
        small_ref[:expert_count, :] = router_ref[:expert_count, :]
        own_at = pl.multiple_of(idx[Y_AT] * row_count, row_count)
        other_at = pl.multiple_of((1 - idx[Y_AT]) * row_count, row_count)
        keep_ref[...] = upstream[pl.ds(own_at, row_count), :]
        send_ref[slot_rows : slot_rows + row_count, :] = upstream[
            pl.ds(other_at, row_count), :
        ].astype(BF16)
        send_ref[:slot_rows, :] = layer_ref[...]
        send_ref[slot_rows + row_count :, :] = down_ref[...]
        full[:, :qkv_width] = matmul_tn(normed_ref[...], all_grads)
        emit_rows(idx, full, outs)

    grad_attention, up_keep, up_send, small, *partial_rows = run(
        attend_back,
        scalars,
        [
            own_select,
            other_select,
            mid_own,
            mid_other,
            context,
            weights,
            qkv,
            probs,
            normed,
            x_full,
            pick_back,
            live_rows,
            gain_moe,
            router_part,
            layer_own,
            down_passed,
        ],
        [
            shape_of((block_len, width), BF16),
            shape_of((row_count, width), F32),
            shape_of((slot_rows + row_count + width // 2, width), BF16),
            shape_of((small_rows, width), F32),
        ]
        + row_shapes,
        [
            pltpu.VMEM((block_len, qkv_width), BF16),
            pltpu.VMEM((width, weight_columns), F32),
            pltpu.VMEM((block_len, width), F32),
        ],
    )
    def small_over_y(idx, small_ref, other_ref, out_ref):
        out_ref[...] = small_ref[...] + other_ref[...]

    (small,) = run(
        small_over_y,
        scalars,
        [small, swap(small, "tensor", 1)],
        [shape_of((small_rows, width), F32)],
    )
    up_send, _ = lax.optimization_barrier((up_send, small))
    up_other = swap(up_send, "tensor", 1)

    out_shapes = [shape_of((shard_rows, head_width), F32)] * 4
    if staged:
        held, outgoing = partial_rows
        from_core = swap(outgoing, "dp", 1)

        small_core = swap(small, "dp", 1)
        extra_rows = 2 * small_rows * small_blocks

        def after_core(idx, small_ref, small_core, held_ref, from_ref, x_send, x_keep, *z_refs):
            z_sends, z_keep, small_keep = z_refs[:-2], z_refs[-2], z_refs[-1]
            small = small_ref[...] + small_core[...]
            small_keep[...] = small

            def total(number, columns):
                return held_ref[number, :, columns] + from_ref[number, :, columns].astype(F32)

            front, rest = slice(0, first_part), slice(first_part, weight_columns)
            for j in range(expert_count):
                x_keep[j] = total(j, front)
                x_send[j] = total(expert_count + j, front).astype(BF16)
                if j > 0:
                    store_halves(z_sends[j - 1], 2 * shard_rows, small)
                for x in range(2):
                    piece = total(x * expert_count + j, rest)
                    if j == 0:
                        z_keep[x] = piece
                    else:
                        z_sends[j - 1][x * shard_rows : (x + 1) * shard_rows, :] = piece.astype(
                            BF16
                        )

        x_send, x_keep, *z_sends, z_keep, small = run(
            after_core,
            scalars,
            [small, small_core, held, from_core],
            [
                shape_of((expert_count, shard_rows, first_part), BF16),
                shape_of((expert_count, shard_rows, first_part), F32),
            ]
            + [shape_of((2 * shard_rows + extra_rows, rest_part), BF16)] * (expert_count - 1)
            + [shape_of((2, shard_rows, rest_part), F32), shape_of((small_rows, width), F32)],
        )
        from_x = swap(x_send, "dp", 2)
        from_z = [swap(piece, "dp", z_masks[j + 1]) for j, piece in enumerate(z_sends)]


        def after_first(idx, small_ref, x_keep, from_x, z_keep, *refs):
            from_z, refs = refs[: expert_count - 1], refs[expert_count - 1 :]
            z_sends, (front_keep, x_send, rest_keep, small_keep) = refs[:-4], refs[-4:]
            front_keep[...] = x_keep[0] + from_x[0].astype(F32)
            for j in range(1, expert_count):
                z_sends[j - 1][...] = (x_keep[j] + from_x[j].astype(F32)).astype(BF16)
            small = small_ref[...]
            rest = [z_keep[0], z_keep[1]]
            for ref in from_z:
                small = small + load_halves(ref, 2 * shard_rows)
                for x in range(2):
                    rest[x] = rest[x] + ref[x * shard_rows : (x + 1) * shard_rows, :].astype(F32)
            small_keep[...] = small
            store_halves(x_send, shard_rows, small)
            rest_keep[...] = rest[0]
            x_send[:shard_rows, :] = rest[1].astype(BF16)

        *z_sends, front_keep, x_send, rest_keep, small = run(
            after_first,
            scalars,
            [small, x_keep, from_x, z_keep] + from_z,
            [shape_of((shard_rows, first_part), BF16)] * (expert_count - 1)
            + [
                shape_of((shard_rows, first_part), F32),
                shape_of((shard_rows + extra_rows, rest_part), BF16),
                shape_of((shard_rows, rest_part), F32),
                shape_of((small_rows, width), F32),
            ],
        )
        from_z = [swap(piece, "dp", z_masks[j + 1]) for j, piece in enumerate(z_sends)]
        from_x = swap(x_send, "dp", 2)
        late = [front_keep]

        def last_sum(idx, small_ref, front_keep, rest_keep, from_x, *refs):
            from_z, refs = refs[: expert_count - 1], refs[expert_count - 1 :]
            outs, (attn_out, moe_out, router_out, table_out, full) = refs[:-5], refs[-5:]
            front = front_keep[...]
            small = small_ref[...] + load_halves(from_x, shard_rows)
            for ref in from_z:
                front = front + ref[...].astype(F32)
            column = iota((LANES, width), 1) - idx[DATA_AT] * shard_rows
            select = (column == iota((LANES, width), 0)).astype(F32)
            shard = matmul_nt(small, select, HIGHEST)
            attn_out[...] = shard[expert_count : expert_count + 1, :shard_rows]
            moe_out[...] = shard[expert_count + 1 : expert_count + 2, :shard_rows]
            router_out[...] = shard[:expert_count, :shard_rows]
            mine = iota((small_rows, width), 0) == expert_count + 2 + idx[Y_AT]
            line = jnp.sum(jnp.where(mine, small, 0.0), axis=0, keepdims=True)
            lines = [line[:, head * LANES : (head + 1) * LANES] for head in range(local_heads)]
            table_out[...] = jnp.concatenate(lines, axis=0)[:, :bucket_count]
            full[:, :first_part] = front
            full[:, first_part:] = rest_keep[...] + from_x[:shard_rows, :].astype(F32)
            for number, out in enumerate(outs):
                out[...] = full[:, number * head_width : (number + 1) * head_width]

        *grad_matrices, grad_attn_scale, grad_moe_scale, grad_router, table = run(
            last_sum,
            scalars,
            [small, front_keep, rest_keep, from_x] + from_z,
            out_shapes
            + [
                shape_of((1, shard_rows), F32),
                shape_of((1, shard_rows), F32),
                shape_of((expert_count, shard_rows), F32),
                shape_of((local_heads, bucket_count), F32),
            ],
            [pltpu.VMEM((shard_rows, weight_columns), F32)],
        )
        grad_attn_scale, grad_moe_scale = grad_attn_scale[0], grad_moe_scale[0]
        grad_router, table = grad_router.T, table.T
    else:
        late = []
        summed = lax.psum_scatter(partial_rows[0], "dp", scatter_dimension=0, tiled=True)
        grad_matrices = [
            summed[:, number * head_width : (number + 1) * head_width] for number in range(4)
        ]
        small = lax.psum(small, "dp")
        shard = lax.dynamic_slice_in_dim(small, data_index * shard_rows, shard_rows, 1)
        grad_router = shard[:expert_count].T
        grad_attn_scale, grad_moe_scale = shard[expert_count], shard[expert_count + 1]
        table = lax.dynamic_slice_in_dim(small, expert_count + 2 + y_index, 1, 0)
        table = table[0, : local_heads * LANES].reshape(local_heads, LANES)[:, :bucket_count].T

    grad_w_out, _ = run(
        fold_grad(1),
        scalars,
        [grads_own, from_c, up_other],
        [shape_of(weight_shape, F32), shape_of((8, LANES), F32)],
        after=late,
    )
    def finish(
        idx, own_ref, other_ref, layer_ref, arrived_ref, ga_ref, keep_ref, tok_ref, gain_ref,
        layer_out, tokens_out, full
    ):
        own_at = pl.multiple_of(idx[Y_AT] * row_count, row_count)
        full[...] = matmul_tn(own_ref[...], layer_ref[...]) + matmul_tn(
            other_ref[...], arrived_ref[:slot_rows, :]
        )
        layer_out[...] = full[pl.ds(own_at, row_count), :].astype(BF16)
        x = tok_ref[...].astype(F32)
        scale = inverse_rms(x)
        scaled = keep_ref[...] + arrived_ref[slot_rows : slot_rows + row_count, :].astype(F32)
        scaled = scaled * gain_ref[:1, :]
        grad = scale * scaled - x * scale**3 * jnp.mean(scaled * x, axis=-1, keepdims=True)
        grad = grad + ga_ref[pl.ds(own_at, row_count), :].astype(F32)
        tokens_out[...] = grad.astype(BF16)

    layer_out, grad_tokens = run(
        finish,
        scalars,
        [
            own_select, other_select, layer_own, up_other, grad_attention, up_keep, tokens, gains,
        ],
        [shape_of((row_count, width), BF16)] * 2,
        [pltpu.VMEM((block_len, width), F32)],
        after=late,
    )

    return (
        layer_out,
        grad_tokens,
        *grad_matrices,
        grad_attn_scale,
        grad_moe_scale,
        grad_router,
        table,
        grad_w_in,
        grad_w_out,
    )


def solution(mesh):
    in_specs = (
        P(("dp", "tensor"), None),
        P(("dp", "tensor"), None),
        P("dp", "tensor"),
        P("dp", "tensor"),
        P("dp", "tensor"),
        P("dp", "tensor"),
        P("dp"),
        P("dp"),
        P("dp", None),
        P(None, "tensor"),
        P(None, ("dp", "tensor")),
        P(None, ("dp", "tensor")),
        P("dp", None),
        P("dp", None),
        P(),
    )
    out_specs = (
        P(("dp", "tensor"), None),
        P(("dp", "tensor"), None),
        P("dp", "tensor"),
        P("dp", "tensor"),
        P("dp", "tensor"),
        P("dp", "tensor"),
        P("dp"),
        P("dp"),
        P("dp", None),
        P(None, "tensor"),
        P(None, ("dp", "tensor")),
        P(None, ("dp", "tensor")),
    )
    return jax.shard_map(body, mesh=mesh, in_specs=in_specs, out_specs=out_specs, check_vma=False)
```
